128 devices in a mesh: dp: 32 (over y, x, z_lo), pool: 4 (over z_hi, core).
Axes of the slice: x: 4, y: 4, z: 4 (z_hi: 2, z_lo: 2; z = z_hi * 2 + z_lo), core: 2. Of those that a mesh axis runs over, the one named last changes fastest.
Arguments:
- hidden_in: bfloat16 [2048, 3584], P(('dp', 'pool')), may hold values from -6 to 6
- expert_ids: int32 [2048, 8], P(('dp', 'pool')), may hold values from 0 to 31, all different within a row; in each aligned block of 16 rows (0 to 15, 16 to 31, ...) at most 8 rows name the same one
- gate_vals: float32 [2048, 8], P(('dp', 'pool')), may hold values from 0.05 to 0.6
- w_gate: bfloat16 [32, 3584, 2048], P('dp', None, 'pool'), may hold values from -0.09375 to 0.09375
- w_up: bfloat16 [32, 3584, 2048], P('dp', None, 'pool'), may hold values from -0.09375 to 0.09375
- w_down: bfloat16 [32, 2048, 3584], P('dp', 'pool'), may hold values from -0.125 to 0.125
- w_latent: bfloat16 [3584, 512], replicated, may hold values from -0.09375 to 0.09375
- w_rope: bfloat16 [3584, 64], replicated, may hold values from -0.09375 to 0.09375
- latent_gain: float32 [512], replicated, may hold values from 0.5 to 1.5
- cache_latent: bfloat16 [1024, 128, 512], P(('dp', 'pool')), may hold values from -6 to 6
- cache_rope: bfloat16 [1024, 64, 128], P(('dp', 'pool')), may hold values from -6 to 6
- send_index: int32 [128, 32], P(('dp', 'pool')), may hold values from 0 to 7
- block_table: int32 [32, 4, 32], P('dp'), may hold values from 0 to 127, as said below
- cached_len: int32 [32, 4], P('dp'), may hold values from 1 to 4096, as said below
- new_counts: int32 [32, 4], P('dp'), may hold values from 1 to 32, 64 in all within a row
- q_latent: bfloat16 [2048, 64, 512], P('dp', 'pool'), may hold values from -7 to 7
- q_rope: bfloat16 [2048, 4096], P('dp', 'pool'), may hold values from -6 to 6
Outputs:
- hidden_out: bfloat16 [2048, 3584], P(('dp', 'pool'))
- new_latent: bfloat16 [2048, 512], P(('dp', 'pool'))
- new_rope: bfloat16 [2048, 64], P(('dp', 'pool'))
- context: bfloat16 [2048, 64, 512], P('dp', 'pool')
The draws below stay inside these ranges and needn't reach their ends.
Inputs may be any that keep to these rules, and one draw needn't show every extreme that they name: `expert_ids`: each row names 8 different experts; among the 16 rows of one device at most 8 name one expert, a bound that some block reaches of them. `new_counts`: the 4 counts of a rank sum to 64, and one of them is 32. `cached_len`: every rank has a chat of exactly 4096 cached tokens. `block_table`: entry j of chat c of rank r, for j below the chat's number of cached blocks, is the index along dp+pool of the holder device that serves that block; no holder device appears twice among one rank's blocks; all other entries are 0.
All inputs are finite; a program needn't handle non-finite values.
Results may differ from the reference program's by a relative error of at most 0.015.
Values may be sent and summed in bfloat16 or wider, within the bound.
A program may use at most 192 MiB of HBM per device.

```python
import math
import jax
import jax.numpy as jnp
import numpy as np
from jax import lax

D = 3584
HEADS = 64
LAT = 512
ROPE = 64
F = 2048
TOPK = 8
BLOCK = 128
CHATS = 4
TOK_RANK = 64
BLK_DEV = 8
EXPERTS = 32
ROWS = 16
TOKENS = 2048
NEWMAX = 32
MAXB = 32
CAP = 8
N_DP = 32
N_POOL = 4
DEVICES = 128


def shuffled(key):
    return jax.random.permutation(key, DEVICES)


def chat_layout(key):
    base = jax.random.fold_in(key, 11)
    key_long, key_blocks, key_trim, key_order = jax.random.split(base, 4)
    longest = jax.random.randint(key_long, (N_DP, 1), 0, CHATS)
    is_long = jnp.arange(CHATS)[None, :] == longest
    blocks = jnp.where(is_long, MAXB, jax.random.randint(key_blocks, (N_DP, CHATS), 1, MAXB + 1))
    trim = jnp.where(is_long, 0, jax.random.randint(key_trim, (N_DP, CHATS), 0, BLOCK))
    lengths = (blocks * BLOCK - trim).astype(jnp.int32)
    orders = jax.vmap(shuffled)(jax.random.split(key_order, N_DP))
    offsets = jnp.cumsum(blocks, axis=1) - blocks
    index = jnp.minimum(offsets[:, :, None] + jnp.arange(MAXB)[None, None, :], DEVICES - 1)
    spread = jnp.broadcast_to(orders[:, None, :], (N_DP, CHATS, DEVICES))
    table = jnp.take_along_axis(spread, index, axis=2)
    table = jnp.where(jnp.arange(MAXB)[None, None, :] < blocks[:, :, None], table, 0).astype(jnp.int32)
    return (lengths, table)


def draw_cached_len(key, part):
    return chat_layout(key)[0]


def draw_block_table(key, part):
    return chat_layout(key)[1]


def draw_cache_latent(key, part):
    own = jax.random.fold_in(key, 5)
    shape = (DEVICES * BLK_DEV, BLOCK, LAT)
    return jax.random.truncated_normal(own, -6.0, 6.0, shape, jnp.float32).astype(jnp.bfloat16)


def draw_q_latent(key, part):
    own = jax.random.fold_in(key, 7)
    shape = (TOKENS, HEADS, LAT)
    return jax.random.truncated_normal(own, -6.0, 6.0, shape, jnp.float32).astype(jnp.bfloat16)


def place_ends(entries, key, smallest, largest):
    index_at = [jax.random.randint(jax.random.fold_in(key, axis), (), 0, length) for axis, length in enumerate(entries.shape)]
    widest = entries.shape.index(max(entries.shape))
    next_to = index_at[:widest] + [(index_at[widest] + 1) % entries.shape[widest]] + index_at[widest + 1:]
    return entries.at[tuple(index_at)].set(smallest).at[tuple(next_to)].set(largest)


def block_scale(key, dims, pieces, low, top_value):
    def one(axis_at, parts):
        steps = jax.random.uniform(jax.random.fold_in(jax.random.fold_in(key, 6), axis_at), (parts,), jnp.float32, low / len(pieces), top_value / len(pieces))
        return jnp.repeat(jnp.exp(steps), dims[axis_at] // parts).reshape((-1,) + (1,) * (len(dims) - axis_at - 1))

    factor_of = one(*pieces[0])
    for cut in pieces[1:]:
        factor_of = factor_of * one(*cut)
    return factor_of


def profile(number_of, total, most, slope):
    weights = [(1 << 20) // math.isqrt(grade ** slope) + 1 for grade in range(2, number_of + 1)]
    spare, given = total - most - (number_of - 1), [1] * (number_of - 1)
    while spare > 0:
        movable = [i for i in range(number_of - 1) if given[i] < most]
        mass, budget = sum([weights[i] for i in movable]), spare
        for i in movable:
            addition = min(most - given[i], max(1, budget * weights[i] // mass), spare)
            given[i] = given[i] + addition
            spare = spare - addition
    return np.array([most] + given)


def uneven(stream_key, amount, total, bound, lean):
    if amount == 2:
        one = jax.random.randint(stream_key, (), max(1, total - bound), min(bound, total - 1) + 1)
        return jnp.stack([one, total - one])
    sizes = jnp.asarray(profile(amount, total, bound, lean), jnp.int32)
    couples = (amount - 1) // 2
    source_of, sink = sizes[1:1 + 2 * couples:2], sizes[2:2 + 2 * couples:2]
    slack = jnp.minimum(source_of - 1, bound - sink)
    moved = jax.random.randint(jax.random.fold_in(stream_key, 1), (couples,), 0, 1 << 20) % (slack + 1)
    sizes = sizes.at[1:1 + 2 * couples:2].set(source_of - moved).at[2:2 + 2 * couples:2].set(sink + moved)
    return sizes[jax.random.permutation(jax.random.fold_in(stream_key, 2), amount)]


def routed_block(key, own, number, rows, amount, top, most, lean):
    order = jax.random.permutation(key, amount)
    heavy_load, common = shares(amount, rows * top, most, lean, True), shares(amount, rows * top, most, lean, False)
    places = jnp.arange(amount)

    def named(sizes, turn):
        used = int((sizes > 0).sum())
        fixed = max(1, used // 4)
        passed = fixed + (places - fixed + turn * (used - fixed)) % max(1, amount - fixed)
        return jnp.zeros((amount,), jnp.int32).at[order[jnp.where(places < fixed, places, passed)]].set(jnp.asarray(sizes, jnp.int32))

    sizes = jnp.where(number % 4 == 0, named(heavy_load, number // 4), named(common, number - number // 4 - 1))
    mixed = jax.random.permutation(jax.random.fold_in(own, 3), amount)
    giver, taker = mixed[0:amount // 2 * 2:2], mixed[1:amount // 2 * 2:2]
    margin = jnp.minimum(sizes[giver] - 1, most - sizes[taker]) // 2
    margin = jnp.where((giver == order[0]) | (taker == order[0]) | (sizes[taker] == 0), 0, jnp.maximum(margin, 0))
    passed = jax.random.randint(jax.random.fold_in(own, 4), (amount // 2,), 0, 1 << 20) % (margin + 1)
    sizes = sizes.at[giver].add(-passed).at[taker].add(passed)
    members = jnp.searchsorted(jnp.cumsum(sizes), jnp.arange(rows * top), side="right").astype(jnp.int32)
    table = members.reshape(top, rows).T
    table = table[jax.random.permutation(jax.random.fold_in(own, 1), rows)]
    turn = jax.random.randint(jax.random.fold_in(own, 2), (rows, 1), 0, top)
    return jnp.take_along_axis(table, (jnp.arange(top)[None, :] + turn) % top, axis=1)


def shares(amount, total, most, lean, full):
    portions = [(1 << 20) // math.isqrt(grade ** lean) + 1 for grade in range(1, amount + 1)]
    largest = most if full else min(most, max(-(-total // amount), total * portions[0] // sum(portions)))
    least = 1 if total - largest >= amount - 1 else 0
    given, surplus = [largest] + [least] * (amount - 1), total - largest - least * (amount - 1)
    while surplus > 0:
        movable = [i for i in range(1, amount) if given[i] < largest] or [i for i in range(1, amount) if given[i] < most]
        pool, budget = sum([portions[i] for i in movable]), surplus
        for i in movable:
            extra = min(most - given[i], max(1, budget * portions[i] // pool), surplus)
            given[i] = given[i] + extra
            surplus = surplus - extra
    return np.array(given)


def centred(key, extent, scale, most, pieces=(), dtype=jnp.bfloat16):
    values = jax.random.normal(key, extent, jnp.float32) * scale
    if len(pieces) > 0:
        values = block_scale(key, extent, pieces, -0.22, 0.18) * values
    return jnp.clip(values, min=-most, max=most).astype(dtype)


def setup_inputs(seed: int = 0) -> dict:
    arg_keys = jax.random.split(jax.random.key(seed), 18)
    hidden_in = centred(arg_keys[0], (TOKENS, D), 1.0, 6.0, ((0, 128),))
    expert_ids_keys = jax.random.split(jax.random.fold_in(arg_keys[1], 1), TOKENS // ROWS)
    expert_ids_turns = jax.random.permutation(jax.random.fold_in(arg_keys[1], 3), TOKENS // ROWS)
    expert_ids = jax.vmap(lambda own, number: routed_block(jax.random.fold_in(arg_keys[1], 2), own, number, ROWS, EXPERTS, TOPK, CAP, 2))(expert_ids_keys, expert_ids_turns).reshape((TOKENS, TOPK))
    gate_vals = jnp.clip(0.05 + 0.55 * jax.random.uniform(arg_keys[2], (TOKENS, TOPK), jnp.float32) ** block_scale(arg_keys[2], (TOKENS, TOPK), ((0, 128),), -0.2, 0.2), 0.05, 0.6)
    w_gate = centred(arg_keys[3], (EXPERTS, D, F), D ** -0.5, 0.09375, ((0, 32), (2, 4)))
    w_up = centred(arg_keys[4], (EXPERTS, D, F), D ** -0.5, 0.09375, ((0, 32), (2, 4)))
    w_down = centred(arg_keys[5], (EXPERTS, F, D), F ** -0.5, 0.125, ((0, 32), (1, 4)))
    w_latent = centred(arg_keys[6], (D, LAT), D ** -0.5, 0.09375)
    w_rope = centred(arg_keys[7], (D, ROPE), D ** -0.5, 0.09375)
    latent_gain = jnp.clip(1.0 + 0.1 * jax.random.normal(arg_keys[8], (LAT,), jnp.float32), 0.5, 1.5)
    cache_latent = draw_cache_latent(jax.random.fold_in(arg_keys[17], 71), 0)
    cache_rope = centred(arg_keys[10], (DEVICES * BLK_DEV, ROPE, BLOCK), 1.0, 6.0, ((0, 128),))
    send_index = place_ends(jax.random.randint(arg_keys[11], (DEVICES, N_DP), 0, BLK_DEV), jax.random.fold_in(arg_keys[11], 1), 0, BLK_DEV - 1).astype(jnp.int32)
    block_table = draw_block_table(jax.random.fold_in(arg_keys[17], 71), 0)
    cached_len = draw_cached_len(jax.random.fold_in(arg_keys[17], 71), 0)
    new_counts = jax.vmap(lambda own: uneven(own, CHATS, TOK_RANK, NEWMAX, 1))(jax.random.split(arg_keys[14], N_DP)).reshape((N_DP, CHATS)).astype(jnp.int32)
    q_latent = draw_q_latent(jax.random.fold_in(arg_keys[17], 71), 0)
    q_rope = centred(arg_keys[16], (TOKENS, HEADS * ROPE), 1.0, 6.0, ((0, 32), (1, 4)))
    return dict(hidden_in=hidden_in, expert_ids=expert_ids, gate_vals=gate_vals, w_gate=w_gate, w_up=w_up, w_down=w_down, w_latent=w_latent, w_rope=w_rope, latent_gain=latent_gain, cache_latent=cache_latent, cache_rope=cache_rope, send_index=send_index, block_table=block_table, cached_len=cached_len, new_counts=new_counts, q_latent=q_latent, q_rope=q_rope)


SCORE_SCALE = 192.0 ** (-0.5)
ROPE_BASE = 10000.0
NORM_EPS = 1e-06

def rotate(values, positions):
    half = values.shape[-1] // 2
    exponent = jnp.arange(half).astype(jnp.float32) * (-2.0 / values.shape[-1])
    frequency = jnp.power(jnp.float32(ROPE_BASE), exponent)
    angle = positions.astype(jnp.float32)[:, None] * frequency[None, :]
    first = values[:, :half]
    second = values[:, half:]
    cosine = jnp.cos(angle)
    sine = jnp.sin(angle)
    return jnp.concatenate([first * cosine - second * sine, second * cosine + first * sine], axis=1)

def chat_positions(counts, lengths, local):
    ends = jnp.cumsum(counts).astype(jnp.int32)
    chat_of = lax.optimization_barrier(jnp.sum((local[:, None] >= ends[None, :]).astype(jnp.int32), axis=1)).astype(jnp.int32)
    starts = (ends - counts).astype(jnp.int32)
    onehot = (chat_of[:, None] == jnp.arange(counts.shape[0]).astype(jnp.int32)[None, :]).astype(jnp.int32)
    return (lax.optimization_barrier(jnp.sum(onehot * (lengths - starts)[None, :], axis=1)) + local).astype(jnp.int32)

def expert_rows(rows, gate_matrix, up_matrix, down_matrix):
    gate = jnp.dot(rows, gate_matrix, preferred_element_type=jnp.float32)
    lifted = jnp.dot(rows, up_matrix, preferred_element_type=jnp.float32)
    activated = (jax.nn.silu(gate) * lifted).astype(jnp.bfloat16)
    quarter = activated.shape[1] // N_POOL
    total = jnp.zeros((rows.shape[0], down_matrix.shape[1]), jnp.float32)
    for part_index in range(N_POOL):
        lower = part_index * quarter
        piece = jnp.dot(activated[:, lower:lower + quarter], down_matrix[lower:lower + quarter], preferred_element_type=jnp.float32).astype(jnp.bfloat16)
        total = total + lax.optimization_barrier(piece).astype(jnp.float32)
    return total

def mixture(hidden_in, expert_ids, gate_vals, w_gate, w_up, w_down):
    limit = N_DP * N_POOL * CAP

    def one_expert(total, index):
        hits = expert_ids == index
        weight = lax.optimization_barrier(jnp.sum(jnp.where(hits, gate_vals, 0.0), axis=1))
        member = jnp.any(hits, axis=1)
        order = jnp.argsort(jnp.where(member, 0, 1).astype(jnp.int32), stable=True)[:limit].astype(jnp.int32)
        output = expert_rows(hidden_in[order], w_gate[index], w_up[index], w_down[index])
        return (total.at[order].add(output * weight[order][:, None]), index)
    start_total = jnp.zeros((TOKENS, D), jnp.float32)
    total, unused = lax.scan(one_expert, start_total, jnp.arange(EXPERTS).astype(jnp.int32))
    return total

def rank_attention(q_lat, q_rot, fresh_lat, fresh_rot, table, lengths, counts, rank, send_index, cache_latent, cache_rope):
    starts = (jnp.cumsum(counts) - counts).astype(jnp.int32)
    query_latent = jnp.concatenate([q_lat, jnp.zeros((NEWMAX, HEADS, LAT), jnp.bfloat16)], axis=0)
    query_rope = jnp.concatenate([q_rot.reshape(TOK_RANK, HEADS, ROPE), jnp.zeros((NEWMAX, HEADS, ROPE), jnp.bfloat16)], axis=0)
    fresh_latent = jnp.concatenate([fresh_lat, jnp.zeros((NEWMAX, LAT), jnp.bfloat16)], axis=0)
    fresh_rope = jnp.concatenate([fresh_rot, jnp.zeros((NEWMAX, ROPE), jnp.bfloat16)], axis=0)
    offsets = jnp.arange(NEWMAX).astype(jnp.int32)
    key_count = MAXB * BLOCK
    context = jnp.zeros((TOK_RANK + NEWMAX, HEADS, LAT), jnp.bfloat16)
    for chat in range(CHATS):
        start = starts[chat]
        holders = table[chat]
        blocks = (holders * BLK_DEV + send_index[holders, rank]).astype(jnp.int32)
        keys_latent = cache_latent[blocks].reshape(key_count, LAT).astype(jnp.float32)
        keys_rope = jnp.swapaxes(cache_rope[blocks], 1, 2).reshape(key_count, ROPE).astype(jnp.float32)
        asks_latent = lax.dynamic_slice_in_dim(query_latent, start, NEWMAX, 0).astype(jnp.float32)
        asks_rope = lax.dynamic_slice_in_dim(query_rope, start, NEWMAX, 0).astype(jnp.float32)
        mine_latent = lax.dynamic_slice_in_dim(fresh_latent, start, NEWMAX, 0).astype(jnp.float32)
        mine_rope = lax.dynamic_slice_in_dim(fresh_rope, start, NEWMAX, 0).astype(jnp.float32)
        old_scores = (jnp.einsum('mhl,kl->mhk', asks_latent, keys_latent) + jnp.einsum('mhr,kr->mhk', asks_rope, keys_rope)) * SCORE_SCALE
        new_scores = (jnp.einsum('mhl,jl->mhj', asks_latent, mine_latent) + jnp.einsum('mhr,jr->mhj', asks_rope, mine_rope)) * SCORE_SCALE
        old_ok = (jnp.arange(key_count) < lengths[chat])[None, None, :]
        new_ok = ((offsets[None, :] <= offsets[:, None]) & (offsets[None, :] < counts[chat]))[:, None, :]
        row_max = jnp.maximum(lax.optimization_barrier(jnp.max(jnp.where(old_ok, old_scores, -jnp.inf), axis=2)), lax.optimization_barrier(jnp.max(jnp.where(new_ok, new_scores, -jnp.inf), axis=2)))
        old_weight = jnp.where(old_ok, jnp.exp(old_scores - row_max[:, :, None]), 0.0)
        new_weight = jnp.where(new_ok, jnp.exp(new_scores - row_max[:, :, None]), 0.0)
        total = lax.optimization_barrier(jnp.sum(old_weight, axis=2)) + lax.optimization_barrier(jnp.sum(new_weight, axis=2))
        old_rounded = lax.optimization_barrier(old_weight.astype(jnp.bfloat16)).astype(jnp.float32)
        new_rounded = lax.optimization_barrier(new_weight.astype(jnp.bfloat16)).astype(jnp.float32)
        mixed = jnp.einsum('mhk,kl->mhl', old_rounded, keys_latent) + jnp.einsum('mhj,jl->mhl', new_rounded, mine_latent)
        result = (mixed / total[:, :, None]).astype(jnp.bfloat16)
        old_rows = lax.dynamic_slice_in_dim(context, start, NEWMAX, 0)
        keep = (offsets < counts[chat])[:, None, None]
        context = lax.dynamic_update_slice_in_dim(context, jnp.where(keep, result, old_rows), start, 0)
    return context[:TOK_RANK]

def reference(hidden_in, expert_ids, gate_vals, w_gate, w_up, w_down, w_latent, w_rope, latent_gain, cache_latent, cache_rope, send_index, block_table, cached_len, new_counts, q_latent, q_rope):
    moe = mixture(hidden_in, expert_ids, gate_vals, w_gate, w_up, w_down)
    hidden_out = (hidden_in.astype(jnp.float32) + moe).astype(jnp.bfloat16)
    latent = jnp.dot(hidden_out, w_latent, preferred_element_type=jnp.float32)
    norm_scale = lax.rsqrt(lax.optimization_barrier(jnp.mean(latent * latent, axis=1, keepdims=True)) + NORM_EPS)
    new_latent = (latent * norm_scale * latent_gain[None, :]).astype(jnp.bfloat16)
    local = jnp.arange(TOK_RANK).astype(jnp.int32)
    positions = jax.vmap(chat_positions, in_axes=(0, 0, None))(new_counts, cached_len, local).reshape(-1)
    new_rope = rotate(jnp.dot(hidden_out, w_rope, preferred_element_type=jnp.float32), positions).astype(jnp.bfloat16)

    def per_rank(items):
        q_lat, q_rot, fresh_lat, fresh_rot, table, lengths, counts, rank = items
        return rank_attention(q_lat, q_rot, fresh_lat, fresh_rot, table, lengths, counts, rank, send_index, cache_latent, cache_rope)
    context = lax.map(per_rank, (q_latent.reshape(N_DP, TOK_RANK, HEADS, LAT), q_rope.reshape(N_DP, TOK_RANK, HEADS * ROPE), new_latent.reshape(N_DP, TOK_RANK, LAT), new_rope.reshape(N_DP, TOK_RANK, ROPE), block_table, cached_len, new_counts, jnp.arange(N_DP).astype(jnp.int32)))
    return (hidden_out, new_latent, new_rope, context.reshape(TOKENS, HEADS, LAT))
```

```python
import functools

import jax
import jax.numpy as jnp
from jax import lax
from jax.experimental import pallas as pl
from jax.experimental.pallas import tpu as pltpu
from jax.sharding import Mesh
from jax.sharding import PartitionSpec as P

SCORE_SCALE = 192.0 ** (-0.5)
LOG2E = 1.4426950408889634
ROPE_BASE = 10000.0
NORM_EPS = 1e-06
BIG = -1e30

N_DP = 32
CHATS = 4
MAXB = 32
BLOCK = 128
LAT = 512
ROPE = 64
TOK = 64
HEADS_DEV = 16
GROUP = 2
TILE = 16
SLOTS = 2 * N_DP + CHATS * (GROUP - 1) + 2


def rotate(values, positions):
    half = values.shape[-1] // 2
    exponent = jnp.arange(half).astype(jnp.float32) * (-2.0 / values.shape[-1])
    frequency = jnp.power(jnp.float32(ROPE_BASE), exponent)
    angle = positions.astype(jnp.float32)[:, None] * frequency[None, :]
    first = values[:, :half]
    second = values[:, half:]
    cosine = jnp.cos(angle)
    sine = jnp.sin(angle)
    return jnp.concatenate([first * cosine - second * sine, second * cosine + first * sine], axis=1)


def chat_positions(counts, lengths, local):
    ends = jnp.cumsum(counts)
    chat_of = jnp.sum((local[:, None] >= ends[None, :]).astype(jnp.int32), axis=1)
    starts = ends - counts
    onehot = (chat_of[:, None] == jnp.arange(counts.shape[0])[None, :]).astype(jnp.int32)
    return jnp.sum(onehot * (lengths - starts)[None, :], axis=1) + local


def attend_kernel(
    table, lengths, counts, where, own_kv, sib_kv, q_own, q_par, r_own, r_par,
    o_own, o_par, s_own, s_par, held, place, sems,
):
    zh, core = where[0], where[1]
    heads = q_own.shape[1]
    rows = TILE * heads

    def copy_in(ref, source, slot):
        return pltpu.make_async_copy(ref.at[source], held.at[slot], sems.at[slot])

    def fetch(holder, slot):
        source = lax.shift_right_logical(holder, 2)

        @pl.when((holder & 1) == core)
        def _():
            copy_in(own_kv, source, slot).start()

        @pl.when((holder & 1) != core)
        def _():
            copy_in(sib_kv, source, slot).start()

    begins, ends = [], []
    slot = jnp.int32(0)
    for chat in range(CHATS):
        length = lengths[0, chat]
        begins.append(slot)

        def step(j, carry):
            slot, last = carry
            holder = table[0, chat * MAXB + j]
            mine = (j * BLOCK < length) & ((lax.shift_right_logical(holder, 1) & 1) == zh)

            @pl.when(mine)
            def _():
                place[slot] = jnp.clip(length - j * BLOCK, 0, BLOCK)
                fetch(holder, slot)

            return jnp.where(mine, slot + 1, slot), jnp.where(mine, holder, last)

        slot, last = lax.fori_loop(0, MAXB, step, (slot, jnp.int32(0)))
        pad = lax.rem(GROUP - lax.rem(slot, GROUP), GROUP)

        def fill(i, carry):
            place[carry] = 0
            fetch(last, carry)
            return carry + 1

        slot = lax.fori_loop(0, pad, fill, slot)
        ends.append(slot)
    total_slots = slot

    def arrive(i, carry):
        copy_in(own_kv, 0, i).wait()
        return carry

    start = jnp.int32(0)
    arrived = jnp.int32(0)
    lane = lax.broadcasted_iota(jnp.int32, (1, BLOCK), 1)
    contract = (((1,), (1,)), ((), ()))
    for chat in range(CHATS):
        count = counts[0, chat]
        first_group = lax.div(begins[chat], GROUP)
        n_groups = lax.div(ends[chat] - begins[chat], GROUP)
        lax.fori_loop(begins[chat], ends[chat], arrive, 0)

        def tile(t, carry):
            base = jnp.minimum(start + t * TILE, TOK - TILE)
            queries = [
                (q[pl.ds(base, TILE)].reshape(rows, LAT), r[pl.ds(base, TILE)].reshape(rows, ROPE))
                for q, r in ((q_own, r_own), (q_par, r_par))
            ]

            def group(g, state):
                at = (first_group + g) * GROUP
                blocks = [held[at + i] for i in range(GROUP)]
                keys = jnp.concatenate([b[:BLOCK] for b in blocks], axis=0)
                ropes = jnp.concatenate(
                    [
                        jnp.concatenate(
                            [b[BLOCK:, k * BLOCK : (k + 1) * BLOCK] for k in range(LAT // BLOCK)],
                            axis=0,
                        )
                        for b in blocks
                    ],
                    axis=1,
                )
                valid = jnp.concatenate([lane < place[at + i] for i in range(GROUP)], axis=1)
                new = []
                for (ql, qr), (m, l, acc) in zip(queries, state):
                    s = lax.dot_general(ql, keys, contract, preferred_element_type=jnp.float32)
                    s = s + jnp.dot(qr, ropes, preferred_element_type=jnp.float32)
                    s = jnp.where(valid, s * (SCORE_SCALE * LOG2E), BIG)
                    m_new = jnp.maximum(m, jnp.max(s, axis=1, keepdims=True))
                    p = jnp.exp2(s - m_new)
                    alpha = jnp.exp2(m - m_new)
                    l = l * alpha + jnp.sum(p, axis=1, keepdims=True)
                    acc = acc * alpha + jnp.dot(
                        p.astype(jnp.bfloat16), keys, preferred_element_type=jnp.float32
                    )
                    new.append((m_new, l, acc))
                return tuple(new)

            empty = (
                jnp.full((rows, 1), BIG, jnp.float32),
                jnp.zeros((rows, 1), jnp.float32),
                jnp.zeros((rows, LAT), jnp.float32),
            )
            state = lax.fori_loop(0, n_groups, group, (empty, empty))
            token = base + lax.broadcasted_iota(jnp.int32, (TILE, 1, 1), 0)
            keep = (token >= start) & (token < start + count)
            for (m, l, acc), o, s in zip(state, (o_own, o_par), (s_own, s_par)):
                some = l > 0.0
                safe = jnp.where(some, l, 1.0)
                value = (acc / safe).astype(jnp.bfloat16).reshape(TILE, heads, LAT)
                lse = jnp.where(some, m + jnp.log2(safe), BIG)
                lse = jnp.broadcast_to(lse, (rows, BLOCK)).reshape(TILE, heads, BLOCK)
                o[pl.ds(base, TILE)] = jnp.where(keep, value, o[pl.ds(base, TILE)])
                s[pl.ds(base, TILE)] = jnp.where(keep, lse, s[pl.ds(base, TILE)])
            return carry

        lax.fori_loop(0, lax.div(count + TILE - 1, TILE), tile, 0)
        start = start + count


def attend(table, lengths, counts, where, own_kv, sib_kv, q_own, q_par, r_own, r_par):
    smem = pl.BlockSpec(memory_space=pltpu.SMEM)
    vmem = pl.BlockSpec(memory_space=pltpu.VMEM)
    hbm = pl.BlockSpec(memory_space=pl.ANY)
    tok, heads, width = q_own.shape
    out = jax.ShapeDtypeStruct((tok, heads, width), jnp.bfloat16)
    stat = jax.ShapeDtypeStruct((tok, heads, BLOCK), jnp.float32)
    return pl.pallas_call(
        attend_kernel,
        out_shape=(out, out, stat, stat),
        in_specs=[smem] * 4 + [hbm] * 2 + [vmem] * 4,
        out_specs=(vmem,) * 4,
        scratch_shapes=[
            pltpu.VMEM((SLOTS,) + own_kv.shape[1:], jnp.bfloat16),
            pltpu.SMEM((SLOTS,), jnp.int32),
            pltpu.SemaphoreType.DMA((SLOTS,)),
        ],
        compiler_params=pltpu.CompilerParams(vmem_limit_bytes=48 * 2**20),
        cost_estimate=pl.CostEstimate(
            flops=9 * 10**9, bytes_accessed=12 * 2**20, transcendentals=4 * 2**20
        ),
        name="attend",
    )(table, lengths, counts, where, own_kv, sib_kv, q_own, q_par, r_own, r_par)


def finish_kernel(q_ref, r_ref, fresh_ref, fresh_rope_ref, ok_ref, oa, ob, sa, sb, out_ref):
    heads = q_ref.shape[1]
    contract = (((1,), (1,)), ((), ()))
    fresh = fresh_ref[...]
    fresh_rope = fresh_rope_ref[...]

    def tile(t, carry):
        at = pl.ds(t * TILE, TILE)
        rows = TILE * heads
        s = lax.dot_general(
            q_ref[at].reshape(rows, LAT), fresh, contract, preferred_element_type=jnp.float32
        ) + lax.dot_general(
            r_ref[at].reshape(rows, ROPE), fresh_rope, contract, preferred_element_type=jnp.float32
        )
        ok = ok_ref[at]
        ok = jnp.broadcast_to(ok[:, None, :], (TILE, heads, TOK)).reshape(rows, TOK)
        s = jnp.where(ok > 0.0, s * (SCORE_SCALE * LOG2E), BIG)
        la = sa[at].reshape(rows, BLOCK)[:, :1]
        lb = sb[at].reshape(rows, BLOCK)[:, :1]
        m = jnp.maximum(jnp.maximum(la, lb), jnp.max(s, axis=1, keepdims=True))
        p = jnp.where(ok > 0.0, jnp.exp2(s - m), 0.0)
        wa = jnp.exp2(la - m)
        wb = jnp.exp2(lb - m)
        total = wa + wb + jnp.sum(p, axis=1, keepdims=True)
        mixed = jnp.dot(p.astype(jnp.bfloat16), fresh, preferred_element_type=jnp.float32)
        mixed = mixed + wa * oa[at].reshape(rows, LAT).astype(jnp.float32)
        mixed = mixed + wb * ob[at].reshape(rows, LAT).astype(jnp.float32)
        out_ref[at] = (mixed / total).astype(jnp.bfloat16).reshape(TILE, heads, LAT)
        return carry

    lax.fori_loop(0, TOK // TILE, tile, 0)


def finish(q_own, r_own, fresh, fresh_rope, ok, oa, ob, sa, sb):
    vmem = pl.BlockSpec(memory_space=pltpu.VMEM)
    return pl.pallas_call(
        finish_kernel,
        out_shape=jax.ShapeDtypeStruct(q_own.shape, jnp.bfloat16),
        in_specs=[vmem] * 9,
        out_specs=vmem,
        compiler_params=pltpu.CompilerParams(vmem_limit_bytes=32 * 2**20),
        name="finish",
    )(q_own, r_own, fresh, fresh_rope, ok, oa, ob, sa, sb)


def swap(value, axis):
    return lax.ppermute(value, axis, [(0, 1), (1, 0)])


def expert_rows(flat_rows, gate_matrix, up_matrix, down_matrix):
    gate = jnp.dot(flat_rows, gate_matrix, preferred_element_type=jnp.float32)
    lifted = jnp.dot(flat_rows, up_matrix, preferred_element_type=jnp.float32)
    activated = (jax.nn.silu(gate) * lifted).astype(jnp.bfloat16)
    return jnp.dot(activated, down_matrix, preferred_element_type=jnp.float32).astype(jnp.bfloat16)


def shards(
    hidden_in,
    expert_ids,
    gate_vals,
    w_gate,
    w_up,
    w_down,
    w_latent,
    w_rope,
    latent_gain,
    cache_latent,
    cache_rope,
    send_index,
    block_table,
    cached_len,
    new_counts,
    q_latent,
    q_rope,
):
    zh, core = lax.axis_index("zh"), lax.axis_index("core")
    rows, width = hidden_in.shape
    fan_count = expert_ids.shape[1]
    capacity = rows // 2
    slots = N_DP * capacity

    flat_ids = expert_ids.reshape(-1)
    onehot = (flat_ids[:, None] == jnp.arange(N_DP)[None, :]).astype(jnp.int32)
    before = jnp.cumsum(onehot, axis=0) - onehot
    target = flat_ids * capacity + jnp.sum(before * onehot, axis=1)
    match = (target[:, None] == jnp.arange(slots)[None, :]).astype(jnp.float32)
    picks = jnp.sum(match.reshape(rows, fan_count, slots), axis=1)
    weights = jnp.sum(
        (match * gate_vals.reshape(-1)[:, None]).reshape(rows, fan_count, slots), axis=1
    )
    outgoing = lax.dot_general(
        picks.astype(jnp.bfloat16),
        hidden_in,
        (((0,), (0,)), ((), ())),
        preferred_element_type=jnp.float32,
    ).astype(jnp.bfloat16)
    spread = jnp.broadcast_to(
        outgoing.reshape(N_DP, 1, capacity, width), (N_DP, 2, capacity, width)
    ).reshape(N_DP * 2, capacity, width)
    arrived = lax.all_to_all(spread, ("dp", "zh"), split_axis=0, concat_axis=0, tiled=True)
    arrived = arrived.reshape(-1, width)
    arrived_sib = swap(arrived, "core")

    packed = jnp.concatenate(
        [cache_rope[:, 16 * k : 16 * (k + 1), :] for k in range(LAT // BLOCK)], axis=2
    )
    blocks = jnp.concatenate([cache_latent, packed], axis=1)[send_index[0]]
    own_kv = lax.all_to_all(blocks, "dp", split_axis=0, concat_axis=0, tiled=True)
    sib_kv = swap(own_kv, "core")
    r_own = q_rope.reshape(TOK, HEADS_DEV, ROPE)
    q_par = swap(q_latent, "zh")
    r_par = swap(q_rope, "zh").reshape(TOK, HEADS_DEV, ROPE)

    matrices = (w_gate[0], w_up[0], w_down[0])
    theirs = expert_rows(arrived_sib, *matrices)
    mine = expert_rows(arrived, *matrices)
    partial = (mine.astype(jnp.float32) + swap(theirs, "core").astype(jnp.float32)).astype(
        jnp.bfloat16
    )
    returned = lax.all_to_all(
        partial.reshape(N_DP * 2, capacity, width),
        ("dp", "zh"),
        split_axis=0,
        concat_axis=0,
        tiled=True,
    )
    summed = jnp.sum(
        returned.reshape(N_DP, 2, capacity, width), axis=1, dtype=jnp.float32
    ).reshape(slots, width)
    mixed = jnp.dot(
        weights,
        summed,
        precision=lax.Precision.HIGHEST,
        preferred_element_type=jnp.float32,
    )
    hidden_out = (hidden_in.astype(jnp.float32) + mixed).astype(jnp.bfloat16)
    latent = jnp.dot(hidden_out, w_latent, preferred_element_type=jnp.float32)
    norm_scale = lax.rsqrt(jnp.mean(latent * latent, axis=1, keepdims=True) + NORM_EPS)
    new_latent = (latent * norm_scale * latent_gain[None, :]).astype(jnp.bfloat16)
    counts = new_counts[0]
    pool = zh * 2 + core
    local = pool * rows + jnp.arange(rows, dtype=jnp.int32)
    positions = chat_positions(counts, cached_len[0], local)
    new_rope = rotate(
        jnp.dot(hidden_out, w_rope, preferred_element_type=jnp.float32), positions
    ).astype(jnp.bfloat16)

    fresh = jnp.concatenate([new_latent, new_rope], axis=1)
    pair = jnp.stack([fresh, swap(fresh, "core")])
    pair = jnp.where(core == 0, pair, pair[::-1])
    quad = jnp.stack([pair, swap(pair, "zh")])
    quad = jnp.where(zh == 0, quad, quad[::-1]).reshape(TOK, LAT + ROPE)

    where = jnp.stack([zh, core]).astype(jnp.int32)
    o_own, o_par, s_own, s_par = attend(
        block_table.reshape(1, CHATS * MAXB),
        cached_len,
        new_counts,
        where,
        own_kv,
        sib_kv,
        q_latent,
        q_par,
        r_own,
        r_par,
    )
    o_back = swap(o_par, "zh")
    s_back = swap(s_par[:, :, 0], "zh")
    s_back = jnp.broadcast_to(s_back[:, :, None], s_own.shape)
    tokens = jnp.arange(TOK, dtype=jnp.int32)
    ends = jnp.cumsum(counts)
    chat_of = jnp.sum((tokens[:, None] >= ends[None, :]).astype(jnp.int32), axis=1)
    ok = (chat_of[:, None] == chat_of[None, :]) & (tokens[None, :] <= tokens[:, None])
    context = finish(
        q_latent,
        r_own,
        quad[:, :LAT],
        quad[:, LAT:],
        ok.astype(jnp.float32),
        o_own,
        o_back,
        s_own,
        s_back,
    )
    return (hidden_out, new_latent, new_rope, context)


def solution(mesh):
    whole = Mesh(mesh.devices.reshape(N_DP, 2, 2), ("dp", "zh", "core"))
    every = ("dp", "zh", "core")
    pool = ("zh", "core")
    return jax.shard_map(
        shards,
        mesh=whole,
        in_specs=(
            P(every, None),
            P(every, None),
            P(every, None),
            P("dp", None, pool),
            P("dp", None, pool),
            P("dp", pool, None),
            P(),
            P(),
            P(),
            P(every, None, None),
            P(every, None, None),
            P(every, None),
            P("dp", None, None),
            P("dp", None),
            P("dp", None),
            P("dp", pool, None),
            P("dp", pool),
        ),
        out_specs=(
            P(every, None),
            P(every, None),
            P(every, None),
            P("dp", pool, None),
        ),
        check_vma=False,
    )
```

```python
import functools

import jax
import jax.numpy as jnp
from jax import lax
from jax.experimental import pallas as pl
from jax.experimental.pallas import tpu as pltpu
from jax.sharding import Mesh
from jax.sharding import PartitionSpec as P

SCORE_SCALE = 192.0 ** (-0.5)
LOG2E = 1.4426950408889634
ROPE_BASE = 10000.0
NORM_EPS = 1e-06
BIG = -1e30

N_DP = 32
CHATS = 4
MAXB = 32
BLOCK = 128
LAT = 512
ROPE = 64
TOK = 64
HEADS_DEV = 16
GROUP = 2
TILE = 16
SLOTS = 2 * N_DP + CHATS * (GROUP - 1) + 2


def rotate(values, positions):
    half = values.shape[-1] // 2
    exponent = jnp.arange(half).astype(jnp.float32) * (-2.0 / values.shape[-1])
    frequency = jnp.power(jnp.float32(ROPE_BASE), exponent)
    angle = positions.astype(jnp.float32)[:, None] * frequency[None, :]
    first = values[:, :half]
    second = values[:, half:]
    cosine = jnp.cos(angle)
    sine = jnp.sin(angle)
    return jnp.concatenate([first * cosine - second * sine, second * cosine + first * sine], axis=1)


def chat_positions(counts, lengths, local):
    ends = jnp.cumsum(counts)
    chat_of = jnp.sum((local[:, None] >= ends[None, :]).astype(jnp.int32), axis=1)
    starts = ends - counts
    onehot = (chat_of[:, None] == jnp.arange(counts.shape[0])[None, :]).astype(jnp.int32)
    return jnp.sum(onehot * (lengths - starts)[None, :], axis=1) + local


def attend_kernel(
    table, lengths, counts, where, own_kv, sib_kv, q_own, q_par, r_own, r_par,
    o_own, o_par, s_own, s_par, held, place, sems,
):
    zh, core, low = where[0], where[1], where[2]
    heads = q_own.shape[1]
    rows = TILE * heads

    def copy_in(ref, source, slot):
        return pltpu.make_async_copy(ref.at[source], held.at[slot], sems.at[slot])

    def fetch(holder, slot):
        source = lax.shift_right_logical(holder, 2)

        @pl.when((holder & 1) == core)
        def _():
            copy_in(own_kv, source, slot).start()

        @pl.when((holder & 1) != core)
        def _():
            copy_in(sib_kv, source, slot).start()

    begins, ends = [], []
    slot = jnp.int32(0)
    for chat in range(CHATS):
        length = lengths[0, chat]
        begins.append(slot)

        def step(j, carry):
            slot, last = carry
            holder = table[0, chat * MAXB + j]
            z = (lax.shift_right_logical(holder, 1) & 1) * 2 + (
                lax.shift_right_logical(holder, 2) & 1
            )
            step_z = jnp.where((z & 1) == low, 0, 1 + 2 * (holder & 1))
            mine = (j * BLOCK < length) & (lax.shift_right_logical((z + step_z) & 3, 1) == zh)

            @pl.when(mine)
            def _():
                place[slot] = jnp.clip(length - j * BLOCK, 0, BLOCK)
                fetch(holder, slot)

            return jnp.where(mine, slot + 1, slot), jnp.where(mine, holder, last)

        slot, last = lax.fori_loop(0, MAXB, step, (slot, jnp.int32(0)))
        pad = lax.rem(GROUP - lax.rem(slot, GROUP), GROUP)

        def fill(i, carry):
            place[carry] = 0
            fetch(last, carry)
            return carry + 1

        slot = lax.fori_loop(0, pad, fill, slot)
        ends.append(slot)
    total_slots = slot

    def arrive(i, carry):
        copy_in(own_kv, 0, i).wait()
        return carry

    start = jnp.int32(0)
    arrived = jnp.int32(0)
    lane = lax.broadcasted_iota(jnp.int32, (1, BLOCK), 1)
    contract = (((1,), (1,)), ((), ()))
    for chat in range(CHATS):
        count = counts[0, chat]
        first_group = lax.div(begins[chat], GROUP)
        n_groups = lax.div(ends[chat] - begins[chat], GROUP)
        lax.fori_loop(begins[chat], ends[chat], arrive, 0)

        def tile(t, carry):
            base = jnp.minimum(start + t * TILE, TOK - TILE)
            queries = [
                (q[pl.ds(base, TILE)].reshape(rows, LAT), r[pl.ds(base, TILE)].reshape(rows, ROPE))
                for q, r in ((q_own, r_own), (q_par, r_par))
            ]

            def group(g, state):
                at = (first_group + g) * GROUP
                blocks = [held[at + i] for i in range(GROUP)]
                keys = jnp.concatenate([b[:BLOCK] for b in blocks], axis=0)
                ropes = jnp.concatenate(
                    [
                        jnp.concatenate(
                            [b[BLOCK:, k * BLOCK : (k + 1) * BLOCK] for k in range(LAT // BLOCK)],
                            axis=0,
                        )
                        for b in blocks
                    ],
                    axis=1,
                )
                valid = jnp.concatenate([lane < place[at + i] for i in range(GROUP)], axis=1)
                new = []
                for (ql, qr), (m, l, acc) in zip(queries, state):
                    s = lax.dot_general(ql, keys, contract, preferred_element_type=jnp.float32)
                    s = s + jnp.dot(qr, ropes, preferred_element_type=jnp.float32)
                    s = jnp.where(valid, s * (SCORE_SCALE * LOG2E), BIG)
                    m_new = jnp.maximum(m, jnp.max(s, axis=1, keepdims=True))
                    p = jnp.exp2(s - m_new)
                    alpha = jnp.exp2(m - m_new)
                    l = l * alpha + jnp.sum(p, axis=1, keepdims=True)
                    acc = acc * alpha + jnp.dot(
                        p.astype(jnp.bfloat16), keys, preferred_element_type=jnp.float32
                    )
                    new.append((m_new, l, acc))
                return tuple(new)

            empty = (
                jnp.full((rows, 1), BIG, jnp.float32),
                jnp.zeros((rows, 1), jnp.float32),
                jnp.zeros((rows, LAT), jnp.float32),
            )
            state = lax.fori_loop(0, n_groups, group, (empty, empty))
            token = base + lax.broadcasted_iota(jnp.int32, (TILE, 1, 1), 0)
            keep = (token >= start) & (token < start + count)
            for (m, l, acc), o, s in zip(state, (o_own, o_par), (s_own, s_par)):
                some = l > 0.0
                safe = jnp.where(some, l, 1.0)
                value = (acc / safe).astype(jnp.bfloat16).reshape(TILE, heads, LAT)
                lse = jnp.where(some, m + jnp.log2(safe), BIG)
                lse = jnp.broadcast_to(lse, (rows, BLOCK)).reshape(TILE, heads, BLOCK)
                o[pl.ds(base, TILE)] = jnp.where(keep, value, o[pl.ds(base, TILE)])
                s[pl.ds(base, TILE)] = jnp.where(keep, lse, s[pl.ds(base, TILE)])
            return carry

        lax.fori_loop(0, lax.div(count + TILE - 1, TILE), tile, 0)
        start = start + count


def attend(table, lengths, counts, where, own_kv, sib_kv, q_own, q_par, r_own, r_par):
    smem = pl.BlockSpec(memory_space=pltpu.SMEM)
    vmem = pl.BlockSpec(memory_space=pltpu.VMEM)
    hbm = pl.BlockSpec(memory_space=pl.ANY)
    tok, heads, width = q_own.shape
    out = jax.ShapeDtypeStruct((tok, heads, width), jnp.bfloat16)
    stat = jax.ShapeDtypeStruct((tok, heads, BLOCK), jnp.float32)
    return pl.pallas_call(
        attend_kernel,
        out_shape=(out, out, stat, stat),
        in_specs=[smem] * 4 + [hbm] * 2 + [vmem] * 4,
        out_specs=(vmem,) * 4,
        scratch_shapes=[
            pltpu.VMEM((SLOTS,) + own_kv.shape[1:], jnp.bfloat16),
            pltpu.SMEM((SLOTS,), jnp.int32),
            pltpu.SemaphoreType.DMA((SLOTS,)),
        ],
        compiler_params=pltpu.CompilerParams(vmem_limit_bytes=48 * 2**20),
        cost_estimate=pl.CostEstimate(
            flops=9 * 10**9, bytes_accessed=12 * 2**20, transcendentals=4 * 2**20
        ),
        name="attend",
    )(table, lengths, counts, where, own_kv, sib_kv, q_own, q_par, r_own, r_par)


def finish_kernel(q_ref, r_ref, fresh_ref, fresh_rope_ref, ok_ref, oa, ob, sa, sb, out_ref):
    heads = q_ref.shape[1]
    contract = (((1,), (1,)), ((), ()))
    fresh = fresh_ref[...]
    fresh_rope = fresh_rope_ref[...]

    def tile(t, carry):
        at = pl.ds(t * TILE, TILE)
        rows = TILE * heads
        s = lax.dot_general(
            q_ref[at].reshape(rows, LAT), fresh, contract, preferred_element_type=jnp.float32
        ) + lax.dot_general(
            r_ref[at].reshape(rows, ROPE), fresh_rope, contract, preferred_element_type=jnp.float32
        )
        ok = ok_ref[at]
        ok = jnp.broadcast_to(ok[:, None, :], (TILE, heads, TOK)).reshape(rows, TOK)
        s = jnp.where(ok > 0.0, s * (SCORE_SCALE * LOG2E), BIG)
        la = sa[at].reshape(rows, BLOCK)[:, :1]
        lb = sb[at].reshape(rows, BLOCK)[:, :1]
        m = jnp.maximum(jnp.maximum(la, lb), jnp.max(s, axis=1, keepdims=True))
        p = jnp.where(ok > 0.0, jnp.exp2(s - m), 0.0)
        wa = jnp.exp2(la - m)
        wb = jnp.exp2(lb - m)
        total = wa + wb + jnp.sum(p, axis=1, keepdims=True)
        mixed = jnp.dot(p.astype(jnp.bfloat16), fresh, preferred_element_type=jnp.float32)
        mixed = mixed + wa * oa[at].reshape(rows, LAT).astype(jnp.float32)
        mixed = mixed + wb * ob[at].reshape(rows, LAT).astype(jnp.float32)
        out_ref[at] = (mixed / total).astype(jnp.bfloat16).reshape(TILE, heads, LAT)
        return carry

    lax.fori_loop(0, TOK // TILE, tile, 0)


def finish(q_own, r_own, fresh, fresh_rope, ok, oa, ob, sa, sb):
    vmem = pl.BlockSpec(memory_space=pltpu.VMEM)
    return pl.pallas_call(
        finish_kernel,
        out_shape=jax.ShapeDtypeStruct(q_own.shape, jnp.bfloat16),
        in_specs=[vmem] * 9,
        out_specs=vmem,
        compiler_params=pltpu.CompilerParams(vmem_limit_bytes=32 * 2**20),
        name="finish",
    )(q_own, r_own, fresh, fresh_rope, ok, oa, ob, sa, sb)

MESH = pl.DeviceIdType.MESH
SENDS = 2 * N_DP
CHUNK = 32


def shifted(dy, dx, dz, sign):
    dp, zh = lax.axis_index("dp"), lax.axis_index("zh")
    y, x, z = lax.div(dp, 8), lax.rem(lax.div(dp, 2), 4), zh * 2 + lax.rem(dp, 2)
    y = lax.rem(y + 4 + sign * dy, 4)
    x = lax.rem(x + 4 + sign * dx, 4)
    z = lax.rem(z + 4 + sign * dz, 4)
    return y * 8 + x * 2 + lax.rem(z, 2), lax.div(z, 2)


def row_place(i, sign):
    j = lax.rem(i * 37, SENDS)
    return shifted(lax.div(j, 16), lax.rem(lax.div(j, 4), 4), lax.rem(j, 4), sign)


def block_place(i, sign):
    j = lax.rem(i * 11, N_DP)
    core = lax.axis_index("core")
    dz = lax.rem(j, 2) * (1 + 2 * core)
    return shifted(lax.div(j, 8), lax.rem(lax.div(j, 2), 4), dz, sign)


def feed_kernel(
    rows, cache, send, q, r, wg_hbm, wu_hbm, wd_hbm,
    own_kv, sib_kv, q_par, r_par, out,
    wg, wu, wd, arr, arr_sib, stage, acts, part, part_sib, part_in,
    w_sem, row_send, row_recv, fwd_send, fwd_recv, part_send, part_recv,
    kv_send, kv_recv, kvf_send, kvf_recv, misc_send, misc_recv,
):
    dp, zh, core = lax.axis_index("dp"), lax.axis_index("zh"), lax.axis_index("core")
    sibling = (dp, zh, 1 - core)
    partner = (dp, 1 - zh, core)
    loads = [
        pltpu.make_async_copy(a, b, w_sem.at[i])
        for i, (a, b) in enumerate(((wg_hbm, wg), (wu_hbm, wu), (wd_hbm, wd)))
    ]
    for load in loads:
        load.start()

    barrier = pltpu.get_barrier_semaphore()

    def greet(i, carry):
        to, to_zh = row_place(i, 1)
        pl.semaphore_signal(barrier, inc=1, device_id=(to, to_zh, core), device_id_type=MESH)
        return carry

    lax.fori_loop(1, SENDS, greet, 0)
    pl.semaphore_signal(barrier, inc=1, device_id=sibling, device_id_type=MESH)
    pl.semaphore_wait(barrier, SENDS)

    def remote(src, dst, send_sem, recv_sem, device):
        return pltpu.make_async_remote_copy(
            src_ref=src, dst_ref=dst, send_sem=send_sem, recv_sem=recv_sem,
            device_id=device, device_id_type=MESH,
        )

    def row_copy(i):
        to, to_zh = row_place(i, 1)
        return remote(rows.at[to], arr.at[i], row_send.at[i], row_recv.at[i], (to, to_zh, core))

    def fwd_copy(i):
        return remote(arr.at[i], arr_sib.at[i], fwd_send.at[i], fwd_recv.at[i], sibling)

    def part_copy(c):
        at = pl.ds(c * CHUNK, CHUNK)
        return remote(
            part_sib.at[at], part_in.at[at], part_send.at[c], part_recv.at[c], sibling
        )

    def kv_copy(i):
        to, to_zh = block_place(i, 1)
        return remote(
            stage.at[i], own_kv.at[dp], kv_send.at[i], kv_recv.at[i], (to, to_zh, core)
        )

    def kvf_copy(i):
        source, _ = block_place(i, -1)
        return remote(
            own_kv.at[source], sib_kv.at[source], kvf_send.at[i], kvf_recv.at[i], sibling
        )

    def start_rows(i, carry):
        row_copy(i).start()
        return carry

    lax.fori_loop(1, SENDS, start_rows, 0)
    arr[0] = rows[dp]

    q_copy = remote(q, q_par, misc_send.at[0], misc_recv.at[0], partner)
    r_copy = remote(r, r_par, misc_send.at[1], misc_recv.at[1], partner)
    q_copy.start()
    r_copy.start()

    def start_blocks(i, carry):
        to, _ = block_place(i, 1)
        stage[i] = cache[send[0, to]]
        kv_copy(i).start()
        return carry

    lax.fori_loop(1, N_DP, start_blocks, 0)
    stage[0] = cache[send[0, dp]]
    mine = pltpu.make_async_copy(stage.at[0], own_kv.at[dp], kv_send.at[0])
    mine.start()
    mine_fwd = remote(stage.at[0], sib_kv.at[dp], kvf_send.at[0], kvf_recv.at[0], sibling)
    mine_fwd.start()
    for load in loads:
        load.wait()

    def experts(source, target, c):
        at = pl.ds(c * CHUNK, CHUNK)
        x = source[at].reshape(CHUNK * source.shape[1], source.shape[2])
        for n in range(2):
            cut = slice(n * 256, (n + 1) * 256)
            gate = jnp.dot(x, wg[:, cut], preferred_element_type=jnp.float32)
            lifted = jnp.dot(x, wu[:, cut], preferred_element_type=jnp.float32)
            acts[:, cut] = (gate / (1.0 + jnp.exp(-gate)) * lifted).astype(jnp.bfloat16)

        def down(n, carry):
            cut = pl.ds(pl.multiple_of(n * 512, 512), 512)
            value = jnp.dot(acts[...], wd[:, cut], preferred_element_type=jnp.float32)
            target[at, :, cut] = value.astype(jnp.bfloat16).reshape(CHUNK, source.shape[1], 512)
            return carry

        lax.fori_loop(0, source.shape[2] // 512, down, 0)

    def chunk(c, carry):
        first = c * CHUNK

        def pass_on(i, carry):
            @pl.when(i > 0)
            def _():
                row_copy(i).wait_recv()

            fwd_copy(i).start()
            return carry

        lax.fori_loop(first, first + CHUNK, pass_on, 0)
        experts(arr, part, c)

        def await_sib(i, carry):
            fwd_copy(i).wait_recv()
            return carry

        lax.fori_loop(first, first + CHUNK, await_sib, 0)
        experts(arr_sib, part_sib, c)
        part_copy(c).start()
        return carry

    lax.fori_loop(0, SENDS // CHUNK, chunk, 0)

    def pass_block(i, carry):
        kv_copy(i).wait_recv()
        kvf_copy(i).start()
        return carry

    lax.fori_loop(1, N_DP, pass_block, 0)

    def add_up(i, carry):
        source, source_zh = row_place(i, -1)
        total = part[i].astype(jnp.float32) + part_in[i].astype(jnp.float32)
        out[source * 2 + source_zh] = total.astype(jnp.bfloat16)
        return carry

    def add_chunk(c, carry):
        part_copy(c).wait()
        lax.fori_loop(c * CHUNK, (c + 1) * CHUNK, add_up, 0)
        return carry

    lax.fori_loop(0, SENDS // CHUNK, add_chunk, 0)

    def end_rows(i, carry):
        row_copy(i).wait_send()
        return carry

    lax.fori_loop(1, SENDS, end_rows, 0)

    def end_fwd(i, carry):
        fwd_copy(i).wait_send()
        return carry

    lax.fori_loop(0, SENDS, end_fwd, 0)

    def end_blocks(i, carry):
        kv_copy(i).wait_send()
        kvf_copy(i).wait()
        return carry

    lax.fori_loop(1, N_DP, end_blocks, 0)
    mine.wait()
    mine_fwd.wait()
    q_copy.wait()
    r_copy.wait()


def feed(rows, cache, send, q, r, wg, wu, wd):
    smem = pl.BlockSpec(memory_space=pltpu.SMEM)
    vmem = pl.BlockSpec(memory_space=pltpu.VMEM)
    hbm = pl.BlockSpec(memory_space=pl.ANY)
    bf16 = jnp.bfloat16
    blocks = jax.ShapeDtypeStruct((N_DP,) + cache.shape[1:], bf16)
    chips = (SENDS,) + rows.shape[1:]
    dma = pltpu.SemaphoreType.DMA
    chunks = SENDS // CHUNK
    return pl.pallas_call(
        feed_kernel,
        out_shape=(
            blocks,
            blocks,
            jax.ShapeDtypeStruct(q.shape, bf16),
            jax.ShapeDtypeStruct(r.shape, bf16),
            jax.ShapeDtypeStruct(chips, bf16),
        ),
        in_specs=[vmem, vmem, smem] + [hbm] * 5,
        out_specs=(hbm, hbm, hbm, hbm, vmem),
        scratch_shapes=[
            pltpu.VMEM(wg.shape, bf16),
            pltpu.VMEM(wu.shape, bf16),
            pltpu.VMEM(wd.shape, bf16),
            pltpu.VMEM(chips, bf16),
            pltpu.VMEM(chips, bf16),
            pltpu.VMEM(blocks.shape, bf16),
            pltpu.VMEM((CHUNK * rows.shape[1], wg.shape[1]), bf16),
            pltpu.VMEM(chips, bf16),
            pltpu.VMEM(chips, bf16),
            pltpu.VMEM(chips, bf16),
            dma((3,)),
            dma((SENDS,)), dma((SENDS,)), dma((SENDS,)), dma((SENDS,)),
            dma((chunks,)), dma((chunks,)),
            dma((N_DP,)), dma((N_DP,)), dma((N_DP,)), dma((N_DP,)),
            dma((2,)), dma((2,)),
        ],
        compiler_params=pltpu.CompilerParams(
            collective_id=1, has_side_effects=True, vmem_limit_bytes=56 * 2**20
        ),
        cost_estimate=pl.CostEstimate(
            flops=11 * 10**9, bytes_accessed=24 * 2**20, transcendentals=2**19
        ),
        name="feed",
    )(rows, cache, send, q, r, wg, wu, wd)


def swap(value, axis):
    return lax.ppermute(value, axis, [(0, 1), (1, 0)])


def shards(
    hidden_in,
    expert_ids,
    gate_vals,
    w_gate,
    w_up,
    w_down,
    w_latent,
    w_rope,
    latent_gain,
    cache_latent,
    cache_rope,
    send_index,
    block_table,
    cached_len,
    new_counts,
    q_latent,
    q_rope,
):
    zh, core = lax.axis_index("zh"), lax.axis_index("core")
    rows, width = hidden_in.shape
    fan_count = expert_ids.shape[1]
    capacity = rows // 2
    slots = N_DP * capacity

    flat_ids = expert_ids.reshape(-1)
    onehot = (flat_ids[:, None] == jnp.arange(N_DP)[None, :]).astype(jnp.int32)
    before = jnp.cumsum(onehot, axis=0) - onehot
    target = flat_ids * capacity + jnp.sum(before * onehot, axis=1)
    match = (target[:, None] == jnp.arange(slots)[None, :]).astype(jnp.float32)
    picks = jnp.sum(match.reshape(rows, fan_count, slots), axis=1)
    weights = jnp.sum(
        (match * gate_vals.reshape(-1)[:, None]).reshape(rows, fan_count, slots), axis=1
    )
    outgoing = lax.dot_general(
        picks.astype(jnp.bfloat16),
        hidden_in,
        (((0,), (0,)), ((), ())),
        preferred_element_type=jnp.float32,
    ).astype(jnp.bfloat16)
    packed = jnp.concatenate(
        [cache_rope[:, 16 * k : 16 * (k + 1), :] for k in range(LAT // BLOCK)], axis=2
    )
    cache = jnp.concatenate([cache_latent, packed], axis=1)
    own_kv, sib_kv, q_par, r_par, partial = feed(
        outgoing.reshape(N_DP, capacity, width),
        cache,
        send_index,
        q_latent,
        q_rope,
        w_gate[0],
        w_up[0],
        w_down[0],
    )
    r_own = q_rope.reshape(TOK, HEADS_DEV, ROPE)
    r_par = r_par.reshape(TOK, HEADS_DEV, ROPE)
    returned = lax.all_to_all(
        partial,
        ("dp", "zh"),
        split_axis=0,
        concat_axis=0,
        tiled=True,
    )
    summed = jnp.sum(
        returned.reshape(N_DP, 2, capacity, width), axis=1, dtype=jnp.float32
    ).reshape(slots, width)
    mixed = jnp.dot(
        weights,
        summed,
        precision=lax.Precision.HIGHEST,
        preferred_element_type=jnp.float32,
    )
    hidden_out = (hidden_in.astype(jnp.float32) + mixed).astype(jnp.bfloat16)
    latent = jnp.dot(hidden_out, w_latent, preferred_element_type=jnp.float32)
    norm_scale = lax.rsqrt(jnp.mean(latent * latent, axis=1, keepdims=True) + NORM_EPS)
    new_latent = (latent * norm_scale * latent_gain[None, :]).astype(jnp.bfloat16)
    counts = new_counts[0]
    pool = zh * 2 + core
    local = pool * rows + jnp.arange(rows, dtype=jnp.int32)
    positions = chat_positions(counts, cached_len[0], local)
    new_rope = rotate(
        jnp.dot(hidden_out, w_rope, preferred_element_type=jnp.float32), positions
    ).astype(jnp.bfloat16)

    fresh = jnp.concatenate([new_latent, new_rope], axis=1)
    pair = jnp.stack([fresh, swap(fresh, "core")])
    pair = jnp.where(core == 0, pair, pair[::-1])
    quad = jnp.stack([pair, swap(pair, "zh")])
    quad = jnp.where(zh == 0, quad, quad[::-1]).reshape(TOK, LAT + ROPE)

    where = jnp.stack([zh, core, lax.axis_index("dp") % 2]).astype(jnp.int32)
    o_own, o_par, s_own, s_par = attend(
        block_table.reshape(1, CHATS * MAXB),
        cached_len,
        new_counts,
        where,
        own_kv,
        sib_kv,
        q_latent,
        q_par,
        r_own,
        r_par,
    )
    o_back = swap(o_par, "zh")
    s_back = swap(s_par[:, :, 0], "zh")
    s_back = jnp.broadcast_to(s_back[:, :, None], s_own.shape)
    tokens = jnp.arange(TOK, dtype=jnp.int32)
    ends = jnp.cumsum(counts)
    chat_of = jnp.sum((tokens[:, None] >= ends[None, :]).astype(jnp.int32), axis=1)
    ok = (chat_of[:, None] == chat_of[None, :]) & (tokens[None, :] <= tokens[:, None])
    context = finish(
        q_latent,
        r_own,
        quad[:, :LAT],
        quad[:, LAT:],
        ok.astype(jnp.float32),
        o_own,
        o_back,
        s_own,
        s_back,
    )
    return (hidden_out, new_latent, new_rope, context)


def solution(mesh):
    whole = Mesh(mesh.devices.reshape(N_DP, 2, 2), ("dp", "zh", "core"))
    every = ("dp", "zh", "core")
    pool = ("zh", "core")
    return jax.shard_map(
        shards,
        mesh=whole,
        in_specs=(
            P(every, None),
            P(every, None),
            P(every, None),
            P("dp", None, pool),
            P("dp", None, pool),
            P("dp", pool, None),
            P(),
            P(),
            P(),
            P(every, None, None),
            P(every, None, None),
            P(every, None),
            P("dp", None, None),
            P("dp", None),
            P("dp", None),
            P("dp", pool, None),
            P("dp", pool),
        ),
        out_specs=(
            P(every, None),
            P(every, None),
            P(every, None),
            P("dp", pool, None),
        ),
        check_vma=False,
    )
```

```python
import functools

import jax
import jax.numpy as jnp
from jax import lax
from jax.experimental import pallas as pl
from jax.experimental.pallas import tpu as pltpu
from jax.sharding import Mesh
from jax.sharding import PartitionSpec as P

SCORE_SCALE = 192.0 ** (-0.5)
LOG2E = 1.4426950408889634
ROPE_BASE = 10000.0
NORM_EPS = 1e-06
BIG = -1e30

N_DP = 32
CHATS = 4
MAXB = 32
BLOCK = 128
LAT = 512
ROPE = 64
TOK = 64
HEADS_DEV = 16
GROUP = 4
TILE = 16
SLOTS = 2 * N_DP + CHATS * (GROUP - 1) + 2


def rotate(values, positions):
    half = values.shape[-1] // 2
    exponent = jnp.arange(half).astype(jnp.float32) * (-2.0 / values.shape[-1])
    frequency = jnp.power(jnp.float32(ROPE_BASE), exponent)
    angle = positions.astype(jnp.float32)[:, None] * frequency[None, :]
    first = values[:, :half]
    second = values[:, half:]
    cosine = jnp.cos(angle)
    sine = jnp.sin(angle)
    return jnp.concatenate([first * cosine - second * sine, second * cosine + first * sine], axis=1)


def chat_positions(counts, lengths, local):
    ends = jnp.cumsum(counts)
    chat_of = jnp.sum((local[:, None] >= ends[None, :]).astype(jnp.int32), axis=1)
    starts = ends - counts
    onehot = (chat_of[:, None] == jnp.arange(counts.shape[0])[None, :]).astype(jnp.int32)
    return jnp.sum(onehot * (lengths - starts)[None, :], axis=1) + local


def attend_kernel(
    table, lengths, counts, where, own_kv, sib_kv, q_ref, r_ref, after,
    o_ref, s_ref, held, place, sems, scores,
):
    zh, core, low = where[0], where[1], where[2]
    heads = q_ref.shape[1]
    rows = TILE * heads

    def copy_in(ref, source, slot):
        return pltpu.make_async_copy(ref.at[source], held.at[slot], sems.at[slot])

    def fetch(holder, slot):
        source = lax.shift_right_logical(holder, 2)

        @pl.when((holder & 1) == core)
        def _():
            copy_in(own_kv, source, slot).start()

        @pl.when((holder & 1) != core)
        def _():
            copy_in(sib_kv, source, slot).start()

    begins, ends = [], []
    slot = jnp.int32(0)
    for chat in range(CHATS):
        length = lengths[0, chat]
        begins.append(slot)

        def step(j, carry):
            slot, last = carry
            holder = table[0, chat * MAXB + j]
            z = (lax.shift_right_logical(holder, 1) & 1) * 2 + (
                lax.shift_right_logical(holder, 2) & 1
            )
            step_z = jnp.where((z & 1) == low, 0, 1 + 2 * (holder & 1))
            mine = (j * BLOCK < length) & (lax.shift_right_logical((z + step_z) & 3, 1) == zh)

            @pl.when(mine)
            def _():
                place[slot] = jnp.clip(length - j * BLOCK, 0, BLOCK)
                fetch(holder, slot)

            return jnp.where(mine, slot + 1, slot), jnp.where(mine, holder, last)

        slot, last = lax.fori_loop(0, MAXB, step, (slot, jnp.int32(0)))
        pad = lax.rem(GROUP - lax.rem(slot, GROUP), GROUP)

        def fill(i, carry):
            place[carry] = 0
            fetch(last, carry)
            return carry + 1

        slot = lax.fori_loop(0, pad, fill, slot)
        ends.append(slot)
    total_slots = slot

    def arrive(i, carry):
        copy_in(own_kv, 0, i).wait()
        return carry

    start = jnp.int32(0)
    arrived = jnp.int32(0)
    lane = lax.broadcasted_iota(jnp.int32, (1, BLOCK), 1)
    contract = (((1,), (1,)), ((), ()))
    for chat in range(CHATS):
        count = counts[0, chat]
        first_group = lax.div(begins[chat], GROUP)
        n_groups = lax.div(ends[chat] - begins[chat], GROUP)
        lax.fori_loop(begins[chat], ends[chat], arrive, 0)

        def tile(t, carry):
            base = jnp.minimum(start + t * TILE, TOK - TILE)
            ql = q_ref[pl.ds(base, TILE)].reshape(rows, LAT)
            qr = r_ref[pl.ds(base, TILE)].reshape(rows, ROPE)

            def keys_of(g):
                at = (first_group + g) * GROUP
                blocks = [held[at + i] for i in range(GROUP)]
                return blocks, jnp.concatenate([b[:BLOCK] for b in blocks], axis=0)

            def score(g, best):
                blocks, keys = keys_of(g)
                ropes = jnp.concatenate(
                    [
                        jnp.concatenate(
                            [b[BLOCK:, k * BLOCK : (k + 1) * BLOCK] for k in range(LAT // BLOCK)],
                            axis=0,
                        )
                        for b in blocks
                    ],
                    axis=1,
                )
                at = (first_group + g) * GROUP
                valid = jnp.concatenate([lane < place[at + i] for i in range(GROUP)], axis=1)
                s = lax.dot_general(ql, keys, contract, preferred_element_type=jnp.float32)
                s = s + jnp.dot(qr, ropes, preferred_element_type=jnp.float32)
                s = jnp.where(valid, s * (SCORE_SCALE * LOG2E), BIG)
                scores[g] = s
                for i in range(GROUP):
                    best = jnp.maximum(best, s[:, i * BLOCK : (i + 1) * BLOCK])
                return best

            def blend(g, state, top):
                total, acc = state
                _, keys = keys_of(g)
                p = jnp.exp2(scores[g] - top)
                for i in range(GROUP):
                    total = total + p[:, i * BLOCK : (i + 1) * BLOCK]
                acc = acc + jnp.dot(p.astype(jnp.bfloat16), keys, preferred_element_type=jnp.float32)
                return total, acc

            def over(step, state):
                def two(g, state):
                    return step(2 * g + 1, step(2 * g, state))

                state = lax.fori_loop(0, lax.div(n_groups, 2), two, state)
                return lax.fori_loop(n_groups - lax.rem(n_groups, 2), n_groups, step, state)

            best = over(score, jnp.full((rows, BLOCK), BIG, jnp.float32))
            top = jnp.max(best, axis=1, keepdims=True)
            total, acc = over(
                lambda g, state: blend(g, state, top),
                (jnp.zeros((rows, BLOCK), jnp.float32), jnp.zeros((rows, LAT), jnp.float32)),
            )
            total = jnp.sum(total, axis=1, keepdims=True)
            token = base + lax.broadcasted_iota(jnp.int32, (TILE, 1, 1), 0)
            keep = (token >= start) & (token < start + count)
            some = total > 0.0
            safe = jnp.where(some, total, 1.0)
            value = (acc / safe).astype(jnp.bfloat16).reshape(TILE, heads, LAT)
            lse = jnp.where(some, top + jnp.log2(safe), BIG)
            lse = jnp.broadcast_to(lse, (rows, BLOCK)).reshape(TILE, heads, BLOCK)
            at = pl.ds(base, TILE)
            o_ref[at] = jnp.where(keep, value, o_ref[at])
            s_ref[at] = jnp.where(keep, lse, s_ref[at])
            return carry

        lax.fori_loop(0, lax.div(count + TILE - 1, TILE), tile, 0)
        start = start + count


def attend(table, lengths, counts, where, own_kv, sib_kv, q, r, after, name):
    smem = pl.BlockSpec(memory_space=pltpu.SMEM)
    vmem = pl.BlockSpec(memory_space=pltpu.VMEM)
    hbm = pl.BlockSpec(memory_space=pl.ANY)
    tok, heads, width = q.shape
    return pl.pallas_call(
        attend_kernel,
        out_shape=(
            jax.ShapeDtypeStruct((tok, heads, width), jnp.bfloat16),
            jax.ShapeDtypeStruct((tok, heads, BLOCK), jnp.float32),
        ),
        in_specs=[smem] * 4 + [hbm] * 2 + [vmem] * 2 + [hbm],
        out_specs=(vmem,) * 2,
        scratch_shapes=[
            pltpu.VMEM((SLOTS,) + own_kv.shape[1:], jnp.bfloat16),
            pltpu.SMEM((SLOTS,), jnp.int32),
            pltpu.SemaphoreType.DMA((SLOTS,)),
            pltpu.VMEM((MAXB // GROUP, TILE * heads, GROUP * BLOCK), jnp.float32),
        ],
        compiler_params=pltpu.CompilerParams(vmem_limit_bytes=48 * 2**20),
        cost_estimate=pl.CostEstimate(
            flops=5 * 10**9, bytes_accessed=40 * 2**20, transcendentals=2 * 2**20
        ),
        name=name,
    )(table, lengths, counts, where, own_kv, sib_kv, q, r, after)


def finish_kernel(q_ref, r_ref, fresh_ref, fresh_rope_ref, ok_ref, oa, ob, sa, sb, out_ref):
    heads = q_ref.shape[1]
    contract = (((1,), (1,)), ((), ()))
    fresh = fresh_ref[...]
    fresh_rope = fresh_rope_ref[...]

    def tile(t, carry):
        at = pl.ds(t * TILE, TILE)
        rows = TILE * heads
        s = lax.dot_general(
            q_ref[at].reshape(rows, LAT), fresh, contract, preferred_element_type=jnp.float32
        ) + lax.dot_general(
            r_ref[at].reshape(rows, ROPE), fresh_rope, contract, preferred_element_type=jnp.float32
        )
        ok = ok_ref[at]
        ok = jnp.broadcast_to(ok[:, None, :], (TILE, heads, TOK)).reshape(rows, TOK)
        s = jnp.where(ok > 0.0, s * (SCORE_SCALE * LOG2E), BIG)
        la = sa[at].reshape(rows, BLOCK)[:, :1]
        lb = sb[at].reshape(rows, BLOCK)[:, :1]
        m = jnp.maximum(jnp.maximum(la, lb), jnp.max(s, axis=1, keepdims=True))
        p = jnp.where(ok > 0.0, jnp.exp2(s - m), 0.0)
        wa = jnp.exp2(la - m)
        wb = jnp.exp2(lb - m)
        total = wa + wb + jnp.sum(p, axis=1, keepdims=True)
        mixed = jnp.dot(p.astype(jnp.bfloat16), fresh, preferred_element_type=jnp.float32)
        mixed = mixed + wa * oa[at].reshape(rows, LAT).astype(jnp.float32)
        mixed = mixed + wb * ob[at].reshape(rows, LAT).astype(jnp.float32)
        out_ref[at] = (mixed / total).astype(jnp.bfloat16).reshape(TILE, heads, LAT)
        return carry

    lax.fori_loop(0, TOK // TILE, tile, 0)


def finish(q_own, r_own, fresh, fresh_rope, ok, oa, ob, sa, sb):
    vmem = pl.BlockSpec(memory_space=pltpu.VMEM)
    return pl.pallas_call(
        finish_kernel,
        out_shape=jax.ShapeDtypeStruct(q_own.shape, jnp.bfloat16),
        in_specs=[vmem] * 9,
        out_specs=vmem,
        compiler_params=pltpu.CompilerParams(vmem_limit_bytes=32 * 2**20),
        name="finish",
    )(q_own, r_own, fresh, fresh_rope, ok, oa, ob, sa, sb)

MESH = pl.DeviceIdType.MESH
SENDS = 2 * N_DP
CHUNK = 32


def shifted(dy, dx, dz, sign):
    dp, zh = lax.axis_index("dp"), lax.axis_index("zh")
    y, x, z = lax.div(dp, 8), lax.rem(lax.div(dp, 2), 4), zh * 2 + lax.rem(dp, 2)
    y = lax.rem(y + 4 + sign * dy, 4)
    x = lax.rem(x + 4 + sign * dx, 4)
    z = lax.rem(z + 4 + sign * dz, 4)
    return y * 8 + x * 2 + lax.rem(z, 2), lax.div(z, 2)


def row_place(i, sign):
    j = lax.rem(i * 37, SENDS)
    sign = sign * (1 - 2 * lax.axis_index("core"))
    return shifted(lax.div(j, 16), lax.rem(lax.div(j, 4), 4), lax.rem(j, 4), sign)


def block_place(i, sign):
    j = lax.rem(i * 15, N_DP)
    sign = sign * (1 - 2 * lax.axis_index("core"))
    return shifted(lax.div(j, 8), lax.rem(j, 4), lax.rem(lax.div(j, 4), 2), sign)


def feed_kernel(
    picks, hidden, latents, ropes, send, q, r, wg_hbm, wu_hbm, wd_hbm,
    own_kv, sib_kv, q_par, r_par, out,
    rows, wg, wu, wd, arr, arr_sib, stage, acts, part, part_sib, part_in,
    w_sem, row_send, row_recv, fwd_send, fwd_recv, part_send, part_recv,
    kv_send, kv_recv, kvf_send, kvf_recv, misc_send, misc_recv,
):
    dp, zh, core = lax.axis_index("dp"), lax.axis_index("zh"), lax.axis_index("core")
    sibling = (dp, zh, 1 - core)
    partner = (dp, 1 - zh, core)
    loads = [
        pltpu.make_async_copy(a, b, w_sem.at[i])
        for i, (a, b) in enumerate(((wg_hbm, wg), (wu_hbm, wu), (wd_hbm, wd)))
    ]
    for load in loads:
        load.start()

    barrier = pltpu.get_barrier_semaphore()

    def greet(i, carry):
        to, to_zh = row_place(i, 1)
        pl.semaphore_signal(barrier, inc=1, device_id=(to, to_zh, core), device_id_type=MESH)
        return carry

    lax.fori_loop(1, SENDS, greet, 0)
    pl.semaphore_signal(barrier, inc=1, device_id=sibling, device_id_type=MESH)

    def pick(n, carry):
        cut = pl.ds(pl.multiple_of(n * 512, 512), 512)
        value = jnp.dot(picks[...], hidden[:, cut], preferred_element_type=jnp.float32)
        rows[:, :, cut] = value.astype(jnp.bfloat16).reshape(rows.shape[0], rows.shape[1], 512)
        return carry

    lax.fori_loop(0, hidden.shape[1] // 512, pick, 0)
    pl.semaphore_wait(barrier, SENDS)

    def remote(src, dst, send_sem, recv_sem, device):
        return pltpu.make_async_remote_copy(
            src_ref=src, dst_ref=dst, send_sem=send_sem, recv_sem=recv_sem,
            device_id=device, device_id_type=MESH,
        )

    def row_copy(i):
        to, to_zh = row_place(i, 1)
        return remote(rows.at[to], arr.at[i], row_send.at[i], row_recv.at[i], (to, to_zh, core))

    def fwd_copy(i):
        return remote(arr.at[i], arr_sib.at[i], fwd_send.at[i], fwd_recv.at[i], sibling)

    def part_copy(c):
        at = pl.ds(c * CHUNK, CHUNK)
        return remote(
            part_sib.at[at], part_in.at[at], part_send.at[c], part_recv.at[c], sibling
        )

    def kv_copy(i):
        to, to_zh = block_place(i, 1)
        return remote(
            stage.at[i], own_kv.at[dp], kv_send.at[i], kv_recv.at[i], (to, to_zh, core)
        )

    def kvf_copy(i):
        source, _ = block_place(i, -1)
        return remote(
            own_kv.at[source], sib_kv.at[source], kvf_send.at[i], kvf_recv.at[i], sibling
        )

    def start_rows(i, carry):
        row_copy(i).start()
        return carry

    lax.fori_loop(1, SENDS, start_rows, 0)
    arr[0] = rows[dp]

    q_copy = remote(q, q_par, misc_send.at[0], misc_recv.at[0], partner)
    r_copy = remote(r, r_par, misc_send.at[1], misc_recv.at[1], partner)
    q_copy.start()
    r_copy.start()

    def load_block(i, to):
        index = send[0, to]
        stage[i, :BLOCK] = latents[index]
        rope = ropes[index]
        for k in range(LAT // BLOCK):
            stage[i, BLOCK:, k * BLOCK : (k + 1) * BLOCK] = rope[16 * k : 16 * (k + 1)]

    def start_blocks(i, carry):
        to, _ = block_place(i, 1)
        load_block(i, to)
        kv_copy(i).start()
        return carry

    lax.fori_loop(1, N_DP, start_blocks, 0)
    load_block(0, dp)
    mine = pltpu.make_async_copy(stage.at[0], own_kv.at[dp], kv_send.at[0])
    mine.start()
    mine_fwd = remote(stage.at[0], sib_kv.at[dp], kvf_send.at[0], kvf_recv.at[0], sibling)
    mine_fwd.start()
    for load in loads:
        load.wait()

    def experts(source, target, c):
        at = pl.ds(c * CHUNK, CHUNK)
        x = source[at].reshape(CHUNK * source.shape[1], source.shape[2])
        for n in range(2):
            cut = slice(n * 256, (n + 1) * 256)
            gate = jnp.dot(x, wg[:, cut], preferred_element_type=jnp.float32)
            lifted = jnp.dot(x, wu[:, cut], preferred_element_type=jnp.float32)
            acts[:, cut] = (gate / (1.0 + jnp.exp(-gate)) * lifted).astype(jnp.bfloat16)

        def down(n, carry):
            cut = pl.ds(pl.multiple_of(n * 512, 512), 512)
            value = jnp.dot(acts[...], wd[:, cut], preferred_element_type=jnp.float32)
            target[at, :, cut] = value.astype(jnp.bfloat16).reshape(CHUNK, source.shape[1], 512)
            return carry

        lax.fori_loop(0, source.shape[2] // 512, down, 0)

    def chunk(c, carry):
        first = c * CHUNK

        def pass_on(i, carry):
            @pl.when(i > 0)
            def _():
                row_copy(i).wait_recv()

            fwd_copy(i).start()
            return carry

        lax.fori_loop(first, first + CHUNK, pass_on, 0)
        experts(arr, part, c)

        def await_sib(i, carry):
            fwd_copy(i).wait_recv()
            return carry

        lax.fori_loop(first, first + CHUNK, await_sib, 0)
        experts(arr_sib, part_sib, c)
        part_copy(c).start()
        return carry

    lax.fori_loop(0, SENDS // CHUNK, chunk, 0)

    def pass_block(i, carry):
        kv_copy(i).wait_recv()
        kvf_copy(i).start()
        return carry

    lax.fori_loop(1, N_DP, pass_block, 0)

    def add_up(i, carry):
        source, source_zh = row_place(i, -1)
        total = part[i].astype(jnp.float32) + part_in[i].astype(jnp.float32)
        out[source * 2 + source_zh] = total.astype(jnp.bfloat16)
        return carry

    def add_chunk(c, carry):
        part_copy(c).wait()
        lax.fori_loop(c * CHUNK, (c + 1) * CHUNK, add_up, 0)
        return carry

    lax.fori_loop(0, SENDS // CHUNK, add_chunk, 0)

    def end_rows(i, carry):
        row_copy(i).wait_send()
        return carry

    lax.fori_loop(1, SENDS, end_rows, 0)

    def end_fwd(i, carry):
        fwd_copy(i).wait_send()
        return carry

    lax.fori_loop(0, SENDS, end_fwd, 0)

    def end_blocks(i, carry):
        kv_copy(i).wait_send()
        kvf_copy(i).wait()
        return carry

    lax.fori_loop(1, N_DP, end_blocks, 0)
    mine.wait()
    mine_fwd.wait()
    q_copy.wait()
    r_copy.wait()


def feed(picks, hidden, latents, ropes, send, q, r, wg, wu, wd):
    smem = pl.BlockSpec(memory_space=pltpu.SMEM)
    vmem = pl.BlockSpec(memory_space=pltpu.VMEM)
    hbm = pl.BlockSpec(memory_space=pl.ANY)
    bf16 = jnp.bfloat16
    packed = BLOCK + ropes.shape[1] * BLOCK // LAT
    blocks = jax.ShapeDtypeStruct((N_DP, packed, LAT), bf16)
    capacity = picks.shape[0] // N_DP
    width = hidden.shape[1]
    chips = (SENDS, capacity, width)
    dma = pltpu.SemaphoreType.DMA
    chunks = SENDS // CHUNK
    return pl.pallas_call(
        feed_kernel,
        out_shape=(
            blocks,
            blocks,
            jax.ShapeDtypeStruct(q.shape, bf16),
            jax.ShapeDtypeStruct(r.shape, bf16),
            jax.ShapeDtypeStruct(chips, bf16),
        ),
        in_specs=[vmem] * 4 + [smem] + [hbm] * 5,
        out_specs=(hbm, hbm, hbm, hbm, vmem),
        scratch_shapes=[
            pltpu.VMEM((N_DP, capacity, width), bf16),
            pltpu.VMEM(wg.shape, bf16),
            pltpu.VMEM(wu.shape, bf16),
            pltpu.VMEM(wd.shape, bf16),
            pltpu.VMEM(chips, bf16),
            pltpu.VMEM(chips, bf16),
            pltpu.VMEM(blocks.shape, bf16),
            pltpu.VMEM((CHUNK * capacity, wg.shape[1]), bf16),
            pltpu.VMEM(chips, bf16),
            pltpu.VMEM(chips, bf16),
            pltpu.VMEM(chips, bf16),
            dma((3,)),
            dma((SENDS,)), dma((SENDS,)), dma((SENDS,)), dma((SENDS,)),
            dma((chunks,)), dma((chunks,)),
            dma((N_DP,)), dma((N_DP,)), dma((N_DP,)), dma((N_DP,)),
            dma((2,)), dma((2,)),
        ],
        compiler_params=pltpu.CompilerParams(
            collective_id=1, has_side_effects=True, vmem_limit_bytes=56 * 2**20
        ),
        cost_estimate=pl.CostEstimate(
            flops=11 * 10**9, bytes_accessed=24 * 2**20, transcendentals=2**19
        ),
        name="feed",
    )(picks, hidden, latents, ropes, send, q, r, wg, wu, wd)


def swap(value, axis):
    return lax.ppermute(value, axis, [(0, 1), (1, 0)])


def shards(
    hidden_in,
    expert_ids,
    gate_vals,
    w_gate,
    w_up,
    w_down,
    w_latent,
    w_rope,
    latent_gain,
    cache_latent,
    cache_rope,
    send_index,
    block_table,
    cached_len,
    new_counts,
    q_latent,
    q_rope,
):
    zh, core = lax.axis_index("zh"), lax.axis_index("core")
    rows, width = hidden_in.shape
    fan_count = expert_ids.shape[1]
    capacity = rows // 2
    slots = N_DP * capacity

    experts = jnp.arange(N_DP, dtype=jnp.int32)
    named = expert_ids.T[:, None, :] == experts[None, :, None]
    hits = jnp.any(named, axis=0)
    before = jnp.cumsum(hits.astype(jnp.int32), axis=1) - hits
    picked = hits[:, None, :] & (
        before[:, None, :] == jnp.arange(capacity, dtype=jnp.int32)[None, :, None]
    )
    picks = picked.astype(jnp.bfloat16).reshape(slots, rows)
    gates = jnp.sum(jnp.where(named, gate_vals.T[:, None, :], 0.0), axis=0)
    weights = jnp.where(picked, gates[:, None, :], 0.0).reshape(slots, rows)

    own_kv, sib_kv, q_par, r_par, partial = feed(
        picks,
        hidden_in,
        cache_latent,
        cache_rope,
        send_index,
        q_latent,
        q_rope,
        w_gate[0],
        w_up[0],
        w_down[0],
    )
    r_own = q_rope.reshape(TOK, HEADS_DEV, ROPE)
    r_par = r_par.reshape(TOK, HEADS_DEV, ROPE)
    returned = lax.all_to_all(
        partial,
        ("dp", "zh"),
        split_axis=0,
        concat_axis=0,
        tiled=True,
    )
    summed = jnp.sum(
        returned.reshape(N_DP, 2, capacity, width), axis=1, dtype=jnp.float32
    ).reshape(slots, width)
    mixed = lax.dot_general(
        weights,
        summed,
        (((0,), (0,)), ((), ())),
        precision=lax.Precision.HIGHEST,
        preferred_element_type=jnp.float32,
    )
    hidden_out = (hidden_in.astype(jnp.float32) + mixed).astype(jnp.bfloat16)
    latent = jnp.dot(hidden_out, w_latent, preferred_element_type=jnp.float32)
    norm_scale = lax.rsqrt(jnp.mean(latent * latent, axis=1, keepdims=True) + NORM_EPS)
    new_latent = (latent * norm_scale * latent_gain[None, :]).astype(jnp.bfloat16)
    counts = new_counts[0]
    pool = zh * 2 + core
    local = pool * rows + jnp.arange(rows, dtype=jnp.int32)
    positions = chat_positions(counts, cached_len[0], local)
    new_rope = rotate(
        jnp.dot(hidden_out, w_rope, preferred_element_type=jnp.float32), positions
    ).astype(jnp.bfloat16)

    fresh = jnp.concatenate([new_latent, new_rope], axis=1)
    pair = jnp.stack([fresh, swap(fresh, "core")])
    pair = jnp.where(core == 0, pair, pair[::-1])
    quad = jnp.stack([pair, swap(pair, "zh")])
    quad = jnp.where(zh == 0, quad, quad[::-1]).reshape(TOK, LAT + ROPE)

    where = jnp.stack([zh, core, lax.axis_index("dp") % 2]).astype(jnp.int32)
    facts = (block_table.reshape(1, CHATS * MAXB), cached_len, new_counts, where, own_kv, sib_kv)
    o_par, s_par = attend(*facts, q_par, r_par, q_latent, "attend_partner")
    o_back = swap(o_par, "zh")
    s_back = swap(s_par[:, :, 0], "zh")
    o_own, s_own = attend(*facts, q_latent, r_own, o_par, "attend_own")
    s_back = jnp.broadcast_to(s_back[:, :, None], s_own.shape)
    tokens = jnp.arange(TOK, dtype=jnp.int32)
    ends = jnp.cumsum(counts)
    chat_of = jnp.sum((tokens[:, None] >= ends[None, :]).astype(jnp.int32), axis=1)
    ok = (chat_of[:, None] == chat_of[None, :]) & (tokens[None, :] <= tokens[:, None])
    context = finish(
        q_latent,
        r_own,
        quad[:, :LAT],
        quad[:, LAT:],
        ok.astype(jnp.float32),
        o_own,
        o_back,
        s_own,
        s_back,
    )
    return (hidden_out, new_latent, new_rope, context)


def solution(mesh):
    whole = Mesh(mesh.devices.reshape(N_DP, 2, 2), ("dp", "zh", "core"))
    every = ("dp", "zh", "core")
    pool = ("zh", "core")
    return jax.shard_map(
        shards,
        mesh=whole,
        in_specs=(
            P(every, None),
            P(every, None),
            P(every, None),
            P("dp", None, pool),
            P("dp", None, pool),
            P("dp", pool, None),
            P(),
            P(),
            P(),
            P(every, None, None),
            P(every, None, None),
            P(every, None),
            P("dp", None, None),
            P("dp", None),
            P("dp", None),
            P("dp", pool, None),
            P("dp", pool),
        ),
        out_specs=(
            P(every, None),
            P(every, None),
            P(every, None),
            P("dp", pool, None),
        ),
        check_vma=False,
    )
```

```python
import functools

import jax
import jax.numpy as jnp
from jax import lax
from jax.experimental import pallas as pl
from jax.experimental.pallas import tpu as pltpu
from jax.sharding import Mesh
from jax.sharding import PartitionSpec as P

SCORE_SCALE = 192.0 ** (-0.5)
LOG2E = 1.4426950408889634
ROPE_BASE = 10000.0
NORM_EPS = 1e-06
BIG = -1e30

N_DP = 32
CHATS = 4
MAXB = 32
BLOCK = 128
LAT = 512
ROPE = 64
TOK = 64
HEADS_DEV = 16
GROUP = 4
TILE = 16
SLOTS = 2 * N_DP + CHATS * (GROUP - 1) + 2


def chat_positions(counts, lengths, local):
    ends = jnp.cumsum(counts)
    chat_of = jnp.sum((local[:, None] >= ends[None, :]).astype(jnp.int32), axis=1)
    starts = ends - counts
    onehot = (chat_of[:, None] == jnp.arange(counts.shape[0])[None, :]).astype(jnp.int32)
    return jnp.sum(onehot * (lengths - starts)[None, :], axis=1) + local


def attend_kernel(
    table, lengths, counts, where, kv, q_ref, r_ref, after,
    o_ref, s_ref, held, place, sems, scores,
):
    zh, core, low = where[0], where[1], where[2]
    heads = q_ref.shape[1]
    rows = TILE * heads

    def copy_in(source, slot):
        return pltpu.make_async_copy(kv.at[source], held.at[slot], sems.at[slot])

    def fetch(holder, slot):
        source = lax.shift_right_logical(holder, 2) + ((holder & 1) ^ core) * N_DP
        copy_in(source, slot).start()

    def list_blocks(chat, begin):
        length = lengths[0, chat]

        def step(j, carry):
            slot, last = carry
            holder = table[0, chat * MAXB + j]
            z = (lax.shift_right_logical(holder, 1) & 1) * 2 + (
                lax.shift_right_logical(holder, 2) & 1
            )
            step_z = jnp.where((z & 1) == low, 0, 1 + 2 * (holder & 1))
            mine = lax.shift_right_logical((z + step_z) & 3, 1) == zh

            @pl.when(mine)
            def _():
                place[slot] = jnp.clip(length - j * BLOCK, 0, BLOCK)
                fetch(holder, slot)

            return jnp.where(mine, slot + 1, slot), jnp.where(mine, holder, last)

        count = lax.shift_right_logical(length + BLOCK - 1, 7)
        slot, last = lax.fori_loop(0, count, step, (begin, jnp.int32(0)))
        pad = lax.rem(GROUP - lax.rem(slot, GROUP), GROUP)

        def fill(i, carry):
            place[carry] = 0
            fetch(last, carry)
            return carry + 1

        return lax.fori_loop(0, pad, fill, slot)

    def arrive(i, carry):
        copy_in(0, i).wait()
        return carry

    begins = [jnp.int32(0)]
    begins.append(list_blocks(0, begins[0]))
    start = jnp.int32(0)
    lane = lax.broadcasted_iota(jnp.int32, (1, BLOCK), 1)
    contract = (((1,), (1,)), ((), ()))
    for chat in range(CHATS):
        if chat + 1 < CHATS:
            begins.append(list_blocks(chat + 1, begins[chat + 1]))
        count = counts[0, chat]
        first_group = lax.div(begins[chat], GROUP)
        n_groups = lax.div(begins[chat + 1] - begins[chat], GROUP)
        lax.fori_loop(begins[chat], begins[chat + 1], arrive, 0)

        def tile(t, carry):
            base = jnp.minimum(start + t * TILE, TOK - TILE)
            ql = q_ref[pl.ds(base, TILE)].reshape(rows, LAT)
            qr = r_ref[pl.ds(base, TILE)].reshape(rows, ROPE)

            def keys_of(g):
                at = (first_group + g) * GROUP
                blocks = [held[at + i] for i in range(GROUP)]
                return blocks, jnp.concatenate([b[:BLOCK] for b in blocks], axis=0)

            def score(g, best):
                blocks, keys = keys_of(g)
                ropes = jnp.concatenate(
                    [
                        jnp.concatenate(
                            [b[BLOCK:, k * BLOCK : (k + 1) * BLOCK] for k in range(LAT // BLOCK)],
                            axis=0,
                        )
                        for b in blocks
                    ],
                    axis=1,
                )
                at = (first_group + g) * GROUP
                valid = jnp.concatenate([lane < place[at + i] for i in range(GROUP)], axis=1)
                s = lax.dot_general(ql, keys, contract, preferred_element_type=jnp.float32)
                s = s + jnp.dot(qr, ropes, preferred_element_type=jnp.float32)
                s = jnp.where(valid, s * (SCORE_SCALE * LOG2E), BIG)
                scores[g] = s
                for i in range(GROUP):
                    best = jnp.maximum(best, s[:, i * BLOCK : (i + 1) * BLOCK])
                return best

            def blend(g, state, top):
                total, acc = state
                _, keys = keys_of(g)
                p = jnp.exp2(scores[g] - top)
                for i in range(GROUP):
                    total = total + p[:, i * BLOCK : (i + 1) * BLOCK]
                acc = acc + jnp.dot(p.astype(jnp.bfloat16), keys, preferred_element_type=jnp.float32)
                return total, acc

            def over(step, state):
                def two(g, state):
                    return step(2 * g + 1, step(2 * g, state))

                state = lax.fori_loop(0, lax.div(n_groups, 2), two, state)
                return lax.fori_loop(n_groups - lax.rem(n_groups, 2), n_groups, step, state)

            best = over(score, jnp.full((rows, BLOCK), BIG, jnp.float32))
            top = jnp.max(best, axis=1, keepdims=True)
            total, acc = over(
                lambda g, state: blend(g, state, top),
                (jnp.zeros((rows, BLOCK), jnp.float32), jnp.zeros((rows, LAT), jnp.float32)),
            )
            total = jnp.sum(total, axis=1, keepdims=True)
            token = base + lax.broadcasted_iota(jnp.int32, (TILE, 1, 1), 0)
            keep = (token >= start) & (token < start + count)
            some = total > 0.0
            safe = jnp.where(some, total, 1.0)
            value = (acc / safe).astype(jnp.bfloat16).reshape(TILE, heads, LAT)
            lse = jnp.where(some, top + jnp.log2(safe), BIG)
            lse = jnp.broadcast_to(lse, (rows, BLOCK)).reshape(TILE, heads, BLOCK)
            at = pl.ds(base, TILE)
            o_ref[at] = jnp.where(keep, value, o_ref[at])
            s_ref[at] = jnp.where(keep, lse, s_ref[at])
            return carry

        lax.fori_loop(0, lax.div(count + TILE - 1, TILE), tile, 0)
        start = start + count


def attend(table, lengths, counts, where, kv, q, r, after, name):
    smem = pl.BlockSpec(memory_space=pltpu.SMEM)
    vmem = pl.BlockSpec(memory_space=pltpu.VMEM)
    hbm = pl.BlockSpec(memory_space=pl.ANY)
    tok, heads, width = q.shape
    return pl.pallas_call(
        attend_kernel,
        out_shape=(
            jax.ShapeDtypeStruct((tok, heads, width), jnp.bfloat16),
            jax.ShapeDtypeStruct((tok, heads, BLOCK), jnp.float32),
        ),
        in_specs=[smem] * 4 + [hbm] + [vmem] * 2 + [hbm],
        out_specs=(vmem,) * 2,
        scratch_shapes=[
            pltpu.VMEM((SLOTS,) + kv.shape[1:], jnp.bfloat16),
            pltpu.SMEM((SLOTS,), jnp.int32),
            pltpu.SemaphoreType.DMA((SLOTS,)),
            pltpu.VMEM((MAXB // GROUP, TILE * heads, GROUP * BLOCK), jnp.float32),
        ],
        compiler_params=pltpu.CompilerParams(vmem_limit_bytes=48 * 2**20),
        cost_estimate=pl.CostEstimate(
            flops=5 * 10**9, bytes_accessed=40 * 2**20, transcendentals=2 * 2**20
        ),
        name=name,
    )(table, lengths, counts, where, kv, q, r, after)


MESH = pl.DeviceIdType.MESH
AXES = ("plane", "zl", "zh", "core")
SENDS = 2 * N_DP
CHUNK = 32
ROW_ORDER = (
    0, 42, 46, 21, 11, 33, 58, 31, 49, 59, 45, 13, 47, 10, 32, 6,
    27, 34, 8, 35, 9, 51, 39, 5, 55, 52, 18, 56, 50, 24, 37, 3,
    40, 2, 44, 14, 36, 15, 53, 61, 28, 30, 63, 23, 43, 22, 48, 7,
    41, 54, 29, 20, 1, 60, 62, 57, 17, 12, 19, 4, 16, 26, 38, 25,
)
BLOCK_ORDER = (
    0, 22, 18, 29, 25, 15, 11, 4, 27, 13, 31, 14, 28, 26, 21, 3,
    19, 1, 12, 9, 5, 23, 10, 24, 7, 8, 6, 16, 2, 20, 30, 17,
)


def place_of():
    return tuple(lax.axis_index(name) for name in AXES)


def shifted(dy, dx, dz, sign):
    plane, zl, zh, _ = place_of()
    y = lax.rem(lax.div(plane, 4) + 4 + sign * dy, 4)
    x = lax.rem(lax.rem(plane, 4) + 4 + sign * dx, 4)
    z = lax.rem(zh * 2 + zl + 4 + sign * dz, 4)
    return y * 4 + x, lax.rem(z, 2), lax.div(z, 2)


def row_place_of(j):
    return shifted(lax.div(j, 16), lax.rem(lax.div(j, 4), 4), lax.rem(j, 4), 1)


def row_place(j, sign):
    sign = sign * (1 - 2 * lax.axis_index("core"))
    return shifted(j // 16, j // 4 % 4, j % 4, sign)


def block_place(j, sign):
    sign = sign * (1 - 2 * lax.axis_index("core"))
    return shifted(j // 8, j % 4, j // 4 % 2, sign)


def feed_kernel(
    picks, hidden, latents, ropes, send, q, r, wg_hbm, wu_hbm, wd_hbm, mine_w,
    kv, q_par, r_par, out, near_w,
    rows, wg, wu, wd, arr, arr_sib, stage, acts, part, part_sib, part_in,
    w_sem, row_send, row_recv, fwd_send, fwd_recv, part_send, part_recv,
    kv_send, kv_recv, kvf_send, kvf_recv, misc_send, misc_recv,
):
    plane, zl, zh, core = place_of()
    dp, z = plane * 2 + zl, zh * 2 + zl
    sibling = (plane, zl, zh, 1 - core)
    partner = (plane, zl, 1 - zh, core)
    loads = [
        pltpu.make_async_copy(a, b, w_sem.at[i])
        for i, (a, b) in enumerate(((wg_hbm, wg), (wu_hbm, wu), (wd_hbm, wd)))
    ]
    for load in loads:
        load.start()

    barrier = pltpu.get_barrier_semaphore()

    def greet(i, carry):
        to = row_place_of(i)
        pl.semaphore_signal(barrier, inc=1, device_id=(*to, core), device_id_type=MESH)
        return carry

    lax.fori_loop(1, SENDS, greet, 0)
    pl.semaphore_signal(barrier, inc=1, device_id=sibling, device_id_type=MESH)

    def pick(n, carry):
        cut = pl.ds(pl.multiple_of(n * 512, 512), 512)
        value = lax.dot_general(
            picks[...],
            hidden[:, cut],
            (((0,), (0,)), ((), ())),
            preferred_element_type=jnp.float32,
        )
        rows[:, :, cut] = value.astype(jnp.bfloat16).reshape(rows.shape[0], rows.shape[1], 512)
        return carry

    lax.fori_loop(0, hidden.shape[1] // 512, pick, 0)
    pl.semaphore_wait(barrier, SENDS)

    def remote(src, dst, send_sem, recv_sem, device):
        return pltpu.make_async_remote_copy(
            src_ref=src, dst_ref=dst, send_sem=send_sem, recv_sem=recv_sem,
            device_id=device, device_id_type=MESH,
        )

    def row_copy(i, to=(0, 0, 0)):
        source = rows.at[to[1] * (N_DP // 2) + to[0]]
        return remote(source, arr.at[i], row_send.at[i], row_recv.at[i], (*to, core))

    def fwd_copy(i):
        return remote(arr.at[i], arr_sib.at[i], fwd_send.at[i], fwd_recv.at[i], sibling)

    def part_copy(c):
        at = pl.ds(c * CHUNK, CHUNK)
        return remote(
            part_sib.at[at], part_in.at[at], part_send.at[c], part_recv.at[c], sibling
        )

    def kv_copy(i, to=(0, 0, 0)):
        return remote(
            stage.at[i], kv.at[dp], kv_send.at[i], kv_recv.at[i], (*to, core)
        )

    def kvf_copy(i, source=0):
        return remote(
            kv.at[source], kv.at[N_DP + source], kvf_send.at[i], kvf_recv.at[i], sibling
        )

    for i in range(1, SENDS):
        row_copy(i, row_place(ROW_ORDER[i], 1)).start()
    arr[0] = rows[zl * (N_DP // 2) + plane]

    q_copy = remote(q, q_par, misc_send.at[0], misc_recv.at[0], partner)
    r_copy = remote(r, r_par, misc_send.at[1], misc_recv.at[1], partner)
    q_copy.start()
    r_copy.start()

    def weight_copy(dz):
        to = shifted(0, 0, dz, 1)
        return remote(
            mine_w.at[to[1]], near_w.at[z], misc_send.at[1 + dz], misc_recv.at[1 + dz], (*to, core)
        )

    for dz in (1, 2, 3):
        weight_copy(dz).start()
    near_w[z] = mine_w[zl]

    def load_block(i, to):
        index = send[0, to]
        stage[i, :BLOCK] = latents[index]
        rope = ropes[index]
        for k in range(LAT // BLOCK):
            stage[i, BLOCK:, k * BLOCK : (k + 1) * BLOCK] = rope[16 * k : 16 * (k + 1)]

    for i in range(1, N_DP):
        to = block_place(BLOCK_ORDER[i], 1)
        load_block(i, to[0] * 2 + to[1])
        kv_copy(i, to).start()
    load_block(0, dp)
    mine = pltpu.make_async_copy(stage.at[0], kv.at[dp], kv_send.at[0])
    mine.start()
    mine_fwd = remote(stage.at[0], kv.at[N_DP + dp], kvf_send.at[0], kvf_recv.at[0], sibling)
    mine_fwd.start()
    for load in loads:
        load.wait()

    def experts(source, target, c):
        at = pl.ds(c * CHUNK, CHUNK)
        x = source[at].reshape(CHUNK * source.shape[1], source.shape[2])
        for n in range(2):
            cut = slice(n * 256, (n + 1) * 256)
            gate = jnp.dot(x, wg[:, cut], preferred_element_type=jnp.float32)
            lifted = jnp.dot(x, wu[:, cut], preferred_element_type=jnp.float32)
            acts[:, cut] = (gate / (1.0 + jnp.exp(-gate)) * lifted).astype(jnp.bfloat16)

        def down(n, carry):
            cut = pl.ds(pl.multiple_of(n * 512, 512), 512)
            value = jnp.dot(acts[...], wd[:, cut], preferred_element_type=jnp.float32)
            target[at, :, cut] = value.astype(jnp.bfloat16).reshape(CHUNK, source.shape[1], 512)
            return carry

        lax.fori_loop(0, source.shape[2] // 512, down, 0)

    def chunk(c, carry):
        first = c * CHUNK

        def pass_on(i, carry):
            @pl.when(i > 0)
            def _():
                row_copy(i).wait_recv()

            fwd_copy(i).start()
            return carry

        lax.fori_loop(first, first + CHUNK, pass_on, 0)
        experts(arr, part, c)

        def await_sib(i, carry):
            fwd_copy(i).wait_recv()
            return carry

        lax.fori_loop(first, first + CHUNK, await_sib, 0)
        experts(arr_sib, part_sib, c)
        part_copy(c).start()
        return carry

    lax.fori_loop(0, SENDS // CHUNK, chunk, 0)

    for i in range(1, N_DP):
        kv_copy(i).wait_recv()
        source = block_place(BLOCK_ORDER[i], -1)
        kvf_copy(i, source[0] * 2 + source[1]).start()

    for i in range(SENDS):
        if i % CHUNK == 0:
            part_copy(i // CHUNK).wait()
        source = row_place(ROW_ORDER[i], -1)
        total = part[i].astype(jnp.float32) + part_in[i].astype(jnp.float32)
        out[source[0] * 4 + source[2] * 2 + source[1]] = total.astype(jnp.bfloat16)

    def end_rows(i, carry):
        row_copy(i).wait_send()
        return carry

    lax.fori_loop(1, SENDS, end_rows, 0)

    def end_fwd(i, carry):
        fwd_copy(i).wait_send()
        return carry

    lax.fori_loop(0, SENDS, end_fwd, 0)

    def end_blocks(i, carry):
        kv_copy(i).wait_send()
        kvf_copy(i).wait()
        return carry

    lax.fori_loop(1, N_DP, end_blocks, 0)
    mine.wait()
    mine_fwd.wait()
    q_copy.wait()
    r_copy.wait()
    for dz in (1, 2, 3):
        weight_copy(dz).wait()


def feed(picks, hidden, latents, ropes, send, q, r, wg, wu, wd, weights):
    smem = pl.BlockSpec(memory_space=pltpu.SMEM)
    vmem = pl.BlockSpec(memory_space=pltpu.VMEM)
    hbm = pl.BlockSpec(memory_space=pl.ANY)
    bf16 = jnp.bfloat16
    packed = BLOCK + ropes.shape[1] * BLOCK // LAT
    blocks = jax.ShapeDtypeStruct((2 * N_DP, packed, LAT), bf16)
    capacity = picks.shape[1] // N_DP
    width = hidden.shape[1]
    chips = (SENDS, capacity, width)
    dma = pltpu.SemaphoreType.DMA
    chunks = SENDS // CHUNK
    return pl.pallas_call(
        feed_kernel,
        out_shape=(
            blocks,
            jax.ShapeDtypeStruct(q.shape, bf16),
            jax.ShapeDtypeStruct(r.shape, bf16),
            jax.ShapeDtypeStruct(chips, bf16),
            jax.ShapeDtypeStruct((4,) + weights.shape[1:], bf16),
        ),
        in_specs=[vmem] * 4 + [smem] + [hbm] * 5 + [vmem],
        out_specs=(hbm, hbm, hbm, vmem, vmem),
        scratch_shapes=[
            pltpu.VMEM((N_DP, capacity, width), bf16),
            pltpu.VMEM(wg.shape, bf16),
            pltpu.VMEM(wu.shape, bf16),
            pltpu.VMEM(wd.shape, bf16),
            pltpu.VMEM(chips, bf16),
            pltpu.VMEM(chips, bf16),
            pltpu.VMEM((N_DP, packed, LAT), bf16),
            pltpu.VMEM((CHUNK * capacity, wg.shape[1]), bf16),
            pltpu.VMEM(chips, bf16),
            pltpu.VMEM(chips, bf16),
            pltpu.VMEM(chips, bf16),
            dma((3,)),
            dma((SENDS,)), dma((SENDS,)), dma((SENDS,)), dma((SENDS,)),
            dma((chunks,)), dma((chunks,)),
            dma((N_DP,)), dma((N_DP,)), dma((N_DP,)), dma((N_DP,)),
            dma((5,)), dma((5,)),
        ],
        compiler_params=pltpu.CompilerParams(
            collective_id=1, has_side_effects=True, vmem_limit_bytes=56 * 2**20
        ),
        cost_estimate=pl.CostEstimate(
            flops=11 * 10**9, bytes_accessed=24 * 2**20, transcendentals=2**19
        ),
        name="feed",
    )(picks, hidden, latents, ropes, send, q, r, wg, wu, wd, weights)


def close_kernel(
    returned_hbm, w_lat_hbm, q_hbm, r_hbm, oa_hbm, ob_hbm, sa_hbm, sb_hbm,
    near_w, hidden, w_rope_ref, w_turn_ref, gain, cosine, sine, ok_ref,
    hidden_out, new_latent, new_rope, out_ref,
    returned, w_lat, q_ref, r_ref, oa, ob, sa, sb,
    sums, sums_out, inbox, fresh, load_sem, sum_send, sum_recv, fresh_send, fresh_recv,
):
    plane, zl, zh, core = place_of()
    z = zh * 2 + zl
    pool = zh * 2 + core
    heads = q_ref.shape[1]
    rows, width = hidden.shape
    loads = [
        pltpu.make_async_copy(a, b, load_sem.at[i])
        for i, (a, b) in enumerate(
            (
                (returned_hbm, returned), (w_lat_hbm, w_lat), (q_hbm, q_ref), (r_hbm, r_ref),
                (oa_hbm, oa), (ob_hbm, ob), (sa_hbm, sa), (sb_hbm, sb),
            )
        )
    ]
    for load in loads:
        load.start()
    column = [(*shifted(0, 0, dz, 1), core) for dz in (1, 2, 3)]
    others = [(plane, zl, zh, 1 - core), (plane, zl, 1 - zh, core), (plane, zl, 1 - zh, 1 - core)]
    barrier = pltpu.get_barrier_semaphore()
    for device in column + [others[0], others[2]]:
        pl.semaphore_signal(barrier, inc=1, device_id=device, device_id_type=MESH)
    pl.semaphore_wait(barrier, 5)
    loads[0].wait()

    def add(at):
        weights = near_w[at]

        for n in range(width // 512):
            cut = slice(n * 512, (n + 1) * 512)
            x = returned[:, at, :, cut].reshape(weights.shape[1], 512)
            both = jnp.dot(weights, x, preferred_element_type=jnp.float32)
            total = both[:rows] + both[rows:]
            sums[at, :, cut] = total
            sums_out[at, :, cut] = total.astype(jnp.bfloat16)

    def sum_copy(dz):
        to = lax.rem(z + dz, 4)
        return pltpu.make_async_remote_copy(
            src_ref=sums_out.at[to], dst_ref=inbox.at[dz - 1],
            send_sem=sum_send.at[dz - 1], recv_sem=sum_recv.at[dz - 1],
            device_id=column[dz - 1], device_id_type=MESH,
        )

    for dz in (2, 1, 3):
        add(lax.rem(z + dz, 4))
        sum_copy(dz).start()
    add(z)
    for dz in (1, 2, 3):
        sum_copy(dz).wait()

    total = hidden[...].astype(jnp.float32) + sums[z]
    for i in range(3):
        total = total + inbox[i].astype(jnp.float32)
    x = total.astype(jnp.bfloat16)
    hidden_out[...] = x
    loads[1].wait()
    latent = jnp.dot(x, w_lat[...], preferred_element_type=jnp.float32)
    plain = jnp.dot(x, w_rope_ref[...], preferred_element_type=jnp.float32)
    turned = jnp.dot(x, w_turn_ref[...], preferred_element_type=jnp.float32)
    scale = lax.rsqrt(jnp.mean(latent * latent, axis=1, keepdims=True) + NORM_EPS)
    latent = (latent * scale * gain[...]).astype(jnp.bfloat16)
    rope = (plain * cosine[...] + turned * sine[...]).astype(jnp.bfloat16)
    new_latent[...] = latent
    new_rope[...] = rope
    blank = jnp.zeros((rows, BLOCK - ROPE), jnp.bfloat16)
    fresh[pool] = jnp.concatenate([latent, rope, blank], axis=1)

    def fresh_copy(i):
        return pltpu.make_async_remote_copy(
            src_ref=fresh.at[pool], dst_ref=fresh.at[pool],
            send_sem=fresh_send.at[i], recv_sem=fresh_recv.at[i],
            device_id=others[i], device_id_type=MESH,
        )

    for i in range(3):
        fresh_copy(i).start()
    for load in loads[2:]:
        load.wait()
    for i in range(3):
        fresh_copy(i).wait()

    contract = (((1,), (1,)), ((), ()))
    keys = fresh[...].reshape(TOK, LAT + BLOCK)
    lat_keys = keys[:, :LAT]
    rope_keys = keys[:, LAT : LAT + ROPE]

    def tile(t, carry):
        at = pl.ds(t * TILE, TILE)
        size = TILE * heads
        s = lax.dot_general(
            q_ref[at].reshape(size, LAT), lat_keys, contract, preferred_element_type=jnp.float32
        ) + lax.dot_general(
            r_ref[at].reshape(size, ROPE), rope_keys, contract, preferred_element_type=jnp.float32
        )
        ok = ok_ref[at]
        ok = jnp.broadcast_to(ok[:, None, :], (TILE, heads, TOK)).reshape(size, TOK)
        s = jnp.where(ok > 0.0, s * (SCORE_SCALE * LOG2E), BIG)
        la = sa[at].reshape(size, BLOCK)[:, :1]
        lb = sb[at].reshape(size, BLOCK)[:, :1]
        m = jnp.maximum(jnp.maximum(la, lb), jnp.max(s, axis=1, keepdims=True))
        p = jnp.where(ok > 0.0, jnp.exp2(s - m), 0.0)
        wa = jnp.exp2(la - m)
        wb = jnp.exp2(lb - m)
        weight = wa + wb + jnp.sum(p, axis=1, keepdims=True)
        mixed = jnp.dot(p.astype(jnp.bfloat16), lat_keys, preferred_element_type=jnp.float32)
        mixed = mixed + wa * oa[at].reshape(size, LAT).astype(jnp.float32)
        mixed = mixed + wb * ob[at].reshape(size, LAT).astype(jnp.float32)
        out_ref[at] = (mixed / weight).astype(jnp.bfloat16).reshape(TILE, heads, LAT)
        return carry

    lax.fori_loop(0, TOK // TILE, tile, 0)


def close(large, small):
    vmem = pl.BlockSpec(memory_space=pltpu.VMEM)
    hbm = pl.BlockSpec(memory_space=pl.ANY)
    q, hidden = large[2], small[1]
    rows, width = hidden.shape
    bf16 = jnp.bfloat16
    dma = pltpu.SemaphoreType.DMA
    return pl.pallas_call(
        close_kernel,
        out_shape=(
            jax.ShapeDtypeStruct(hidden.shape, bf16),
            jax.ShapeDtypeStruct((rows, LAT), bf16),
            jax.ShapeDtypeStruct((rows, ROPE), bf16),
            jax.ShapeDtypeStruct(q.shape, bf16),
        ),
        in_specs=[hbm] * len(large) + [vmem] * len(small),
        out_specs=(vmem,) * 4,
        scratch_shapes=[
            *(pltpu.VMEM(a.shape, a.dtype) for a in large),
            pltpu.VMEM((4, rows, width), jnp.float32),
            pltpu.VMEM((4, rows, width), bf16),
            pltpu.VMEM((3, rows, width), bf16),
            pltpu.VMEM((4, rows, LAT + BLOCK), bf16),
            dma((len(large),)),
            dma((3,)), dma((3,)),
            dma((3,)), dma((3,)),
        ],
        compiler_params=pltpu.CompilerParams(
            collective_id=2, has_side_effects=True, vmem_limit_bytes=48 * 2**20
        ),
        name="close",
    )(*large, *small)


def swap(value, axis):
    return lax.ppermute(value, axis, [(0, 1), (1, 0)])


def shards(
    hidden_in,
    expert_ids,
    gate_vals,
    w_gate,
    w_up,
    w_down,
    w_latent,
    w_rope,
    latent_gain,
    cache_latent,
    cache_rope,
    send_index,
    block_table,
    cached_len,
    new_counts,
    q_latent,
    q_rope,
):
    _, zl, zh, core = place_of()
    rows, width = hidden_in.shape
    capacity = rows // 2

    turn = jnp.arange(N_DP, dtype=jnp.int32)
    experts = turn % (N_DP // 2) * 2 + turn // (N_DP // 2)
    named = expert_ids[:, :, None] == experts[None, None, :]
    hits = jnp.any(named, axis=1)
    before = jnp.cumsum(hits.astype(jnp.int32), axis=0) - hits
    picked = hits[:, :, None] & (
        before[:, :, None] == jnp.arange(capacity, dtype=jnp.int32)[None, None, :]
    )
    picks = picked.astype(jnp.bfloat16).reshape(rows, N_DP * capacity)
    gates = jnp.sum(jnp.where(named, gate_vals[:, :, None], 0.0), axis=1)
    weights = jnp.where(picked, gates[:, :, None], 0.0).reshape(rows, 2, -1)
    high = weights.astype(jnp.bfloat16)
    low = (weights - high.astype(jnp.float32)).astype(jnp.bfloat16)
    split = jnp.concatenate([high, low], axis=0).transpose(1, 0, 2)

    kv, q_par, r_par, partial, near_w = feed(
        picks,
        hidden_in,
        cache_latent,
        cache_rope,
        send_index,
        q_latent,
        q_rope,
        w_gate[0],
        w_up[0],
        w_down[0],
        split,
    )
    r_own = q_rope.reshape(TOK, HEADS_DEV, ROPE)
    r_par = r_par.reshape(TOK, HEADS_DEV, ROPE)
    returned = lax.all_to_all(partial, "plane", split_axis=0, concat_axis=0, tiled=True)

    where = jnp.stack([zh, core, zl]).astype(jnp.int32)
    facts = (block_table.reshape(1, CHATS * MAXB), cached_len, new_counts, where, kv)
    o_par, s_par = attend(*facts, q_par, r_par, q_latent, "attend_partner")
    o_back = swap(o_par, "zh")
    s_back = swap(s_par[:, :, 0], "zh")
    o_own, s_own = attend(*facts, q_latent, r_own, o_par, "attend_own")
    s_back = jnp.broadcast_to(s_back[:, :, None], s_own.shape)
    counts = new_counts[0]
    local = (zh * 2 + core) * rows + jnp.arange(rows, dtype=jnp.int32)
    positions = chat_positions(counts, cached_len[0], local)
    half = ROPE // 2
    exponent = jnp.arange(half).astype(jnp.float32) * (-2.0 / ROPE)
    frequency = jnp.power(jnp.float32(ROPE_BASE), exponent)
    angle = positions.astype(jnp.float32)[:, None] * frequency[None, :]
    cosine = jnp.tile(jnp.cos(angle), (1, 2))
    sine = jnp.tile(jnp.sin(angle), (1, 2))
    w_turn = jnp.concatenate([-w_rope[:, half:], w_rope[:, :half]], axis=1)
    tokens = jnp.arange(TOK, dtype=jnp.int32)
    ends = jnp.cumsum(counts)
    chat_of = jnp.sum((tokens[:, None] >= ends[None, :]).astype(jnp.int32), axis=1)
    ok = (chat_of[:, None] == chat_of[None, :]) & (tokens[None, :] <= tokens[:, None])
    return close(
        (
            returned.reshape(N_DP // 2, 4, capacity, width),
            w_latent,
            q_latent,
            r_own,
            o_own,
            o_back,
            s_own,
            s_back,
        ),
        (
            near_w,
            hidden_in,
            w_rope,
            w_turn,
            latent_gain[None, :],
            cosine,
            sine,
            ok.astype(jnp.float32),
        ),
    )


def solution(mesh):
    whole = Mesh(mesh.devices.reshape(N_DP // 2, 2, 2, 2), AXES)
    every = AXES
    dp = ("plane", "zl")
    pool = ("zh", "core")
    return jax.shard_map(
        shards,
        mesh=whole,
        in_specs=(
            P(every, None),
            P(every, None),
            P(every, None),
            P(dp, None, pool),
            P(dp, None, pool),
            P(dp, pool, None),
            P(),
            P(),
            P(),
            P(every, None, None),
            P(every, None, None),
            P(every, None),
            P(dp, None, None),
            P(dp, None),
            P(dp, None),
            P(dp, pool, None),
            P(dp, pool),
        ),
        out_specs=(
            P(every, None),
            P(every, None),
            P(every, None),
            P(dp, pool, None),
        ),
        check_vma=False,
    )
```

```python
import functools

import jax
import jax.numpy as jnp
from jax import lax
from jax.experimental import pallas as pl
from jax.experimental.pallas import tpu as pltpu
from jax.sharding import Mesh
from jax.sharding import PartitionSpec as P

SCORE_SCALE = 192.0 ** (-0.5)
LOG2E = 1.4426950408889634
ROPE_BASE = 10000.0
NORM_EPS = 1e-06
BIG = -1e30

N_DP = 32
CHATS = 4
MAXB = 32
BLOCK = 128
LAT = 512
ROPE = 64
TOK = 64
HEADS_DEV = 16
GROUP = 4
TILE = 16
SLOTS = 2 * N_DP + CHATS * (GROUP - 1) + 2


def chat_positions(counts, lengths, local):
    ends = jnp.cumsum(counts)
    chat_of = jnp.sum((local[:, None] >= ends[None, :]).astype(jnp.int32), axis=1)
    starts = ends - counts
    onehot = (chat_of[:, None] == jnp.arange(counts.shape[0])[None, :]).astype(jnp.int32)
    return jnp.sum(onehot * (lengths - starts)[None, :], axis=1) + local


def attend_kernel(
    table, lengths, counts, where, kv, q_ref, r_ref, after,
    o_ref, s_ref, held, place, sems, scores,
):
    zh, core, low = where[0], where[1], where[2]
    heads = q_ref.shape[1]
    rows = TILE * heads

    def copy_in(source, slot):
        return pltpu.make_async_copy(kv.at[source], held.at[slot], sems.at[slot])

    def fetch(holder, slot):
        source = lax.shift_right_logical(holder, 2) + ((holder & 1) ^ core) * N_DP
        copy_in(source, slot).start()

    def list_blocks(chat, begin):
        length = lengths[0, chat]

        def step(j, carry):
            slot, last = carry
            holder = table[0, chat * MAXB + j]
            z = (lax.shift_right_logical(holder, 1) & 1) * 2 + (
                lax.shift_right_logical(holder, 2) & 1
            )
            step_z = jnp.where((z & 1) == low, 0, 1 + 2 * (holder & 1))
            mine = lax.shift_right_logical((z + step_z) & 3, 1) == zh

            @pl.when(mine)
            def _():
                place[slot] = jnp.clip(length - j * BLOCK, 0, BLOCK)
                fetch(holder, slot)

            return jnp.where(mine, slot + 1, slot), jnp.where(mine, holder, last)

        count = lax.shift_right_logical(length + BLOCK - 1, 7)
        slot, last = lax.fori_loop(0, count, step, (begin, jnp.int32(0)))
        pad = lax.rem(GROUP - lax.rem(slot, GROUP), GROUP)

        def fill(i, carry):
            place[carry] = 0
            fetch(last, carry)
            return carry + 1

        return lax.fori_loop(0, pad, fill, slot)

    def arrive(i, carry):
        copy_in(0, i).wait()
        return carry

    begins = [jnp.int32(0)]
    begins.append(list_blocks(0, begins[0]))
    start = jnp.int32(0)
    lane = lax.broadcasted_iota(jnp.int32, (1, BLOCK), 1)
    contract = (((1,), (1,)), ((), ()))
    for chat in range(CHATS):
        if chat + 1 < CHATS:
            begins.append(list_blocks(chat + 1, begins[chat + 1]))
        count = counts[0, chat]
        first_group = lax.div(begins[chat], GROUP)
        n_groups = lax.div(begins[chat + 1] - begins[chat], GROUP)
        lax.fori_loop(begins[chat], begins[chat + 1], arrive, 0)

        def tile(t, carry):
            base = jnp.minimum(start + t * TILE, TOK - TILE)
            ql = q_ref[pl.ds(base, TILE)].reshape(rows, LAT)
            qr = r_ref[pl.ds(base, TILE)].reshape(rows, ROPE)

            def keys_of(g):
                at = (first_group + g) * GROUP
                blocks = [held[at + i] for i in range(GROUP)]
                return blocks, jnp.concatenate([b[:BLOCK] for b in blocks], axis=0)

            def score(g, best):
                blocks, keys = keys_of(g)
                ropes = jnp.concatenate(
                    [
                        jnp.concatenate(
                            [b[BLOCK:, k * BLOCK : (k + 1) * BLOCK] for k in range(LAT // BLOCK)],
                            axis=0,
                        )
                        for b in blocks
                    ],
                    axis=1,
                )
                at = (first_group + g) * GROUP
                valid = jnp.concatenate([lane < place[at + i] for i in range(GROUP)], axis=1)
                s = lax.dot_general(ql, keys, contract, preferred_element_type=jnp.float32)
                s = s + jnp.dot(qr, ropes, preferred_element_type=jnp.float32)
                s = jnp.where(valid, s * (SCORE_SCALE * LOG2E), BIG)
                scores[g] = s
                for i in range(GROUP):
                    best = jnp.maximum(best, s[:, i * BLOCK : (i + 1) * BLOCK])
                return best

            def blend(g, state, top):
                total, acc = state
                _, keys = keys_of(g)
                p = jnp.exp2(scores[g] - top)
                for i in range(GROUP):
                    total = total + p[:, i * BLOCK : (i + 1) * BLOCK]
                acc = acc + jnp.dot(p.astype(jnp.bfloat16), keys, preferred_element_type=jnp.float32)
                return total, acc

            def over(step, state):
                def two(g, state):
                    return step(2 * g + 1, step(2 * g, state))

                state = lax.fori_loop(0, lax.div(n_groups, 2), two, state)
                return lax.fori_loop(n_groups - lax.rem(n_groups, 2), n_groups, step, state)

            best = over(score, jnp.full((rows, BLOCK), BIG, jnp.float32))
            top = jnp.max(best, axis=1, keepdims=True)
            total, acc = over(
                lambda g, state: blend(g, state, top),
                (jnp.zeros((rows, BLOCK), jnp.float32), jnp.zeros((rows, LAT), jnp.float32)),
            )
            total = jnp.sum(total, axis=1, keepdims=True)
            token = base + lax.broadcasted_iota(jnp.int32, (TILE, 1, 1), 0)
            keep = (token >= start) & (token < start + count)
            some = total > 0.0
            safe = jnp.where(some, total, 1.0)
            value = (acc / safe).astype(jnp.bfloat16).reshape(TILE, heads, LAT)
            lse = jnp.where(some, top + jnp.log2(safe), BIG)
            lse = jnp.broadcast_to(lse, (rows, BLOCK)).reshape(TILE, heads, BLOCK)
            at = pl.ds(base, TILE)
            o_ref[at] = jnp.where(keep, value, o_ref[at])
            s_ref[at] = jnp.where(keep, lse, s_ref[at])
            return carry

        lax.fori_loop(0, lax.div(count + TILE - 1, TILE), tile, 0)
        start = start + count


def attend(table, lengths, counts, where, kv, q, r, after, name):
    smem = pl.BlockSpec(memory_space=pltpu.SMEM)
    vmem = pl.BlockSpec(memory_space=pltpu.VMEM)
    hbm = pl.BlockSpec(memory_space=pl.ANY)
    tok, heads, width = q.shape
    return pl.pallas_call(
        attend_kernel,
        out_shape=(
            jax.ShapeDtypeStruct((tok, heads, width), jnp.bfloat16),
            jax.ShapeDtypeStruct((tok, heads, BLOCK), jnp.float32),
        ),
        in_specs=[smem] * 4 + [hbm] + [vmem] * 2 + [hbm],
        out_specs=(vmem,) * 2,
        scratch_shapes=[
            pltpu.VMEM((SLOTS,) + kv.shape[1:], jnp.bfloat16),
            pltpu.SMEM((SLOTS,), jnp.int32),
            pltpu.SemaphoreType.DMA((SLOTS,)),
            pltpu.VMEM((MAXB // GROUP, TILE * heads, GROUP * BLOCK), jnp.float32),
        ],
        compiler_params=pltpu.CompilerParams(vmem_limit_bytes=48 * 2**20),
        cost_estimate=pl.CostEstimate(
            flops=5 * 10**9, bytes_accessed=40 * 2**20, transcendentals=2 * 2**20
        ),
        name=name,
    )(table, lengths, counts, where, kv, q, r, after)


MESH = pl.DeviceIdType.MESH
AXES = ("plane", "zl", "zh", "core")
SENDS = 2 * N_DP
CHUNK = 32
ROW_ORDER = (
    0, 42, 46, 21, 11, 33, 58, 31, 49, 59, 45, 13, 47, 10, 32, 6,
    27, 34, 8, 35, 9, 51, 39, 5, 55, 52, 18, 56, 50, 24, 37, 3,
    40, 2, 44, 14, 36, 15, 53, 61, 28, 30, 63, 23, 43, 22, 48, 7,
    41, 54, 29, 20, 1, 60, 62, 57, 17, 12, 19, 4, 16, 26, 38, 25,
)
BLOCK_ORDER = (
    0, 22, 18, 29, 25, 15, 11, 4, 27, 13, 31, 14, 28, 26, 21, 3,
    19, 1, 12, 9, 5, 23, 10, 24, 7, 8, 6, 16, 2, 20, 30, 17,
)


def place_of():
    return tuple(lax.axis_index(name) for name in AXES)


def neighbours():
    plane, zl, zh, _ = place_of()
    y, x, z = lax.div(plane, 4), lax.rem(plane, 4), zh * 2 + zl
    ys = [lax.rem(y + d, 4) * 4 for d in range(4)]
    xs = [lax.rem(x + d, 4) for d in range(4)]
    zs = [lax.rem(z + d, 4) for d in range(4)]
    lows, highs = [lax.rem(v, 2) for v in zs], [lax.div(v, 2) for v in zs]

    def shifted(dy, dx, dz):
        return ys[dy % 4] + xs[dx % 4], lows[dz % 4], highs[dz % 4]

    return shifted


def facing(shifted, core):
    def either(dy, dx, dz, sign):
        ahead = shifted(sign * dy, sign * dx, sign * dz)
        back = shifted(-sign * dy, -sign * dx, -sign * dz)
        return tuple(a + core * (b - a) for a, b in zip(ahead, back))

    return either


def feed_kernel(
    ids, gate_vals, hidden, latents, ropes, send, q, r, wg_hbm, wu_hbm, wd_hbm,
    kv, q_par, r_par, out, near_w,
    rows, mine_w, wg, wu, wd, arr, arr_sib, stage, acts, part, part_sib, part_in,
    w_sem, row_send, row_recv, fwd_send, fwd_recv, part_send, part_recv,
    kv_send, kv_recv, kvf_send, kvf_recv, misc_send, misc_recv,
):
    plane, zl, zh, core = place_of()
    dp, z = plane * 2 + zl, zh * 2 + zl
    shifted = neighbours()
    either = facing(shifted, core)

    def row_place(j, sign):
        return either(j // 16, j // 4 % 4, j % 4, sign)

    def block_place(j, sign):
        return either(j // 8, j % 4, j // 4 % 2, sign)

    sibling = (plane, zl, zh, 1 - core)
    partner = (plane, zl, 1 - zh, core)
    loads = [
        pltpu.make_async_copy(a, b, w_sem.at[i])
        for i, (a, b) in enumerate(((wg_hbm, wg), (wu_hbm, wu), (wd_hbm, wd)))
    ]
    for load in loads:
        load.start()

    barrier = pltpu.get_barrier_semaphore()

    for j in range(1, SENDS):
        to = (*shifted(j // 16, j // 4 % 4, j % 4), core)
        pl.semaphore_signal(barrier, inc=1, device_id=to, device_id_type=MESH)
    pl.semaphore_signal(barrier, inc=1, device_id=sibling, device_id_type=MESH)

    fan, count = ids.shape
    capacity = rows.shape[1]
    slots = N_DP * capacity
    slot = lax.broadcasted_iota(jnp.int32, (slots, count), 0)
    turn = lax.div(slot, capacity)
    half = N_DP // 2
    expert = lax.rem(turn, half) * 2 + lax.div(turn, half)
    hits = jnp.zeros((slots, count), jnp.float32)
    gates = jnp.zeros((slots, count), jnp.float32)
    for k in range(fan):
        same = ids[k : k + 1, :] == expert
        hits = hits + jnp.where(same, 1.0, 0.0)
        gates = gates + jnp.where(same, gate_vals[k : k + 1, :], 0.0)
    line = lax.broadcasted_iota(jnp.int32, (count, count), 0)
    across = lax.broadcasted_iota(jnp.int32, (count, count), 1)
    earlier = jnp.where(line < across, 1.0, 0.0).astype(jnp.bfloat16)
    before = jnp.dot(hits.astype(jnp.bfloat16), earlier, preferred_element_type=jnp.float32)
    wanted = lax.rem(slot, capacity).astype(jnp.float32)
    picked = jnp.where(before == wanted, hits, 0.0)
    picks = picked.astype(jnp.bfloat16)
    weight = picked * gates
    high = weight.astype(jnp.bfloat16)
    low = (weight - high.astype(jnp.float32)).astype(jnp.bfloat16)
    unit = jnp.where(line == across, 1.0, 0.0).astype(jnp.bfloat16)
    turned = (((1,), (1,)), ((), ()))
    for side in range(2):
        at = slice(side * slots // 2, (side + 1) * slots // 2)
        for i, term in enumerate((high, low)):
            value = lax.dot_general(unit, term[at], turned, preferred_element_type=jnp.float32)
            mine_w[side, i * count : (i + 1) * count] = value.astype(jnp.bfloat16)

    def pick(n, carry):
        cut = pl.ds(pl.multiple_of(n * 512, 512), 512)
        value = jnp.dot(picks, hidden[:, cut], preferred_element_type=jnp.float32)
        rows[:, :, cut] = value.astype(jnp.bfloat16).reshape(rows.shape[0], rows.shape[1], 512)
        return carry

    lax.fori_loop(0, hidden.shape[1] // 512, pick, 0)
    pl.semaphore_wait(barrier, SENDS)

    def remote(src, dst, send_sem, recv_sem, device):
        return pltpu.make_async_remote_copy(
            src_ref=src, dst_ref=dst, send_sem=send_sem, recv_sem=recv_sem,
            device_id=device, device_id_type=MESH,
        )

    def row_copy(i, to=(0, 0, 0)):
        source = rows.at[to[1] * (N_DP // 2) + to[0]]
        return remote(source, arr.at[i], row_send.at[i], row_recv.at[i], (*to, core))

    def fwd_copy(i):
        return remote(arr.at[i], arr_sib.at[i], fwd_send.at[i], fwd_recv.at[i], sibling)

    def part_copy(c):
        at = pl.ds(c * CHUNK, CHUNK)
        return remote(
            part_sib.at[at], part_in.at[at], part_send.at[c], part_recv.at[c], sibling
        )

    def kv_copy(i, to=(0, 0, 0)):
        return remote(
            stage.at[i], kv.at[dp], kv_send.at[i], kv_recv.at[i], (*to, core)
        )

    def kvf_copy(i, source=0):
        return remote(
            kv.at[source], kv.at[N_DP + source], kvf_send.at[i], kvf_recv.at[i], sibling
        )

    for i in range(1, SENDS):
        row_copy(i, row_place(ROW_ORDER[i], 1)).start()
    arr[0] = rows[zl * (N_DP // 2) + plane]

    q_copy = remote(q, q_par, misc_send.at[0], misc_recv.at[0], partner)
    r_copy = remote(r, r_par, misc_send.at[1], misc_recv.at[1], partner)
    q_copy.start()
    r_copy.start()

    def weight_copy(dz):
        to = shifted(0, 0, dz)
        return remote(
            mine_w.at[to[1]], near_w.at[z], misc_send.at[1 + dz], misc_recv.at[1 + dz], (*to, core)
        )

    for dz in (1, 2, 3):
        weight_copy(dz).start()
    near_w[z] = mine_w[zl]

    def load_block(i, to):
        index = send[0, to]
        stage[i, :BLOCK] = latents[index]
        rope = ropes[index]
        for k in range(LAT // BLOCK):
            stage[i, BLOCK:, k * BLOCK : (k + 1) * BLOCK] = rope[16 * k : 16 * (k + 1)]

    for i in range(1, N_DP):
        to = block_place(BLOCK_ORDER[i], 1)
        load_block(i, to[0] * 2 + to[1])
        kv_copy(i, to).start()
    load_block(0, dp)
    mine = pltpu.make_async_copy(stage.at[0], kv.at[dp], kv_send.at[0])
    mine.start()
    mine_fwd = remote(stage.at[0], kv.at[N_DP + dp], kvf_send.at[0], kvf_recv.at[0], sibling)
    mine_fwd.start()
    for load in loads:
        load.wait()

    def experts(source, target, c):
        at = pl.ds(c * CHUNK, CHUNK)
        x = source[at].reshape(CHUNK * source.shape[1], source.shape[2])
        for n in range(2):
            cut = slice(n * 256, (n + 1) * 256)
            gate = jnp.dot(x, wg[:, cut], preferred_element_type=jnp.float32)
            lifted = jnp.dot(x, wu[:, cut], preferred_element_type=jnp.float32)
            acts[:, cut] = (gate / (1.0 + jnp.exp(-gate)) * lifted).astype(jnp.bfloat16)

        def down(n, carry):
            cut = pl.ds(pl.multiple_of(n * 512, 512), 512)
            value = jnp.dot(acts[...], wd[:, cut], preferred_element_type=jnp.float32)
            target[at, :, cut] = value.astype(jnp.bfloat16).reshape(CHUNK, source.shape[1], 512)
            return carry

        lax.fori_loop(0, source.shape[2] // 512, down, 0)

    def chunk(c, carry):
        first = c * CHUNK

        def pass_on(i, carry):
            @pl.when(i > 0)
            def _():
                row_copy(i).wait_recv()

            fwd_copy(i).start()
            return carry

        lax.fori_loop(first, first + CHUNK, pass_on, 0)
        experts(arr, part, c)

        def await_sib(i, carry):
            fwd_copy(i).wait_recv()
            return carry

        lax.fori_loop(first, first + CHUNK, await_sib, 0)
        experts(arr_sib, part_sib, c)
        part_copy(c).start()
        return carry

    lax.fori_loop(0, SENDS // CHUNK, chunk, 0)

    for i in range(1, N_DP):
        kv_copy(i).wait_recv()
        source = block_place(BLOCK_ORDER[i], -1)
        kvf_copy(i, source[0] * 2 + source[1]).start()

    for i in range(SENDS):
        if i % CHUNK == 0:
            part_copy(i // CHUNK).wait()
        source = row_place(ROW_ORDER[i], -1)
        total = part[i].astype(jnp.float32) + part_in[i].astype(jnp.float32)
        out[source[0] * 4 + source[2] * 2 + source[1]] = total.astype(jnp.bfloat16)

    def end_rows(i, carry):
        row_copy(i).wait_send()
        return carry

    lax.fori_loop(1, SENDS, end_rows, 0)

    def end_fwd(i, carry):
        fwd_copy(i).wait_send()
        return carry

    lax.fori_loop(0, SENDS, end_fwd, 0)

    def end_blocks(i, carry):
        kv_copy(i).wait_send()
        kvf_copy(i).wait()
        return carry

    lax.fori_loop(1, N_DP, end_blocks, 0)
    mine.wait()
    mine_fwd.wait()
    q_copy.wait()
    r_copy.wait()
    for dz in (1, 2, 3):
        weight_copy(dz).wait()


def feed(ids, gate_vals, hidden, latents, ropes, send, q, r, wg, wu, wd):
    smem = pl.BlockSpec(memory_space=pltpu.SMEM)
    vmem = pl.BlockSpec(memory_space=pltpu.VMEM)
    hbm = pl.BlockSpec(memory_space=pl.ANY)
    bf16 = jnp.bfloat16
    packed = BLOCK + ropes.shape[1] * BLOCK // LAT
    blocks = jax.ShapeDtypeStruct((2 * N_DP, packed, LAT), bf16)
    count, width = hidden.shape
    capacity = count // 2
    weights = (2 * count, N_DP * capacity // 2)
    chips = (SENDS, capacity, width)
    dma = pltpu.SemaphoreType.DMA
    chunks = SENDS // CHUNK
    return pl.pallas_call(
        feed_kernel,
        out_shape=(
            blocks,
            jax.ShapeDtypeStruct(q.shape, bf16),
            jax.ShapeDtypeStruct(r.shape, bf16),
            jax.ShapeDtypeStruct(chips, bf16),
            jax.ShapeDtypeStruct((4,) + weights, bf16),
        ),
        in_specs=[vmem] * 5 + [smem] + [hbm] * 5,
        out_specs=(hbm, hbm, hbm, vmem, vmem),
        scratch_shapes=[
            pltpu.VMEM((N_DP, capacity, width), bf16),
            pltpu.VMEM((2,) + weights, bf16),
            pltpu.VMEM(wg.shape, bf16),
            pltpu.VMEM(wu.shape, bf16),
            pltpu.VMEM(wd.shape, bf16),
            pltpu.VMEM(chips, bf16),
            pltpu.VMEM(chips, bf16),
            pltpu.VMEM((N_DP, packed, LAT), bf16),
            pltpu.VMEM((CHUNK * capacity, wg.shape[1]), bf16),
            pltpu.VMEM(chips, bf16),
            pltpu.VMEM(chips, bf16),
            pltpu.VMEM(chips, bf16),
            dma((3,)),
            dma((SENDS,)), dma((SENDS,)), dma((SENDS,)), dma((SENDS,)),
            dma((chunks,)), dma((chunks,)),
            dma((N_DP,)), dma((N_DP,)), dma((N_DP,)), dma((N_DP,)),
            dma((5,)), dma((5,)),
        ],
        compiler_params=pltpu.CompilerParams(
            collective_id=1, has_side_effects=True, vmem_limit_bytes=56 * 2**20
        ),
        cost_estimate=pl.CostEstimate(
            flops=11 * 10**9, bytes_accessed=24 * 2**20, transcendentals=2**19
        ),
        name="feed",
    )(ids, gate_vals, hidden, latents, ropes, send, q, r, wg, wu, wd)


def close_kernel(
    returned_hbm, w_lat_hbm, q_hbm, r_hbm, oa_hbm, ob_hbm, sa_hbm, sb_hbm,
    near_w, hidden, w_rope_ref, w_turn_ref, gain, cosine, sine, ok_ref,
    hidden_out, new_latent, new_rope, out_ref,
    returned, w_lat, q_ref, r_ref, oa, ob, sa, sb,
    sums, sums_out, inbox, fresh, load_sem, sum_send, sum_recv, fresh_send, fresh_recv,
):
    plane, zl, zh, core = place_of()
    z = zh * 2 + zl
    pool = zh * 2 + core
    heads = q_ref.shape[1]
    rows, width = hidden.shape
    loads = [
        pltpu.make_async_copy(a, b, load_sem.at[i])
        for i, (a, b) in enumerate(
            (
                (returned_hbm, returned), (w_lat_hbm, w_lat), (q_hbm, q_ref), (r_hbm, r_ref),
                (oa_hbm, oa), (ob_hbm, ob), (sa_hbm, sa), (sb_hbm, sb),
            )
        )
    ]
    for load in loads:
        load.start()
    shifted = neighbours()
    column = [(*shifted(0, 0, dz), core) for dz in (1, 2, 3)]
    others = [(plane, zl, zh, 1 - core), (plane, zl, 1 - zh, core), (plane, zl, 1 - zh, 1 - core)]
    barrier = pltpu.get_barrier_semaphore()
    for device in column + [others[0], others[2]]:
        pl.semaphore_signal(barrier, inc=1, device_id=device, device_id_type=MESH)
    pl.semaphore_wait(barrier, 5)
    loads[0].wait()

    def add(at):
        weights = near_w[at]

        for n in range(width // 512):
            cut = slice(n * 512, (n + 1) * 512)
            x = returned[:, at, :, cut].reshape(weights.shape[1], 512)
            both = jnp.dot(weights, x, preferred_element_type=jnp.float32)
            total = both[:rows] + both[rows:]
            sums[at, :, cut] = total
            sums_out[at, :, cut] = total.astype(jnp.bfloat16)

    def sum_copy(dz):
        to = lax.rem(z + dz, 4)
        return pltpu.make_async_remote_copy(
            src_ref=sums_out.at[to], dst_ref=inbox.at[dz - 1],
            send_sem=sum_send.at[dz - 1], recv_sem=sum_recv.at[dz - 1],
            device_id=column[dz - 1], device_id_type=MESH,
        )

    for dz in (2, 1, 3):
        add(lax.rem(z + dz, 4))
        sum_copy(dz).start()
    add(z)
    for dz in (1, 2, 3):
        sum_copy(dz).wait()

    total = hidden[...].astype(jnp.float32) + sums[z]
    for i in range(3):
        total = total + inbox[i].astype(jnp.float32)
    x = total.astype(jnp.bfloat16)
    hidden_out[...] = x
    loads[1].wait()
    latent = jnp.dot(x, w_lat[...], preferred_element_type=jnp.float32)
    plain = jnp.dot(x, w_rope_ref[...], preferred_element_type=jnp.float32)
    turned = jnp.dot(x, w_turn_ref[...], preferred_element_type=jnp.float32)
    scale = lax.rsqrt(jnp.mean(latent * latent, axis=1, keepdims=True) + NORM_EPS)
    latent = (latent * scale * gain[...]).astype(jnp.bfloat16)
    rope = (plain * cosine[...] + turned * sine[...]).astype(jnp.bfloat16)
    new_latent[...] = latent
    new_rope[...] = rope
    blank = jnp.zeros((rows, BLOCK - ROPE), jnp.bfloat16)
    fresh[pool] = jnp.concatenate([latent, rope, blank], axis=1)

    def fresh_copy(i):
        return pltpu.make_async_remote_copy(
            src_ref=fresh.at[pool], dst_ref=fresh.at[pool],
            send_sem=fresh_send.at[i], recv_sem=fresh_recv.at[i],
            device_id=others[i], device_id_type=MESH,
        )

    for i in range(3):
        fresh_copy(i).start()
    for load in loads[2:]:
        load.wait()
    for i in range(3):
        fresh_copy(i).wait()

    contract = (((1,), (1,)), ((), ()))
    keys = fresh[...].reshape(TOK, LAT + BLOCK)
    lat_keys = keys[:, :LAT]
    rope_keys = keys[:, LAT : LAT + ROPE]

    def tile(t, carry):
        at = pl.ds(t * TILE, TILE)
        size = TILE * heads
        s = lax.dot_general(
            q_ref[at].reshape(size, LAT), lat_keys, contract, preferred_element_type=jnp.float32
        ) + lax.dot_general(
            r_ref[at].reshape(size, ROPE), rope_keys, contract, preferred_element_type=jnp.float32
        )
        ok = ok_ref[at]
        ok = jnp.broadcast_to(ok[:, None, :], (TILE, heads, TOK)).reshape(size, TOK)
        s = jnp.where(ok > 0.0, s * (SCORE_SCALE * LOG2E), BIG)
        la = sa[at].reshape(size, BLOCK)[:, :1]
        lb = sb[at].reshape(size, BLOCK)[:, :1]
        m = jnp.maximum(jnp.maximum(la, lb), jnp.max(s, axis=1, keepdims=True))
        p = jnp.where(ok > 0.0, jnp.exp2(s - m), 0.0)
        wa = jnp.exp2(la - m)
        wb = jnp.exp2(lb - m)
        weight = wa + wb + jnp.sum(p, axis=1, keepdims=True)
        mixed = jnp.dot(p.astype(jnp.bfloat16), lat_keys, preferred_element_type=jnp.float32)
        mixed = mixed + wa * oa[at].reshape(size, LAT).astype(jnp.float32)
        mixed = mixed + wb * ob[at].reshape(size, LAT).astype(jnp.float32)
        out_ref[at] = (mixed / weight).astype(jnp.bfloat16).reshape(TILE, heads, LAT)
        return carry

    lax.fori_loop(0, TOK // TILE, tile, 0)


def close(large, small):
    vmem = pl.BlockSpec(memory_space=pltpu.VMEM)
    hbm = pl.BlockSpec(memory_space=pl.ANY)
    q, hidden = large[2], small[1]
    rows, width = hidden.shape
    bf16 = jnp.bfloat16
    dma = pltpu.SemaphoreType.DMA
    return pl.pallas_call(
        close_kernel,
        out_shape=(
            jax.ShapeDtypeStruct(hidden.shape, bf16),
            jax.ShapeDtypeStruct((rows, LAT), bf16),
            jax.ShapeDtypeStruct((rows, ROPE), bf16),
            jax.ShapeDtypeStruct(q.shape, bf16),
        ),
        in_specs=[hbm] * len(large) + [vmem] * len(small),
        out_specs=(vmem,) * 4,
        scratch_shapes=[
            *(pltpu.VMEM(a.shape, a.dtype) for a in large),
            pltpu.VMEM((4, rows, width), jnp.float32),
            pltpu.VMEM((4, rows, width), bf16),
            pltpu.VMEM((3, rows, width), bf16),
            pltpu.VMEM((4, rows, LAT + BLOCK), bf16),
            dma((len(large),)),
            dma((3,)), dma((3,)),
            dma((3,)), dma((3,)),
        ],
        compiler_params=pltpu.CompilerParams(
            collective_id=2, has_side_effects=True, vmem_limit_bytes=48 * 2**20
        ),
        name="close",
    )(*large, *small)


def swap(value, axis):
    return lax.ppermute(value, axis, [(0, 1), (1, 0)])


def shards(
    hidden_in,
    expert_ids,
    gate_vals,
    w_gate,
    w_up,
    w_down,
    w_latent,
    w_rope,
    latent_gain,
    cache_latent,
    cache_rope,
    send_index,
    block_table,
    cached_len,
    new_counts,
    q_latent,
    q_rope,
):
    _, zl, zh, core = place_of()
    rows, width = hidden_in.shape
    capacity = rows // 2

    kv, q_par, r_par, partial, near_w = feed(
        expert_ids.T,
        gate_vals.T,
        hidden_in,
        cache_latent,
        cache_rope,
        send_index,
        q_latent,
        q_rope,
        w_gate[0],
        w_up[0],
        w_down[0],
    )
    r_own = q_rope.reshape(TOK, HEADS_DEV, ROPE)
    r_par = r_par.reshape(TOK, HEADS_DEV, ROPE)
    returned = lax.all_to_all(partial, "plane", split_axis=0, concat_axis=0, tiled=True)

    where = jnp.stack([zh, core, zl]).astype(jnp.int32)
    facts = (block_table.reshape(1, CHATS * MAXB), cached_len, new_counts, where, kv)
    o_par, s_par = attend(*facts, q_par, r_par, q_latent, "attend_partner")
    o_back = swap(o_par, "zh")
    s_back = swap(s_par[:, :, 0], "zh")
    o_own, s_own = attend(*facts, q_latent, r_own, o_par, "attend_own")
    s_back = jnp.broadcast_to(s_back[:, :, None], s_own.shape)
    counts = new_counts[0]
    local = (zh * 2 + core) * rows + jnp.arange(rows, dtype=jnp.int32)
    positions = chat_positions(counts, cached_len[0], local)
    half = ROPE // 2
    exponent = jnp.arange(half).astype(jnp.float32) * (-2.0 / ROPE)
    frequency = jnp.power(jnp.float32(ROPE_BASE), exponent)
    angle = positions.astype(jnp.float32)[:, None] * frequency[None, :]
    cosine = jnp.tile(jnp.cos(angle), (1, 2))
    sine = jnp.tile(jnp.sin(angle), (1, 2))
    w_turn = jnp.concatenate([-w_rope[:, half:], w_rope[:, :half]], axis=1)
    tokens = jnp.arange(TOK, dtype=jnp.int32)
    ends = jnp.cumsum(counts)
    chat_of = jnp.sum((tokens[:, None] >= ends[None, :]).astype(jnp.int32), axis=1)
    ok = (chat_of[:, None] == chat_of[None, :]) & (tokens[None, :] <= tokens[:, None])
    return close(
        (
            returned.reshape(N_DP // 2, 4, capacity, width),
            w_latent,
            q_latent,
            r_own,
            o_own,
            o_back,
            s_own,
            s_back,
        ),
        (
            near_w,
            hidden_in,
            w_rope,
            w_turn,
            latent_gain[None, :],
            cosine,
            sine,
            ok.astype(jnp.float32),
        ),
    )


def solution(mesh):
    whole = Mesh(mesh.devices.reshape(N_DP // 2, 2, 2, 2), AXES)
    every = AXES
    dp = ("plane", "zl")
    pool = ("zh", "core")
    return jax.shard_map(
        shards,
        mesh=whole,
        in_specs=(
            P(every, None),
            P(every, None),
            P(every, None),
            P(dp, None, pool),
            P(dp, None, pool),
            P(dp, pool, None),
            P(),
            P(),
            P(),
            P(every, None, None),
            P(every, None, None),
            P(every, None),
            P(dp, None, None),
            P(dp, None),
            P(dp, None),
            P(dp, pool, None),
            P(dp, pool),
        ),
        out_specs=(
            P(every, None),
            P(every, None),
            P(every, None),
            P(dp, pool, None),
        ),
        check_vma=False,
    )
```

```python
import functools

import jax
import jax.numpy as jnp
from jax import lax
from jax.experimental import pallas as pl
from jax.experimental.pallas import tpu as pltpu
from jax.sharding import Mesh
from jax.sharding import PartitionSpec as P

SCORE_SCALE = 192.0 ** (-0.5)
LOG2E = 1.4426950408889634
ROPE_BASE = 10000.0
NORM_EPS = 1e-06
BIG = -1e30

N_DP = 32
CHATS = 4
MAXB = 32
BLOCK = 128
LAT = 512
ROPE = 64
TOK = 64
HEADS_DEV = 16
GROUP = 4
TILE = 16
SLOTS = 2 * N_DP + CHATS * (GROUP - 1) + 2


def chat_positions(counts, lengths, local):
    ends = jnp.cumsum(counts)
    chat_of = jnp.sum((local[:, None] >= ends[None, :]).astype(jnp.int32), axis=1)
    starts = ends - counts
    onehot = (chat_of[:, None] == jnp.arange(counts.shape[0])[None, :]).astype(jnp.int32)
    return jnp.sum(onehot * (lengths - starts)[None, :], axis=1) + local


def attend_kernel(
    table, lengths, counts, where, kv, q_ref, r_ref, after,
    o_ref, s_ref, held, place, sems, scores,
):
    zh, core, low = where[0], where[1], where[2]
    heads = q_ref.shape[1]
    rows = TILE * heads

    def copy_in(source, slot):
        return pltpu.make_async_copy(kv.at[source], held.at[slot], sems.at[slot])

    def fetch(holder, slot):
        source = lax.shift_right_logical(holder, 2) + ((holder & 1) ^ core) * N_DP
        copy_in(source, slot).start()

    def list_blocks(chat, begin):
        length = lengths[0, chat]

        def step(j, carry):
            slot, last = carry
            holder = table[0, chat * MAXB + j]
            z = (lax.shift_right_logical(holder, 1) & 1) * 2 + (
                lax.shift_right_logical(holder, 2) & 1
            )
            step_z = jnp.where((z & 1) == low, 0, 1 + 2 * (holder & 1))
            mine = lax.shift_right_logical((z + step_z) & 3, 1) == zh

            @pl.when(mine)
            def _():
                place[slot] = jnp.clip(length - j * BLOCK, 0, BLOCK)
                fetch(holder, slot)

            return jnp.where(mine, slot + 1, slot), jnp.where(mine, holder, last)

        count = lax.shift_right_logical(length + BLOCK - 1, 7)
        slot, last = lax.fori_loop(0, count, step, (begin, jnp.int32(0)))
        pad = lax.rem(GROUP - lax.rem(slot, GROUP), GROUP)

        def fill(i, carry):
            place[carry] = 0
            fetch(last, carry)
            return carry + 1

        return lax.fori_loop(0, pad, fill, slot)

    def arrive(i, carry):
        copy_in(0, i).wait()
        return carry

    begins = [jnp.int32(0)]
    begins.append(list_blocks(0, begins[0]))
    start = jnp.int32(0)
    lane = lax.broadcasted_iota(jnp.int32, (1, BLOCK), 1)
    contract = (((1,), (1,)), ((), ()))
    for chat in range(CHATS):
        if chat + 1 < CHATS:
            begins.append(list_blocks(chat + 1, begins[chat + 1]))
        count = counts[0, chat]
        first_group = lax.div(begins[chat], GROUP)
        n_groups = lax.div(begins[chat + 1] - begins[chat], GROUP)
        lax.fori_loop(begins[chat], begins[chat + 1], arrive, 0)

        def tile(t, carry):
            base = jnp.minimum(start + t * TILE, TOK - TILE)
            ql = q_ref[pl.ds(base, TILE)].reshape(rows, LAT)
            qr = r_ref[pl.ds(base, TILE)].reshape(rows, ROPE)

            def keys_of(g):
                at = (first_group + g) * GROUP
                blocks = [held[at + i] for i in range(GROUP)]
                return blocks, jnp.concatenate([b[:BLOCK] for b in blocks], axis=0)

            def score(g, best):
                blocks, keys = keys_of(g)
                ropes = jnp.concatenate(
                    [
                        jnp.concatenate(
                            [b[BLOCK:, k * BLOCK : (k + 1) * BLOCK] for k in range(LAT // BLOCK)],
                            axis=0,
                        )
                        for b in blocks
                    ],
                    axis=1,
                )
                at = (first_group + g) * GROUP
                valid = jnp.concatenate([lane < place[at + i] for i in range(GROUP)], axis=1)
                s = lax.dot_general(ql, keys, contract, preferred_element_type=jnp.float32)
                s = s + jnp.dot(qr, ropes, preferred_element_type=jnp.float32)
                s = jnp.where(valid, s * (SCORE_SCALE * LOG2E), BIG)
                scores[g] = s
                for i in range(GROUP):
                    best = jnp.maximum(best, s[:, i * BLOCK : (i + 1) * BLOCK])
                return best

            def blend(g, state, top):
                total, acc = state
                _, keys = keys_of(g)
                p = jnp.exp2(scores[g] - top)
                for i in range(GROUP):
                    total = total + p[:, i * BLOCK : (i + 1) * BLOCK]
                acc = acc + jnp.dot(p.astype(jnp.bfloat16), keys, preferred_element_type=jnp.float32)
                return total, acc

            def over(step, state):
                def two(g, state):
                    return step(2 * g + 1, step(2 * g, state))

                state = lax.fori_loop(0, lax.div(n_groups, 2), two, state)
                return lax.fori_loop(n_groups - lax.rem(n_groups, 2), n_groups, step, state)

            best = over(score, jnp.full((rows, BLOCK), BIG, jnp.float32))
            top = jnp.max(best, axis=1, keepdims=True)
            total, acc = over(
                lambda g, state: blend(g, state, top),
                (jnp.zeros((rows, BLOCK), jnp.float32), jnp.zeros((rows, LAT), jnp.float32)),
            )
            total = jnp.sum(total, axis=1, keepdims=True)
            token = base + lax.broadcasted_iota(jnp.int32, (TILE, 1, 1), 0)
            keep = (token >= start) & (token < start + count)
            some = total > 0.0
            safe = jnp.where(some, total, 1.0)
            value = (acc / safe).astype(jnp.bfloat16).reshape(TILE, heads, LAT)
            lse = jnp.where(some, top + jnp.log2(safe), BIG)
            lse = jnp.broadcast_to(lse, (rows, BLOCK)).reshape(TILE, heads, BLOCK)
            at = pl.ds(base, TILE)
            o_ref[at] = jnp.where(keep, value, o_ref[at])
            s_ref[at] = jnp.where(keep, lse, s_ref[at])
            return carry

        lax.fori_loop(0, lax.div(count + TILE - 1, TILE), tile, 0)
        start = start + count


def attend(table, lengths, counts, where, kv, q, r, after, name):
    smem = pl.BlockSpec(memory_space=pltpu.SMEM)
    vmem = pl.BlockSpec(memory_space=pltpu.VMEM)
    hbm = pl.BlockSpec(memory_space=pl.ANY)
    tok, heads, width = q.shape
    return pl.pallas_call(
        attend_kernel,
        out_shape=(
            jax.ShapeDtypeStruct((tok, heads, width), jnp.bfloat16),
            jax.ShapeDtypeStruct((tok, heads, BLOCK), jnp.float32),
        ),
        in_specs=[smem] * 4 + [hbm] + [vmem] * 2 + [hbm],
        out_specs=(vmem,) * 2,
        scratch_shapes=[
            pltpu.VMEM((SLOTS,) + kv.shape[1:], jnp.bfloat16),
            pltpu.SMEM((SLOTS,), jnp.int32),
            pltpu.SemaphoreType.DMA((SLOTS,)),
            pltpu.VMEM((MAXB // GROUP, TILE * heads, GROUP * BLOCK), jnp.float32),
        ],
        compiler_params=pltpu.CompilerParams(vmem_limit_bytes=56 * 2**20),
        cost_estimate=pl.CostEstimate(
            flops=5 * 10**9, bytes_accessed=40 * 2**20, transcendentals=2 * 2**20
        ),
        name=name,
    )(table, lengths, counts, where, kv, q, r, after)


MESH = pl.DeviceIdType.MESH
AXES = ("plane", "zl", "zh", "core")
SENDS = 2 * N_DP
CHUNK = 32
ROW_ORDER = (
    0, 42, 46, 21, 11, 33, 58, 31, 49, 59, 45, 13, 47, 10, 32, 6,
    27, 34, 8, 35, 9, 51, 39, 5, 55, 52, 18, 56, 50, 24, 37, 3,
    40, 2, 44, 14, 36, 15, 53, 61, 28, 30, 63, 23, 43, 22, 48, 7,
    41, 54, 29, 20, 1, 60, 62, 57, 17, 12, 19, 4, 16, 26, 38, 25,
)
BLOCK_ORDER = (
    0, 22, 18, 29, 25, 15, 11, 4, 27, 13, 31, 14, 28, 26, 21, 3,
    19, 1, 12, 9, 5, 23, 10, 24, 7, 8, 6, 16, 2, 20, 30, 17,
)


def place_of():
    return tuple(lax.axis_index(name) for name in AXES)


def neighbours():
    plane, zl, zh, _ = place_of()
    y, x, z = lax.div(plane, 4), lax.rem(plane, 4), zh * 2 + zl
    ys = [lax.rem(y + d, 4) * 4 for d in range(4)]
    xs = [lax.rem(x + d, 4) for d in range(4)]
    zs = [lax.rem(z + d, 4) for d in range(4)]
    lows, highs = [lax.rem(v, 2) for v in zs], [lax.div(v, 2) for v in zs]

    def shifted(dy, dx, dz):
        return ys[dy % 4] + xs[dx % 4], lows[dz % 4], highs[dz % 4]

    return shifted


def facing(shifted, core):
    def either(dy, dx, dz, sign):
        ahead = shifted(sign * dy, sign * dx, sign * dz)
        back = shifted(-sign * dy, -sign * dx, -sign * dz)
        return tuple(a + core * (b - a) for a, b in zip(ahead, back))

    return either


def feed_kernel(
    ids, gate_vals, hidden, latents, ropes, send, q, r, wg_hbm, wu_hbm, wd_hbm,
    kv, q_par, r_par, out, near_w,
    rows, mine_w, wg, wu, wd, arr, arr_sib, stage, acts, part, part_sib, part_in,
    w_sem, row_send, row_recv, fwd_send, fwd_recv, part_send, part_recv,
    kv_send, kv_recv, kvf_send, kvf_recv, misc_send, misc_recv,
):
    plane, zl, zh, core = place_of()
    dp, z = plane * 2 + zl, zh * 2 + zl
    shifted = neighbours()
    either = facing(shifted, core)

    def row_place(j, sign):
        return either(j // 16, j // 4 % 4, j % 4, sign)

    def block_place(j, sign):
        return either(j // 8, j % 4, j // 4 % 2, sign)

    sibling = (plane, zl, zh, 1 - core)
    partner = (plane, zl, 1 - zh, core)
    loads = [
        pltpu.make_async_copy(a, b, w_sem.at[i])
        for i, (a, b) in enumerate(((wg_hbm, wg), (wu_hbm, wu), (wd_hbm, wd)))
    ]
    for load in loads:
        load.start()

    barrier = pltpu.get_barrier_semaphore()

    for j in range(1, SENDS):
        to = (*shifted(j // 16, j // 4 % 4, j % 4), core)
        pl.semaphore_signal(barrier, inc=1, device_id=to, device_id_type=MESH)
    pl.semaphore_signal(barrier, inc=1, device_id=sibling, device_id_type=MESH)

    fan, count = ids.shape
    capacity = rows.shape[1]
    slots = N_DP * capacity
    slot = lax.broadcasted_iota(jnp.int32, (slots, count), 0)
    turn = lax.div(slot, capacity)
    half = N_DP // 2
    expert = lax.rem(turn, half) * 2 + lax.div(turn, half)
    hits = jnp.zeros((slots, count), jnp.float32)
    gates = jnp.zeros((slots, count), jnp.float32)
    for k in range(fan):
        same = ids[k : k + 1, :] == expert
        hits = hits + jnp.where(same, 1.0, 0.0)
        gates = gates + jnp.where(same, gate_vals[k : k + 1, :], 0.0)
    line = lax.broadcasted_iota(jnp.int32, (count, count), 0)
    across = lax.broadcasted_iota(jnp.int32, (count, count), 1)
    earlier = jnp.where(line < across, 1.0, 0.0).astype(jnp.bfloat16)
    before = jnp.dot(hits.astype(jnp.bfloat16), earlier, preferred_element_type=jnp.float32)
    wanted = lax.rem(slot, capacity).astype(jnp.float32)
    picked = jnp.where(before == wanted, hits, 0.0)
    picks = picked.astype(jnp.bfloat16)
    weight = picked * gates
    high = weight.astype(jnp.bfloat16)
    low = (weight - high.astype(jnp.float32)).astype(jnp.bfloat16)
    unit = jnp.where(line == across, 1.0, 0.0).astype(jnp.bfloat16)
    turned = (((1,), (1,)), ((), ()))
    for side in range(2):
        at = slice(side * slots // 2, (side + 1) * slots // 2)
        for i, term in enumerate((high, low)):
            value = lax.dot_general(unit, term[at], turned, preferred_element_type=jnp.float32)
            mine_w[side, i * count : (i + 1) * count] = value.astype(jnp.bfloat16)

    def pick(n, carry):
        cut = pl.ds(pl.multiple_of(n * 512, 512), 512)
        value = jnp.dot(picks, hidden[:, cut], preferred_element_type=jnp.float32)
        rows[:, :, cut] = value.astype(jnp.bfloat16).reshape(rows.shape[0], rows.shape[1], 512)
        return carry

    lax.fori_loop(0, hidden.shape[1] // 512, pick, 0)
    pl.semaphore_wait(barrier, SENDS)

    def remote(src, dst, send_sem, recv_sem, device):
        return pltpu.make_async_remote_copy(
            src_ref=src, dst_ref=dst, send_sem=send_sem, recv_sem=recv_sem,
            device_id=device, device_id_type=MESH,
        )

    def row_copy(i, to=(0, 0, 0)):
        source = rows.at[to[1] * (N_DP // 2) + to[0]]
        return remote(source, arr.at[i], row_send.at[i], row_recv.at[i], (*to, core))

    def fwd_copy(i):
        return remote(arr.at[i], arr_sib.at[i], fwd_send.at[i], fwd_recv.at[i], sibling)

    def part_copy(c):
        at = pl.ds(c * CHUNK, CHUNK)
        return remote(
            part_sib.at[at], part_in.at[at], part_send.at[c], part_recv.at[c], sibling
        )

    def kv_copy(i, to=(0, 0, 0)):
        return remote(
            stage.at[i], kv.at[dp], kv_send.at[i], kv_recv.at[i], (*to, core)
        )

    def kvf_copy(i, source=0):
        return remote(
            kv.at[source], kv.at[N_DP + source], kvf_send.at[i], kvf_recv.at[i], sibling
        )

    for i in range(1, SENDS):
        row_copy(i, row_place(ROW_ORDER[i], 1)).start()
    arr[0] = rows[zl * (N_DP // 2) + plane]

    q_copy = remote(q, q_par, misc_send.at[0], misc_recv.at[0], partner)
    r_copy = remote(r, r_par, misc_send.at[1], misc_recv.at[1], partner)
    q_copy.start()
    r_copy.start()

    def weight_copy(dz):
        to = shifted(0, 0, dz)
        return remote(
            mine_w.at[to[1]], near_w.at[z], misc_send.at[1 + dz], misc_recv.at[1 + dz], (*to, core)
        )

    for dz in (1, 2, 3):
        weight_copy(dz).start()
    near_w[z] = mine_w[zl]

    def load_block(i, to):
        index = send[0, to]
        stage[i, :BLOCK] = latents[index]
        rope = ropes[index]
        for k in range(LAT // BLOCK):
            stage[i, BLOCK:, k * BLOCK : (k + 1) * BLOCK] = rope[16 * k : 16 * (k + 1)]

    for i in range(1, N_DP):
        to = block_place(BLOCK_ORDER[i], 1)
        load_block(i, to[0] * 2 + to[1])
        kv_copy(i, to).start()
    load_block(0, dp)
    mine = pltpu.make_async_copy(stage.at[0], kv.at[dp], kv_send.at[0])
    mine.start()
    mine_fwd = remote(stage.at[0], kv.at[N_DP + dp], kvf_send.at[0], kvf_recv.at[0], sibling)
    mine_fwd.start()
    for load in loads:
        load.wait()

    def experts(source, target, c):
        at = pl.ds(c * CHUNK, CHUNK)
        x = source[at].reshape(CHUNK * source.shape[1], source.shape[2])
        for n in range(2):
            cut = slice(n * 256, (n + 1) * 256)
            gate = jnp.dot(x, wg[:, cut], preferred_element_type=jnp.float32)
            lifted = jnp.dot(x, wu[:, cut], preferred_element_type=jnp.float32)
            acts[:, cut] = (gate / (1.0 + jnp.exp(-gate)) * lifted).astype(jnp.bfloat16)

        def down(n, carry):
            cut = pl.ds(pl.multiple_of(n * 512, 512), 512)
            value = jnp.dot(acts[...], wd[:, cut], preferred_element_type=jnp.float32)
            target[at, :, cut] = value.astype(jnp.bfloat16).reshape(CHUNK, source.shape[1], 512)
            return carry

        lax.fori_loop(0, source.shape[2] // 512, down, 0)

    def chunk(c, carry):
        first = c * CHUNK

        def pass_on(i, carry):
            @pl.when(i > 0)
            def _():
                row_copy(i).wait_recv()

            fwd_copy(i).start()
            return carry

        lax.fori_loop(first, first + CHUNK, pass_on, 0)
        experts(arr, part, c)

        def await_sib(i, carry):
            fwd_copy(i).wait_recv()
            return carry

        lax.fori_loop(first, first + CHUNK, await_sib, 0)
        experts(arr_sib, part_sib, c)
        part_copy(c).start()
        return carry

    lax.fori_loop(0, SENDS // CHUNK, chunk, 0)

    for i in range(1, N_DP):
        kv_copy(i).wait_recv()
        source = block_place(BLOCK_ORDER[i], -1)
        kvf_copy(i, source[0] * 2 + source[1]).start()

    for i in range(SENDS):
        if i % CHUNK == 0:
            part_copy(i // CHUNK).wait()
        source = row_place(ROW_ORDER[i], -1)
        total = part[i].astype(jnp.float32) + part_in[i].astype(jnp.float32)
        out[source[0] * 4 + source[2] * 2 + source[1]] = total.astype(jnp.bfloat16)

    def end_rows(i, carry):
        row_copy(i).wait_send()
        return carry

    lax.fori_loop(1, SENDS, end_rows, 0)

    def end_fwd(i, carry):
        fwd_copy(i).wait_send()
        return carry

    lax.fori_loop(0, SENDS, end_fwd, 0)

    def end_blocks(i, carry):
        kv_copy(i).wait_send()
        kvf_copy(i).wait()
        return carry

    lax.fori_loop(1, N_DP, end_blocks, 0)
    mine.wait()
    mine_fwd.wait()
    q_copy.wait()
    r_copy.wait()
    for dz in (1, 2, 3):
        weight_copy(dz).wait()


def feed(ids, gate_vals, hidden, latents, ropes, send, q, r, wg, wu, wd):
    smem = pl.BlockSpec(memory_space=pltpu.SMEM)
    vmem = pl.BlockSpec(memory_space=pltpu.VMEM)
    hbm = pl.BlockSpec(memory_space=pl.ANY)
    bf16 = jnp.bfloat16
    packed = BLOCK + ropes.shape[1] * BLOCK // LAT
    blocks = jax.ShapeDtypeStruct((2 * N_DP, packed, LAT), bf16)
    count, width = hidden.shape
    capacity = count // 2
    weights = (2 * count, N_DP * capacity // 2)
    chips = (SENDS, capacity, width)
    dma = pltpu.SemaphoreType.DMA
    chunks = SENDS // CHUNK
    return pl.pallas_call(
        feed_kernel,
        out_shape=(
            blocks,
            jax.ShapeDtypeStruct(q.shape, bf16),
            jax.ShapeDtypeStruct(r.shape, bf16),
            jax.ShapeDtypeStruct(chips, bf16),
            jax.ShapeDtypeStruct((4,) + weights, bf16),
        ),
        in_specs=[vmem] * 5 + [smem] + [hbm] * 5,
        out_specs=(hbm, hbm, hbm, vmem, vmem),
        scratch_shapes=[
            pltpu.VMEM((N_DP, capacity, width), bf16),
            pltpu.VMEM((2,) + weights, bf16),
            pltpu.VMEM(wg.shape, bf16),
            pltpu.VMEM(wu.shape, bf16),
            pltpu.VMEM(wd.shape, bf16),
            pltpu.VMEM(chips, bf16),
            pltpu.VMEM(chips, bf16),
            pltpu.VMEM((N_DP, packed, LAT), bf16),
            pltpu.VMEM((CHUNK * capacity, wg.shape[1]), bf16),
            pltpu.VMEM(chips, bf16),
            pltpu.VMEM(chips, bf16),
            pltpu.VMEM(chips, bf16),
            dma((3,)),
            dma((SENDS,)), dma((SENDS,)), dma((SENDS,)), dma((SENDS,)),
            dma((chunks,)), dma((chunks,)),
            dma((N_DP,)), dma((N_DP,)), dma((N_DP,)), dma((N_DP,)),
            dma((5,)), dma((5,)),
        ],
        compiler_params=pltpu.CompilerParams(
            collective_id=1, has_side_effects=True, vmem_limit_bytes=56 * 2**20
        ),
        cost_estimate=pl.CostEstimate(
            flops=11 * 10**9, bytes_accessed=24 * 2**20, transcendentals=2**19
        ),
        name="feed",
    )(ids, gate_vals, hidden, latents, ropes, send, q, r, wg, wu, wd)


def close_kernel(
    returned_hbm, w_lat_hbm, q_hbm, r_hbm, oa_hbm, ob_hbm, sa_hbm, sb_hbm,
    near_w, hidden, w_rope_ref, gain, cosine, sine, ok_ref,
    hidden_out, new_latent, new_rope, out_ref,
    returned, w_lat, q_ref, r_ref, oa, ob, sa, sb,
    sums, sums_out, inbox, fresh, load_sem, sum_send, sum_recv, fresh_send, fresh_recv,
):
    plane, zl, zh, core = place_of()
    z = zh * 2 + zl
    pool = zh * 2 + core
    heads = q_ref.shape[1]
    rows, width = hidden.shape
    loads = [
        pltpu.make_async_copy(a, b, load_sem.at[i])
        for i, (a, b) in enumerate(
            (
                (returned_hbm, returned), (w_lat_hbm, w_lat), (q_hbm, q_ref), (r_hbm, r_ref),
                (oa_hbm, oa), (ob_hbm, ob), (sa_hbm, sa), (sb_hbm, sb),
            )
        )
    ]
    for load in loads:
        load.start()
    shifted = neighbours()
    column = [(*shifted(0, 0, dz), core) for dz in (1, 2, 3)]
    others = [(plane, zl, zh, 1 - core), (plane, zl, 1 - zh, core), (plane, zl, 1 - zh, 1 - core)]
    barrier = pltpu.get_barrier_semaphore()
    for device in column + [others[0], others[2]]:
        pl.semaphore_signal(barrier, inc=1, device_id=device, device_id_type=MESH)
    pl.semaphore_wait(barrier, 5)
    loads[0].wait()

    def add(at):
        weights = near_w[at]

        for n in range(width // 512):
            cut = slice(n * 512, (n + 1) * 512)
            x = returned[:, at, :, cut].reshape(weights.shape[1], 512)
            both = jnp.dot(weights, x, preferred_element_type=jnp.float32)
            total = both[:rows] + both[rows:]
            sums[at, :, cut] = total
            sums_out[at, :, cut] = total.astype(jnp.bfloat16)

    def sum_copy(dz):
        to = lax.rem(z + dz, 4)
        return pltpu.make_async_remote_copy(
            src_ref=sums_out.at[to], dst_ref=inbox.at[dz - 1],
            send_sem=sum_send.at[dz - 1], recv_sem=sum_recv.at[dz - 1],
            device_id=column[dz - 1], device_id_type=MESH,
        )

    for dz in (2, 1, 3):
        add(lax.rem(z + dz, 4))
        sum_copy(dz).start()
    add(z)
    for dz in (1, 2, 3):
        sum_copy(dz).wait()

    total = hidden[...].astype(jnp.float32) + sums[z]
    for i in range(3):
        total = total + inbox[i].astype(jnp.float32)
    x = total.astype(jnp.bfloat16)
    hidden_out[...] = x
    loads[1].wait()
    latent = jnp.dot(x, w_lat[...], preferred_element_type=jnp.float32)
    plain = jnp.dot(x, w_rope_ref[...], preferred_element_type=jnp.float32)
    half = ROPE // 2
    turned = jnp.concatenate([-plain[:, half:], plain[:, :half]], axis=1)
    scale = lax.rsqrt(jnp.mean(latent * latent, axis=1, keepdims=True) + NORM_EPS)
    latent = (latent * scale * gain[...]).astype(jnp.bfloat16)
    rope = (plain * cosine[...] + turned * sine[...]).astype(jnp.bfloat16)
    new_latent[...] = latent
    new_rope[...] = rope
    blank = jnp.zeros((rows, BLOCK - ROPE), jnp.bfloat16)
    fresh[pool] = jnp.concatenate([latent, rope, blank], axis=1)

    def fresh_copy(i):
        return pltpu.make_async_remote_copy(
            src_ref=fresh.at[pool], dst_ref=fresh.at[pool],
            send_sem=fresh_send.at[i], recv_sem=fresh_recv.at[i],
            device_id=others[i], device_id_type=MESH,
        )

    for i in range(3):
        fresh_copy(i).start()
    for load in loads[2:]:
        load.wait()
    for i in range(3):
        fresh_copy(i).wait()

    contract = (((1,), (1,)), ((), ()))
    keys = fresh[...].reshape(TOK, LAT + BLOCK)
    lat_keys = keys[:, :LAT]
    rope_keys = keys[:, LAT : LAT + ROPE]

    for t in range(TOK // TILE):
        at = pl.ds(t * TILE, TILE)
        size = TILE * heads
        s = lax.dot_general(
            q_ref[at].reshape(size, LAT), lat_keys, contract, preferred_element_type=jnp.float32
        ) + lax.dot_general(
            r_ref[at].reshape(size, ROPE), rope_keys, contract, preferred_element_type=jnp.float32
        )
        ok = ok_ref[at]
        ok = jnp.broadcast_to(ok[:, None, :], (TILE, heads, TOK)).reshape(size, TOK)
        s = jnp.where(ok > 0.0, s * (SCORE_SCALE * LOG2E), BIG)
        la = sa[at].reshape(size, BLOCK)[:, :1]
        lb = sb[at].reshape(size, BLOCK)[:, :1]
        m = jnp.maximum(jnp.maximum(la, lb), jnp.max(s, axis=1, keepdims=True))
        p = jnp.where(ok > 0.0, jnp.exp2(s - m), 0.0)
        wa = jnp.exp2(la - m)
        wb = jnp.exp2(lb - m)
        weight = wa + wb + jnp.sum(p, axis=1, keepdims=True)
        mixed = jnp.dot(p.astype(jnp.bfloat16), lat_keys, preferred_element_type=jnp.float32)
        mixed = mixed + wa * oa[at].reshape(size, LAT).astype(jnp.float32)
        mixed = mixed + wb * ob[at].reshape(size, LAT).astype(jnp.float32)
        out_ref[at] = (mixed / weight).astype(jnp.bfloat16).reshape(TILE, heads, LAT)


def close(large, small):
    vmem = pl.BlockSpec(memory_space=pltpu.VMEM)
    hbm = pl.BlockSpec(memory_space=pl.ANY)
    q, hidden = large[2], small[1]
    rows, width = hidden.shape
    bf16 = jnp.bfloat16
    dma = pltpu.SemaphoreType.DMA
    return pl.pallas_call(
        close_kernel,
        out_shape=(
            jax.ShapeDtypeStruct(hidden.shape, bf16),
            jax.ShapeDtypeStruct((rows, LAT), bf16),
            jax.ShapeDtypeStruct((rows, ROPE), bf16),
            jax.ShapeDtypeStruct(q.shape, bf16),
        ),
        in_specs=[hbm] * len(large) + [vmem] * len(small),
        out_specs=(vmem,) * 4,
        scratch_shapes=[
            *(pltpu.VMEM(a.shape, a.dtype) for a in large),
            pltpu.VMEM((4, rows, width), jnp.float32),
            pltpu.VMEM((4, rows, width), bf16),
            pltpu.VMEM((3, rows, width), bf16),
            pltpu.VMEM((4, rows, LAT + BLOCK), bf16),
            dma((len(large),)),
            dma((3,)), dma((3,)),
            dma((3,)), dma((3,)),
        ],
        compiler_params=pltpu.CompilerParams(
            collective_id=2, has_side_effects=True, vmem_limit_bytes=56 * 2**20
        ),
        name="close",
    )(*large, *small)


def swap(value, axis):
    return lax.ppermute(value, axis, [(0, 1), (1, 0)])


def shards(
    hidden_in,
    expert_ids,
    gate_vals,
    w_gate,
    w_up,
    w_down,
    w_latent,
    w_rope,
    latent_gain,
    cache_latent,
    cache_rope,
    send_index,
    block_table,
    cached_len,
    new_counts,
    q_latent,
    q_rope,
):
    _, zl, zh, core = place_of()
    rows, width = hidden_in.shape
    capacity = rows // 2

    kv, q_par, r_par, partial, near_w = feed(
        expert_ids.T,
        gate_vals.T,
        hidden_in,
        cache_latent,
        cache_rope,
        send_index,
        q_latent,
        q_rope,
        w_gate[0],
        w_up[0],
        w_down[0],
    )
    r_own = q_rope.reshape(TOK, HEADS_DEV, ROPE)
    r_par = r_par.reshape(TOK, HEADS_DEV, ROPE)
    returned = lax.all_to_all(partial, "plane", split_axis=0, concat_axis=0, tiled=True)

    where = jnp.stack([zh, core, zl]).astype(jnp.int32)
    facts = (block_table.reshape(1, CHATS * MAXB), cached_len, new_counts, where, kv)
    o_par, s_par = attend(*facts, q_par, r_par, q_latent, "attend_partner")
    o_back = swap(o_par, "zh")
    s_back = swap(s_par[:, :, 0], "zh")
    o_own, s_own = attend(*facts, q_latent, r_own, o_par, "attend_own")
    s_back = jnp.broadcast_to(s_back[:, :, None], s_own.shape)
    counts = new_counts[0]
    local = (zh * 2 + core) * rows + jnp.arange(rows, dtype=jnp.int32)
    positions = chat_positions(counts, cached_len[0], local)
    half = ROPE // 2
    exponent = jnp.arange(half).astype(jnp.float32) * (-2.0 / ROPE)
    frequency = jnp.power(jnp.float32(ROPE_BASE), exponent)
    angle = positions.astype(jnp.float32)[:, None] * frequency[None, :]
    cosine = jnp.tile(jnp.cos(angle), (1, 2))
    sine = jnp.tile(jnp.sin(angle), (1, 2))
    tokens = jnp.arange(TOK, dtype=jnp.int32)
    ends = jnp.cumsum(counts)
    chat_of = jnp.sum((tokens[:, None] >= ends[None, :]).astype(jnp.int32), axis=1)
    ok = (chat_of[:, None] == chat_of[None, :]) & (tokens[None, :] <= tokens[:, None])
    return close(
        (
            returned.reshape(N_DP // 2, 4, capacity, width),
            w_latent,
            q_latent,
            r_own,
            o_own,
            o_back,
            s_own,
            s_back,
        ),
        (
            near_w,
            hidden_in,
            w_rope,
            latent_gain[None, :],
            cosine,
            sine,
            ok.astype(jnp.float32),
        ),
    )


def solution(mesh):
    whole = Mesh(mesh.devices.reshape(N_DP // 2, 2, 2, 2), AXES)
    every = AXES
    dp = ("plane", "zl")
    pool = ("zh", "core")
    return jax.shard_map(
        shards,
        mesh=whole,
        in_specs=(
            P(every, None),
            P(every, None),
            P(every, None),
            P(dp, None, pool),
            P(dp, None, pool),
            P(dp, pool, None),
            P(),
            P(),
            P(),
            P(every, None, None),
            P(every, None, None),
            P(every, None),
            P(dp, None, None),
            P(dp, None),
            P(dp, None),
            P(dp, pool, None),
            P(dp, pool),
        ),
        out_specs=(
            P(every, None),
            P(every, None),
            P(every, None),
            P(dp, pool, None),
        ),
        check_vma=False,
    )
```

```python
import functools

import jax
import jax.numpy as jnp
from jax import lax
from jax.experimental import pallas as pl
from jax.experimental.pallas import tpu as pltpu
from jax.sharding import Mesh
from jax.sharding import PartitionSpec as P

SCORE_SCALE = 192.0 ** (-0.5)
LOG2E = 1.4426950408889634
ROPE_BASE = 10000.0
NORM_EPS = 1e-06
BIG = -1e30

N_DP = 32
CHATS = 4
MAXB = 32
BLOCK = 128
LAT = 512
ROPE = 64
TOK = 64
HEADS_DEV = 16
GROUP = 4
TILE = 16
SLOTS = 2 * N_DP + CHATS * (GROUP - 1) + 2


def chat_positions(counts, lengths, local):
    ends = jnp.cumsum(counts)
    chat_of = jnp.sum((local[:, None] >= ends[None, :]).astype(jnp.int32), axis=1)
    starts = ends - counts
    onehot = (chat_of[:, None] == jnp.arange(counts.shape[0])[None, :]).astype(jnp.int32)
    return jnp.sum(onehot * (lengths - starts)[None, :], axis=1) + local


def attend_kernel(
    table, lengths, counts, where, kv, q_ref, r_ref, after,
    o_ref, s_ref, held, place, sems, scores,
):
    zh, core, low = where[0], where[1], where[2]
    heads = q_ref.shape[1]
    rows = TILE * heads

    def copy_in(source, slot):
        return pltpu.make_async_copy(kv.at[source], held.at[slot], sems.at[slot])

    def fetch(holder, slot):
        source = lax.shift_right_logical(holder, 2) + ((holder & 1) ^ core) * N_DP
        copy_in(source, slot).start()

    def list_blocks(chat, begin):
        length = lengths[0, chat]

        def step(j, carry):
            slot, last = carry
            holder = table[0, chat * MAXB + j]
            z = (lax.shift_right_logical(holder, 1) & 1) * 2 + (
                lax.shift_right_logical(holder, 2) & 1
            )
            step_z = jnp.where((z & 1) == low, 0, 1 + 2 * (holder & 1))
            mine = lax.shift_right_logical((z + step_z) & 3, 1) == zh

            @pl.when(mine)
            def _():
                place[slot] = jnp.clip(length - j * BLOCK, 0, BLOCK)
                fetch(holder, slot)

            return jnp.where(mine, slot + 1, slot), jnp.where(mine, holder, last)

        count = lax.shift_right_logical(length + BLOCK - 1, 7)
        slot, last = lax.fori_loop(0, count, step, (begin, jnp.int32(0)))
        pad = lax.rem(GROUP - lax.rem(slot, GROUP), GROUP)

        def fill(i, carry):
            place[carry] = 0
            fetch(last, carry)
            return carry + 1

        return lax.fori_loop(0, pad, fill, slot)

    def arrive(i, carry):
        copy_in(0, i).wait()
        return carry

    begins = [jnp.int32(0)]
    begins.append(list_blocks(0, begins[0]))
    start = jnp.int32(0)
    lane = lax.broadcasted_iota(jnp.int32, (1, BLOCK), 1)
    contract = (((1,), (1,)), ((), ()))
    for chat in range(CHATS):
        if chat + 1 < CHATS:
            begins.append(list_blocks(chat + 1, begins[chat + 1]))
        count = counts[0, chat]
        first_group = lax.div(begins[chat], GROUP)
        n_groups = lax.div(begins[chat + 1] - begins[chat], GROUP)
        lax.fori_loop(begins[chat], begins[chat + 1], arrive, 0)

        def tile(t, carry):
            base = jnp.minimum(start + t * TILE, TOK - TILE)
            ql = q_ref[pl.ds(base, TILE)].reshape(rows, LAT)
            qr = r_ref[pl.ds(base, TILE)].reshape(rows, ROPE)

            def keys_of(g):
                at = (first_group + g) * GROUP
                blocks = [held[at + i] for i in range(GROUP)]
                return blocks, jnp.concatenate([b[:BLOCK] for b in blocks], axis=0)

            def score(g, best):
                blocks, keys = keys_of(g)
                ropes = jnp.concatenate(
                    [
                        jnp.concatenate(
                            [b[BLOCK:, k * BLOCK : (k + 1) * BLOCK] for k in range(LAT // BLOCK)],
                            axis=0,
                        )
                        for b in blocks
                    ],
                    axis=1,
                )
                at = (first_group + g) * GROUP
                valid = jnp.concatenate([lane < place[at + i] for i in range(GROUP)], axis=1)
                s = lax.dot_general(ql, keys, contract, preferred_element_type=jnp.float32)
                s = s + jnp.dot(qr, ropes, preferred_element_type=jnp.float32)
                s = jnp.where(valid, s * (SCORE_SCALE * LOG2E), BIG)
                scores[g] = s
                for i in range(GROUP):
                    best = jnp.maximum(best, s[:, i * BLOCK : (i + 1) * BLOCK])
                return best

            def blend(g, state, top):
                total, acc = state
                _, keys = keys_of(g)
                p = jnp.exp2(scores[g] - top)
                for i in range(GROUP):
                    total = total + p[:, i * BLOCK : (i + 1) * BLOCK]
                acc = acc + jnp.dot(p.astype(jnp.bfloat16), keys, preferred_element_type=jnp.float32)
                return total, acc

            def over(step, state):
                def two(g, state):
                    return step(2 * g + 1, step(2 * g, state))

                state = lax.fori_loop(0, lax.div(n_groups, 2), two, state)
                return lax.fori_loop(n_groups - lax.rem(n_groups, 2), n_groups, step, state)

            best = over(score, jnp.full((rows, BLOCK), BIG, jnp.float32))
            top = jnp.max(best, axis=1, keepdims=True)
            total, acc = over(
                lambda g, state: blend(g, state, top),
                (jnp.zeros((rows, BLOCK), jnp.float32), jnp.zeros((rows, LAT), jnp.float32)),
            )
            total = jnp.sum(total, axis=1, keepdims=True)
            token = base + lax.broadcasted_iota(jnp.int32, (TILE, 1, 1), 0)
            keep = (token >= start) & (token < start + count)
            some = total > 0.0
            safe = jnp.where(some, total, 1.0)
            value = (acc / safe).astype(jnp.bfloat16).reshape(TILE, heads, LAT)
            lse = jnp.where(some, top + jnp.log2(safe), BIG)
            lse = jnp.broadcast_to(lse, (rows, BLOCK)).reshape(TILE, heads, BLOCK)
            at = pl.ds(base, TILE)
            o_ref[at] = jnp.where(keep, value, o_ref[at])
            s_ref[at] = jnp.where(keep, lse, s_ref[at])
            return carry

        lax.fori_loop(0, lax.div(count + TILE - 1, TILE), tile, 0)
        start = start + count


def attend(table, lengths, counts, where, kv, q, r, after, name):
    smem = pl.BlockSpec(memory_space=pltpu.SMEM)
    vmem = pl.BlockSpec(memory_space=pltpu.VMEM)
    hbm = pl.BlockSpec(memory_space=pl.ANY)
    tok, heads, width = q.shape
    return pl.pallas_call(
        attend_kernel,
        out_shape=(
            jax.ShapeDtypeStruct((tok, heads, width), jnp.bfloat16),
            jax.ShapeDtypeStruct((tok, heads, BLOCK), jnp.float32),
        ),
        in_specs=[smem] * 4 + [hbm] + [vmem] * 2 + [hbm],
        out_specs=(vmem,) * 2,
        scratch_shapes=[
            pltpu.VMEM((SLOTS,) + kv.shape[1:], jnp.bfloat16),
            pltpu.SMEM((SLOTS,), jnp.int32),
            pltpu.SemaphoreType.DMA((SLOTS,)),
            pltpu.VMEM((MAXB // GROUP, TILE * heads, GROUP * BLOCK), jnp.float32),
        ],
        compiler_params=pltpu.CompilerParams(vmem_limit_bytes=48 * 2**20),
        cost_estimate=pl.CostEstimate(
            flops=5 * 10**9, bytes_accessed=40 * 2**20, transcendentals=2 * 2**20
        ),
        name=name,
    )(table, lengths, counts, where, kv, q, r, after)


MESH = pl.DeviceIdType.MESH
AXES = ("plane", "zl", "zh", "core")
SENDS = 2 * N_DP
CHUNK = 32
ROW_ORDER = (
    0, 42, 46, 21, 11, 33, 58, 31, 49, 59, 45, 13, 47, 10, 32, 6,
    27, 34, 8, 35, 9, 51, 39, 5, 55, 52, 18, 56, 50, 24, 37, 3,
    40, 2, 44, 14, 36, 15, 53, 61, 28, 30, 63, 23, 43, 22, 48, 7,
    41, 54, 29, 20, 1, 60, 62, 57, 17, 12, 19, 4, 16, 26, 38, 25,
)
BLOCK_ORDER = (
    0, 22, 18, 29, 25, 15, 11, 4, 27, 13, 31, 14, 28, 26, 21, 3,
    19, 1, 12, 9, 5, 23, 10, 24, 7, 8, 6, 16, 2, 20, 30, 17,
)


def place_of():
    return tuple(lax.axis_index(name) for name in AXES)


def neighbours():
    plane, zl, zh, _ = place_of()
    y, x, z = lax.div(plane, 4), lax.rem(plane, 4), zh * 2 + zl
    ys = [lax.rem(y + d, 4) * 4 for d in range(4)]
    xs = [lax.rem(x + d, 4) for d in range(4)]
    zs = [lax.rem(z + d, 4) for d in range(4)]
    lows, highs = [lax.rem(v, 2) for v in zs], [lax.div(v, 2) for v in zs]

    def shifted(dy, dx, dz):
        return ys[dy % 4] + xs[dx % 4], lows[dz % 4], highs[dz % 4]

    return shifted


def facing(shifted, core):
    def either(dy, dx, dz, sign):
        ahead = shifted(sign * dy, sign * dx, sign * dz)
        back = shifted(-sign * dy, -sign * dx, -sign * dz)
        return tuple(a + core * (b - a) for a, b in zip(ahead, back))

    return either


def feed_kernel(
    ids, gate_vals, hidden, latents, ropes, send, q, r, wg_hbm, wu_hbm, wd_hbm,
    kv, q_par, r_par, out, near_w,
    rows, mine_w, wg, wu, wd, arr, arr_sib, stage, acts, part, part_sib, part_in,
    w_sem, row_send, row_recv, fwd_send, fwd_recv, part_send, part_recv,
    kv_send, kv_recv, kvf_send, kvf_recv, misc_send, misc_recv,
):
    plane, zl, zh, core = place_of()
    dp, z = plane * 2 + zl, zh * 2 + zl
    shifted = neighbours()
    either = facing(shifted, core)

    def row_place(j, sign):
        return either(j // 16, j // 4 % 4, j % 4, sign)

    def block_place(j, sign):
        return either(j // 8, j % 4, j // 4 % 2, sign)

    sibling = (plane, zl, zh, 1 - core)
    partner = (plane, zl, 1 - zh, core)
    loads = [
        pltpu.make_async_copy(a, b, w_sem.at[i])
        for i, (a, b) in enumerate(((wg_hbm, wg), (wu_hbm, wu), (wd_hbm, wd)))
    ]
    for load in loads:
        load.start()

    barrier = pltpu.get_barrier_semaphore()

    for j in range(1, SENDS):
        to = (*shifted(j // 16, j // 4 % 4, j % 4), core)
        pl.semaphore_signal(barrier, inc=1, device_id=to, device_id_type=MESH)
    pl.semaphore_signal(barrier, inc=1, device_id=sibling, device_id_type=MESH)

    fan, count = ids.shape
    capacity = rows.shape[1]
    slots = N_DP * capacity
    slot = lax.broadcasted_iota(jnp.int32, (slots, count), 0)
    turn = lax.div(slot, capacity)
    half = N_DP // 2
    expert = lax.rem(turn, half) * 2 + lax.div(turn, half)
    hits = jnp.zeros((slots, count), jnp.float32)
    gates = jnp.zeros((slots, count), jnp.float32)
    for k in range(fan):
        same = ids[k : k + 1, :] == expert
        hits = hits + jnp.where(same, 1.0, 0.0)
        gates = gates + jnp.where(same, gate_vals[k : k + 1, :], 0.0)
    line = lax.broadcasted_iota(jnp.int32, (count, count), 0)
    across = lax.broadcasted_iota(jnp.int32, (count, count), 1)
    earlier = jnp.where(line < across, 1.0, 0.0).astype(jnp.bfloat16)
    before = jnp.dot(hits.astype(jnp.bfloat16), earlier, preferred_element_type=jnp.float32)
    wanted = lax.rem(slot, capacity).astype(jnp.float32)
    picked = jnp.where(before == wanted, hits, 0.0)
    picks = picked.astype(jnp.bfloat16)
    weight = picked * gates
    high = weight.astype(jnp.bfloat16)
    low = (weight - high.astype(jnp.float32)).astype(jnp.bfloat16)
    unit = jnp.where(line == across, 1.0, 0.0).astype(jnp.bfloat16)
    turned = (((1,), (1,)), ((), ()))
    for side in range(2):
        at = slice(side * slots // 2, (side + 1) * slots // 2)
        for i, term in enumerate((high, low)):
            value = lax.dot_general(unit, term[at], turned, preferred_element_type=jnp.float32)
            mine_w[side, i * count : (i + 1) * count] = value.astype(jnp.bfloat16)

    def pick(n, carry):
        cut = pl.ds(pl.multiple_of(n * 512, 512), 512)
        value = jnp.dot(picks, hidden[:, cut], preferred_element_type=jnp.float32)
        rows[:, :, cut] = value.astype(jnp.bfloat16).reshape(rows.shape[0], rows.shape[1], 512)
        return carry

    lax.fori_loop(0, hidden.shape[1] // 512, pick, 0)
    pl.semaphore_wait(barrier, SENDS)

    def remote(src, dst, send_sem, recv_sem, device):
        return pltpu.make_async_remote_copy(
            src_ref=src, dst_ref=dst, send_sem=send_sem, recv_sem=recv_sem,
            device_id=device, device_id_type=MESH,
        )

    def row_copy(i, to=(0, 0, 0)):
        source = rows.at[to[1] * (N_DP // 2) + to[0]]
        return remote(source, arr.at[i], row_send.at[i], row_recv.at[i], (*to, core))

    def fwd_copy(i):
        return remote(arr.at[i], arr_sib.at[i], fwd_send.at[i], fwd_recv.at[i], sibling)

    def part_copy(c):
        at = pl.ds(c * CHUNK, CHUNK)
        return remote(
            part_sib.at[at], part_in.at[at], part_send.at[c], part_recv.at[c], sibling
        )

    def kv_copy(i, to=(0, 0, 0)):
        return remote(
            stage.at[i], kv.at[dp], kv_send.at[i], kv_recv.at[i], (*to, core)
        )

    def kvf_copy(i, source=0):
        return remote(
            kv.at[source], kv.at[N_DP + source], kvf_send.at[i], kvf_recv.at[i], sibling
        )

    for i in range(1, SENDS):
        row_copy(i, row_place(ROW_ORDER[i], 1)).start()
    arr[0] = rows[zl * (N_DP // 2) + plane]

    q_copy = remote(q, q_par, misc_send.at[0], misc_recv.at[0], partner)
    r_copy = remote(r, r_par, misc_send.at[1], misc_recv.at[1], partner)
    q_copy.start()
    r_copy.start()

    def weight_copy(dz):
        to = shifted(0, 0, dz)
        return remote(
            mine_w.at[to[1]], near_w.at[z], misc_send.at[1 + dz], misc_recv.at[1 + dz], (*to, core)
        )

    for dz in (1, 2, 3):
        weight_copy(dz).start()
    near_w[z] = mine_w[zl]

    def load_block(i, to):
        index = send[0, to]
        stage[i, :BLOCK] = latents[index]
        rope = ropes[index]
        for k in range(LAT // BLOCK):
            stage[i, BLOCK:, k * BLOCK : (k + 1) * BLOCK] = rope[16 * k : 16 * (k + 1)]

    for i in range(1, N_DP):
        to = block_place(BLOCK_ORDER[i], 1)
        load_block(i, to[0] * 2 + to[1])
        kv_copy(i, to).start()
    load_block(0, dp)
    mine = pltpu.make_async_copy(stage.at[0], kv.at[dp], kv_send.at[0])
    mine.start()
    mine_fwd = remote(stage.at[0], kv.at[N_DP + dp], kvf_send.at[0], kvf_recv.at[0], sibling)
    mine_fwd.start()
    for load in loads:
        load.wait()

    def experts(source, target, c):
        at = pl.ds(c * CHUNK, CHUNK)
        x = source[at].reshape(CHUNK * source.shape[1], source.shape[2])
        for n in range(2):
            cut = slice(n * 256, (n + 1) * 256)
            gate = jnp.dot(x, wg[:, cut], preferred_element_type=jnp.float32)
            lifted = jnp.dot(x, wu[:, cut], preferred_element_type=jnp.float32)
            acts[:, cut] = (gate / (1.0 + jnp.exp(-gate)) * lifted).astype(jnp.bfloat16)

        def down(n, carry):
            cut = pl.ds(pl.multiple_of(n * 512, 512), 512)
            value = jnp.dot(acts[...], wd[:, cut], preferred_element_type=jnp.float32)
            target[at, :, cut] = value.astype(jnp.bfloat16).reshape(CHUNK, source.shape[1], 512)
            return carry

        lax.fori_loop(0, source.shape[2] // 512, down, 0)

    def chunk(c, carry):
        first = c * CHUNK

        def pass_on(i, carry):
            @pl.when(i > 0)
            def _():
                row_copy(i).wait_recv()

            fwd_copy(i).start()
            return carry

        lax.fori_loop(first, first + CHUNK, pass_on, 0)
        experts(arr, part, c)

        def await_sib(i, carry):
            fwd_copy(i).wait_recv()
            return carry

        lax.fori_loop(first, first + CHUNK, await_sib, 0)
        experts(arr_sib, part_sib, c)
        part_copy(c).start()
        return carry

    lax.fori_loop(0, SENDS // CHUNK, chunk, 0)

    for i in range(1, N_DP):
        kv_copy(i).wait_recv()
        source = block_place(BLOCK_ORDER[i], -1)
        kvf_copy(i, source[0] * 2 + source[1]).start()

    for i in range(SENDS):
        if i % CHUNK == 0:
            part_copy(i // CHUNK).wait()
        source = row_place(ROW_ORDER[i], -1)
        total = part[i].astype(jnp.float32) + part_in[i].astype(jnp.float32)
        out[source[0] * 4 + source[2] * 2 + source[1]] = total.astype(jnp.bfloat16)

    def end_rows(i, carry):
        row_copy(i).wait_send()
        return carry

    lax.fori_loop(1, SENDS, end_rows, 0)

    def end_fwd(i, carry):
        fwd_copy(i).wait_send()
        return carry

    lax.fori_loop(0, SENDS, end_fwd, 0)

    def end_blocks(i, carry):
        kv_copy(i).wait_send()
        kvf_copy(i).wait()
        return carry

    lax.fori_loop(1, N_DP, end_blocks, 0)
    mine.wait()
    mine_fwd.wait()
    q_copy.wait()
    r_copy.wait()
    for dz in (1, 2, 3):
        weight_copy(dz).wait()


def feed(ids, gate_vals, hidden, latents, ropes, send, q, r, wg, wu, wd):
    smem = pl.BlockSpec(memory_space=pltpu.SMEM)
    vmem = pl.BlockSpec(memory_space=pltpu.VMEM)
    hbm = pl.BlockSpec(memory_space=pl.ANY)
    bf16 = jnp.bfloat16
    packed = BLOCK + ropes.shape[1] * BLOCK // LAT
    blocks = jax.ShapeDtypeStruct((2 * N_DP, packed, LAT), bf16)
    count, width = hidden.shape
    capacity = count // 2
    weights = (2 * count, N_DP * capacity // 2)
    chips = (SENDS, capacity, width)
    dma = pltpu.SemaphoreType.DMA
    chunks = SENDS // CHUNK
    return pl.pallas_call(
        feed_kernel,
        out_shape=(
            blocks,
            jax.ShapeDtypeStruct(q.shape, bf16),
            jax.ShapeDtypeStruct(r.shape, bf16),
            jax.ShapeDtypeStruct(chips, bf16),
            jax.ShapeDtypeStruct((4,) + weights, bf16),
        ),
        in_specs=[vmem] * 5 + [smem] + [hbm] * 5,
        out_specs=(hbm, hbm, hbm, vmem, vmem),
        scratch_shapes=[
            pltpu.VMEM((N_DP, capacity, width), bf16),
            pltpu.VMEM((2,) + weights, bf16),
            pltpu.VMEM(wg.shape, bf16),
            pltpu.VMEM(wu.shape, bf16),
            pltpu.VMEM(wd.shape, bf16),
            pltpu.VMEM(chips, bf16),
            pltpu.VMEM(chips, bf16),
            pltpu.VMEM((N_DP, packed, LAT), bf16),
            pltpu.VMEM((CHUNK * capacity, wg.shape[1]), bf16),
            pltpu.VMEM(chips, bf16),
            pltpu.VMEM(chips, bf16),
            pltpu.VMEM(chips, bf16),
            dma((3,)),
            dma((SENDS,)), dma((SENDS,)), dma((SENDS,)), dma((SENDS,)),
            dma((chunks,)), dma((chunks,)),
            dma((N_DP,)), dma((N_DP,)), dma((N_DP,)), dma((N_DP,)),
            dma((5,)), dma((5,)),
        ],
        compiler_params=pltpu.CompilerParams(
            collective_id=1, has_side_effects=True, vmem_limit_bytes=56 * 2**20
        ),
        cost_estimate=pl.CostEstimate(
            flops=11 * 10**9, bytes_accessed=24 * 2**20, transcendentals=2**19
        ),
        name="feed",
    )(ids, gate_vals, hidden, latents, ropes, send, q, r, wg, wu, wd)


def close_kernel(
    returned_hbm, w_lat_hbm, q_hbm, r_hbm, oa_hbm, ob_hbm, sa_hbm, sb_hbm,
    near_w, hidden, w_rope_ref, gain, cosine, sine, ok_ref,
    hidden_out, new_latent, new_rope, out_ref,
    returned, w_lat, q_ref, r_ref, oa, ob, sa, sb,
    sums, sums_out, inbox, fresh, load_sem, sum_send, sum_recv, fresh_send, fresh_recv,
):
    plane, zl, zh, core = place_of()
    z = zh * 2 + zl
    pool = zh * 2 + core
    heads = q_ref.shape[1]
    rows, width = hidden.shape
    loads = [
        pltpu.make_async_copy(a, b, load_sem.at[i])
        for i, (a, b) in enumerate(
            (
                (returned_hbm, returned), (w_lat_hbm, w_lat), (q_hbm, q_ref), (r_hbm, r_ref),
                (oa_hbm, oa), (ob_hbm, ob), (sa_hbm, sa), (sb_hbm, sb),
            )
        )
    ]
    for load in loads:
        load.start()
    shifted = neighbours()
    column = [(*shifted(0, 0, dz), core) for dz in (1, 2, 3)]
    others = [(plane, zl, zh, 1 - core), (plane, zl, 1 - zh, core), (plane, zl, 1 - zh, 1 - core)]
    barrier = pltpu.get_barrier_semaphore()
    for device in column + [others[0], others[2]]:
        pl.semaphore_signal(barrier, inc=1, device_id=device, device_id_type=MESH)
    pl.semaphore_wait(barrier, 5)
    loads[0].wait()

    def add(at):
        weights = near_w[at]

        for n in range(width // 512):
            cut = slice(n * 512, (n + 1) * 512)
            x = returned[:, at, :, cut].reshape(weights.shape[1], 512)
            both = jnp.dot(weights, x, preferred_element_type=jnp.float32)
            total = both[:rows] + both[rows:]
            sums[at, :, cut] = total
            sums_out[at, :, cut] = total.astype(jnp.bfloat16)

    def sum_copy(dz):
        to = lax.rem(z + dz, 4)
        return pltpu.make_async_remote_copy(
            src_ref=sums_out.at[to], dst_ref=inbox.at[dz - 1],
            send_sem=sum_send.at[dz - 1], recv_sem=sum_recv.at[dz - 1],
            device_id=column[dz - 1], device_id_type=MESH,
        )

    for dz in (2, 1, 3):
        add(lax.rem(z + dz, 4))
        sum_copy(dz).start()
    add(z)
    for dz in (1, 2, 3):
        sum_copy(dz).wait()

    total = hidden[...].astype(jnp.float32) + sums[z]
    for i in range(3):
        total = total + inbox[i].astype(jnp.float32)
    x = total.astype(jnp.bfloat16)
    hidden_out[...] = x
    loads[1].wait()
    latent = jnp.dot(x, w_lat[...], preferred_element_type=jnp.float32)
    plain = jnp.dot(x, w_rope_ref[...], preferred_element_type=jnp.float32)
    half = ROPE // 2
    turned = jnp.concatenate([-plain[:, half:], plain[:, :half]], axis=1)
    scale = lax.rsqrt(jnp.mean(latent * latent, axis=1, keepdims=True) + NORM_EPS)
    latent = (latent * scale * gain[...]).astype(jnp.bfloat16)
    rope = (plain * cosine[...] + turned * sine[...]).astype(jnp.bfloat16)
    new_latent[...] = latent
    new_rope[...] = rope
    blank = jnp.zeros((rows, BLOCK - ROPE), jnp.bfloat16)
    fresh[pool] = jnp.concatenate([latent, rope, blank], axis=1)

    def fresh_copy(i):
        return pltpu.make_async_remote_copy(
            src_ref=fresh.at[pool], dst_ref=fresh.at[pool],
            send_sem=fresh_send.at[i], recv_sem=fresh_recv.at[i],
            device_id=others[i], device_id_type=MESH,
        )

    for i in range(3):
        fresh_copy(i).start()
    for load in loads[2:]:
        load.wait()
    for i in range(3):
        fresh_copy(i).wait()

    contract = (((1,), (1,)), ((), ()))
    keys = fresh[...].reshape(TOK, LAT + BLOCK)
    lat_keys = keys[:, :LAT]
    rope_keys = keys[:, LAT : LAT + ROPE]

    for t in range(TOK // TILE):
        at = pl.ds(t * TILE, TILE)
        size = TILE * heads
        s = lax.dot_general(
            q_ref[at].reshape(size, LAT), lat_keys, contract, preferred_element_type=jnp.float32
        ) + lax.dot_general(
            r_ref[at].reshape(size, ROPE), rope_keys, contract, preferred_element_type=jnp.float32
        )
        ok = ok_ref[at]
        ok = jnp.broadcast_to(ok[:, None, :], (TILE, heads, TOK)).reshape(size, TOK)
        s = jnp.where(ok > 0.0, s * (SCORE_SCALE * LOG2E), BIG)
        la = sa[at].reshape(size, BLOCK)[:, :1]
        lb = sb[at].reshape(size, BLOCK)[:, :1]
        m = jnp.maximum(jnp.maximum(la, lb), jnp.max(s, axis=1, keepdims=True))
        p = jnp.where(ok > 0.0, jnp.exp2(s - m), 0.0)
        wa = jnp.exp2(la - m)
        wb = jnp.exp2(lb - m)
        weight = wa + wb + jnp.sum(p, axis=1, keepdims=True)
        mixed = jnp.dot(p.astype(jnp.bfloat16), lat_keys, preferred_element_type=jnp.float32)
        mixed = mixed + wa * oa[at].reshape(size, LAT).astype(jnp.float32)
        mixed = mixed + wb * ob[at].reshape(size, LAT).astype(jnp.float32)
        out_ref[at] = (mixed / weight).astype(jnp.bfloat16).reshape(TILE, heads, LAT)


def close(large, small):
    vmem = pl.BlockSpec(memory_space=pltpu.VMEM)
    hbm = pl.BlockSpec(memory_space=pl.ANY)
    q, hidden = large[2], small[1]
    rows, width = hidden.shape
    bf16 = jnp.bfloat16
    dma = pltpu.SemaphoreType.DMA
    return pl.pallas_call(
        close_kernel,
        out_shape=(
            jax.ShapeDtypeStruct(hidden.shape, bf16),
            jax.ShapeDtypeStruct((rows, LAT), bf16),
            jax.ShapeDtypeStruct((rows, ROPE), bf16),
            jax.ShapeDtypeStruct(q.shape, bf16),
        ),
        in_specs=[hbm] * len(large) + [vmem] * len(small),
        out_specs=(vmem,) * 4,
        scratch_shapes=[
            *(pltpu.VMEM(a.shape, a.dtype) for a in large),
            pltpu.VMEM((4, rows, width), jnp.float32),
            pltpu.VMEM((4, rows, width), bf16),
            pltpu.VMEM((3, rows, width), bf16),
            pltpu.VMEM((4, rows, LAT + BLOCK), bf16),
            dma((len(large),)),
            dma((3,)), dma((3,)),
            dma((3,)), dma((3,)),
        ],
        compiler_params=pltpu.CompilerParams(
            collective_id=2, has_side_effects=True, vmem_limit_bytes=48 * 2**20
        ),
        name="close",
    )(*large, *small)


def swap(value, axis):
    return lax.ppermute(value, axis, [(0, 1), (1, 0)])


def shards(
    hidden_in,
    expert_ids,
    gate_vals,
    w_gate,
    w_up,
    w_down,
    w_latent,
    w_rope,
    latent_gain,
    cache_latent,
    cache_rope,
    send_index,
    block_table,
    cached_len,
    new_counts,
    q_latent,
    q_rope,
):
    _, zl, zh, core = place_of()
    rows, width = hidden_in.shape
    capacity = rows // 2

    kv, q_par, r_par, partial, near_w = feed(
        expert_ids.T,
        gate_vals.T,
        hidden_in,
        cache_latent,
        cache_rope,
        send_index,
        q_latent,
        q_rope,
        w_gate[0],
        w_up[0],
        w_down[0],
    )
    r_own = q_rope.reshape(TOK, HEADS_DEV, ROPE)
    r_par = r_par.reshape(TOK, HEADS_DEV, ROPE)
    returned = lax.all_to_all(partial, "plane", split_axis=0, concat_axis=0, tiled=True)

    where = jnp.stack([zh, core, zl]).astype(jnp.int32)
    facts = (block_table.reshape(1, CHATS * MAXB), cached_len, new_counts, where, kv)
    o_par, s_par = attend(*facts, q_par, r_par, q_latent, "attend_partner")
    o_back = swap(o_par, "zh")
    s_back = swap(s_par[:, :, 0], "zh")
    o_own, s_own = attend(*facts, q_latent, r_own, o_par, "attend_own")
    s_back = jnp.broadcast_to(s_back[:, :, None], s_own.shape)
    counts = new_counts[0]
    local = (zh * 2 + core) * rows + jnp.arange(rows, dtype=jnp.int32)
    positions = chat_positions(counts, cached_len[0], local)
    half = ROPE // 2
    exponent = jnp.arange(half).astype(jnp.float32) * (-2.0 / ROPE)
    frequency = jnp.power(jnp.float32(ROPE_BASE), exponent)
    angle = positions.astype(jnp.float32)[:, None] * frequency[None, :]
    cosine = jnp.tile(jnp.cos(angle), (1, 2))
    sine = jnp.tile(jnp.sin(angle), (1, 2))
    tokens = jnp.arange(TOK, dtype=jnp.int32)
    ends = jnp.cumsum(counts)
    chat_of = jnp.sum((tokens[:, None] >= ends[None, :]).astype(jnp.int32), axis=1)
    ok = (chat_of[:, None] == chat_of[None, :]) & (tokens[None, :] <= tokens[:, None])
    return close(
        (
            returned.reshape(N_DP // 2, 4, capacity, width),
            w_latent,
            q_latent,
            r_own,
            o_own,
            o_back,
            s_own,
            s_back,
        ),
        (
            near_w,
            hidden_in,
            w_rope,
            latent_gain[None, :],
            cosine,
            sine,
            ok.astype(jnp.float32),
        ),
    )


def solution(mesh):
    whole = Mesh(mesh.devices.reshape(N_DP // 2, 2, 2, 2), AXES)
    every = AXES
    dp = ("plane", "zl")
    pool = ("zh", "core")
    return jax.shard_map(
        shards,
        mesh=whole,
        in_specs=(
            P(every, None),
            P(every, None),
            P(every, None),
            P(dp, None, pool),
            P(dp, None, pool),
            P(dp, pool, None),
            P(),
            P(),
            P(),
            P(every, None, None),
            P(every, None, None),
            P(every, None),
            P(dp, None, None),
            P(dp, None),
            P(dp, None),
            P(dp, pool, None),
            P(dp, pool),
        ),
        out_specs=(
            P(every, None),
            P(every, None),
            P(every, None),
            P(dp, pool, None),
        ),
        check_vma=False,
    )
```
